32 devices in a mesh: dp: 2 (over y), seq: 4 (over z), tensor: 4 (over x, core).
Axes of the slice: x: 2, y: 2, z: 4, core: 2. Of those that a mesh axis runs over, the one named last changes fastest.
Arguments:
- stream: float32 [4096, 2048], P(('dp', 'seq')), may hold values from -6 to 6
- cotangent: float32 [4096, 2048], P(('dp', 'seq')), may hold values from -6 to 6
- w_input: float32 [2048, 16, 768], P(('dp', 'seq'), 'tensor'), may hold values from -0.125 to 0.125
- w_rates: float32 [2048, 16, 2], P(('dp', 'seq'), 'tensor'), may hold values from -0.125 to 0.125
- w_conv: float32 [4, 16, 512], replicated, may hold values from -3 to 3
- w_output: float32 [16, 256, 2048], P('tensor', None, ('dp', 'seq')), may hold values from -0.1875 to 0.1875
- w_swiglu: float32 [2048, 2, 5632], P(('dp', 'seq'), None, 'tensor'), may hold values from -0.125 to 0.125
- w_down: float32 [5632, 2048], P('tensor', ('dp', 'seq')), may hold values from -0.078125 to 0.078125
- w_gains: float32 [2, 2048], replicated, may hold values from 0.5 to 1.5
- w_scale: float32 [256], replicated, may hold values from 0.5 to 1.5
- w_heads: float32 [2, 16], replicated, may hold values from -6 to 2.7, as said below
- m_input: float32 [2, 2048, 16, 768], P(None, ('dp', 'seq'), 'tensor'), may hold values from -2 to 2, as said below
- m_rates: float32 [2, 2048, 16, 2], P(None, ('dp', 'seq'), 'tensor'), may hold values from -2 to 2, as said below
- m_conv: float32 [2, 4, 16, 512], replicated, may hold values from -2 to 2, as said below
- m_output: float32 [2, 16, 256, 2048], P(None, 'tensor', None, ('dp', 'seq')), may hold values from -2 to 2, as said below
- m_swiglu: float32 [2, 2048, 2, 5632], P(None, ('dp', 'seq'), None, 'tensor'), may hold values from -2 to 2, as said below
- m_down: float32 [2, 5632, 2048], P(None, 'tensor', ('dp', 'seq')), may hold values from -2 to 2, as said below
- m_gains: float32 [2, 2, 2048], replicated, may hold values from -2 to 2, as said below
- m_scale: float32 [2, 256], replicated, may hold values from -2 to 2, as said below
- m_heads: float32 [2, 2, 16], replicated, may hold values from -2 to 2, as said below
Outputs:
- result: float32 [4096, 2048], P(('dp', 'seq'))
- grad_stream: float32 [4096, 2048], P(('dp', 'seq'))
- g_input: float32 [2048, 16, 768], P(('dp', 'seq'), 'tensor')
- g_rates: float32 [2048, 16, 2], P(('dp', 'seq'), 'tensor')
- g_conv: float32 [4, 16, 512], replicated
- g_output: float32 [16, 256, 2048], P('tensor', None, ('dp', 'seq'))
- g_swiglu: float32 [2048, 2, 5632], P(('dp', 'seq'), None, 'tensor')
- g_down: float32 [5632, 2048], P('tensor', ('dp', 'seq'))
- g_gains: float32 [2, 2048], replicated
- g_scale: float32 [256], replicated
- g_heads: float32 [2, 16], replicated
- new_input: float32 [2048, 16, 768], P(('dp', 'seq'), 'tensor')
- new_rates: float32 [2048, 16, 2], P(('dp', 'seq'), 'tensor')
- new_conv: float32 [4, 16, 512], replicated
- new_output: float32 [16, 256, 2048], P('tensor', None, ('dp', 'seq'))
- new_swiglu: float32 [2048, 2, 5632], P(('dp', 'seq'), None, 'tensor')
- new_down: float32 [5632, 2048], P('tensor', ('dp', 'seq'))
- new_gains: float32 [2, 2048], replicated
- new_scale: float32 [256], replicated
- new_heads: float32 [2, 16], replicated
- moment_input: float32 [2, 2048, 16, 768], P(None, ('dp', 'seq'), 'tensor')
- moment_rates: float32 [2, 2048, 16, 2], P(None, ('dp', 'seq'), 'tensor')
- moment_conv: float32 [2, 4, 16, 512], replicated
- moment_output: float32 [2, 16, 256, 2048], P(None, 'tensor', None, ('dp', 'seq'))
- moment_swiglu: float32 [2, 2048, 2, 5632], P(None, ('dp', 'seq'), None, 'tensor')
- moment_down: float32 [2, 5632, 2048], P(None, 'tensor', ('dp', 'seq'))
- moment_gains: float32 [2, 2, 2048], replicated
- moment_scale: float32 [2, 256], replicated
- moment_heads: float32 [2, 2, 16], replicated
The draws below stay inside these ranges and needn't reach their ends.
Inputs may be any that keep to these rules, and one draw needn't show every extreme that they name: `w_heads`: row 0 holds logarithms of decay rates, row 1 decay biases. `m_input`: slice 0 holds first moments, slice 1 second moments, which are positive. `m_rates`: slice 0 holds first moments, slice 1 second moments, which are positive. `m_conv`: slice 0 holds first moments, slice 1 second moments, which are positive. `m_output`: slice 0 holds first moments, slice 1 second moments, which are positive. `m_swiglu`: slice 0 holds first moments, slice 1 second moments, which are positive. `m_down`: slice 0 holds first moments, slice 1 second moments, which are positive. `m_gains`: slice 0 holds first moments, slice 1 second moments, which are positive. `m_scale`: slice 0 holds first moments, slice 1 second moments, which are positive. `m_heads`: slice 0 holds first moments, slice 1 second moments, which are positive.
All inputs are finite; a program needn't handle non-finite values.
Results may differ from the reference program's by a relative error of at most 0.012.
The reference program's roundings to bfloat16 on the way count: a program that leaves them out, or rounds other values in their place, can miss the bound.
Values may be sent and summed in bfloat16 or wider, within the bound.
No kernel may reach another device: no remote copies, remote signals or barrier semaphores. Data moves between devices by JAX's collectives and lax.ppermute only.
A program may use at most 320 MiB of HBM per device.

```python
import math
import jax
import jax.numpy as jnp
from jax import lax

D = 2048
H = 16
DK = 128
DV = 256
FF = 5632
KCONV = 4
BLOCK = 64
ADAM_STEP = 5
LENGTH = 2048
SEQS = 2
TOKENS = 4096


def moment_pair(key, shape, spread, least, most):
    first = jnp.clip(spread * jax.random.normal(jax.random.fold_in(key, 1), shape, jnp.float32), -2.0, 2.0)
    second = jnp.exp(jax.random.uniform(jax.random.fold_in(key, 2), shape, jnp.float32, math.log(least), math.log(most)))
    return jnp.stack([first, second])


def scaled_pair(key, shape, spread, least, most):
    first = jnp.clip(spread * jax.random.normal(jax.random.fold_in(key, 1), shape, jnp.float32), -2.0, 2.0)
    factor = jnp.exp(jax.random.uniform(jax.random.fold_in(key, 2), shape, jnp.float32, math.log(least), math.log(most)))
    return jnp.stack([first, spread * spread * factor])


def draw_w_heads(key, part):
    key = jax.random.fold_in(key, 201)
    first = jax.random.uniform(jax.random.fold_in(key, 1), (H,), jnp.float32, -2.3, 2.7)
    second = jax.random.uniform(jax.random.fold_in(key, 2), (H,), jnp.float32, -6.0, -2.0)
    return jnp.stack([first, second])


def draw_m_input(key, part):
    key = jax.random.fold_in(key, 101)
    shape = (D, H, 2 * DK + 2 * DV)
    spread = 1.0 / math.sqrt(TOKENS)
    return scaled_pair(key, shape, spread, 0.1, 2.0)


def draw_m_rates(key, part):
    key = jax.random.fold_in(key, 102)
    shape = (D, H, 2)
    return moment_pair(key, shape, 0.3, 0.01, 1.0)


def draw_m_conv(key, part):
    key = jax.random.fold_in(key, 103)
    shape = (KCONV, H, 2 * DK + DV)
    spread = 1.0 / math.sqrt(TOKENS)
    return scaled_pair(key, shape, spread, 0.1, 2.0)


def draw_m_output(key, part):
    key = jax.random.fold_in(key, 104)
    shape = (H, DV, D)
    spread = 0.8 / math.sqrt(TOKENS)
    return scaled_pair(key, shape, spread, 0.1, 2.0)


def draw_m_swiglu(key, part):
    key = jax.random.fold_in(key, 105)
    shape = (D, 2, FF)
    spread = 0.5 / math.sqrt(TOKENS)
    return scaled_pair(key, shape, spread, 0.1, 2.0)


def draw_m_down(key, part):
    key = jax.random.fold_in(key, 106)
    shape = (FF, D)
    spread = 0.8 / math.sqrt(TOKENS)
    return scaled_pair(key, shape, spread, 0.1, 2.0)


def draw_m_gains(key, part):
    key = jax.random.fold_in(key, 107)
    shape = (2, D)
    return moment_pair(key, shape, 0.3, 0.01, 1.0)


def draw_m_scale(key, part):
    key = jax.random.fold_in(key, 108)
    shape = (DV,)
    return moment_pair(key, shape, 0.3, 0.01, 1.0)


def draw_m_heads(key, part):
    key = jax.random.fold_in(key, 109)
    shape = (2, H)
    return moment_pair(key, shape, 0.4, 0.0001, 0.01)


def levels(key, shape, cuts, low, top_value):
    def one(dim, blocks):
        steps = jax.random.uniform(jax.random.fold_in(jax.random.fold_in(key, 6), dim), (blocks,), jnp.float32, low / len(cuts), top_value / len(cuts))
        return jnp.repeat(jnp.exp(steps), shape[dim] // blocks).reshape((-1,) + (1,) * (len(shape) - dim - 1))

    level = one(*cuts[0])
    for cut in cuts[1:]:
        level = level * one(*cut)
    return level


def gaussian(stream_key, shape, scale, most, pieces=(), kind=jnp.bfloat16):
    values = jax.random.normal(stream_key, shape, jnp.float32) * scale
    if len(pieces) > 0:
        values = levels(stream_key, shape, pieces, -0.22, 0.18) * values
    return jnp.clip(values, min=-most, max=most).astype(kind)


def setup_inputs(seed: int = 0) -> dict:
    splits = jax.random.split(jax.random.key(seed), 21)
    return {
        "stream": gaussian(splits[0], (TOKENS, D), 1.0, 6.0, ((0, 8),), jnp.float32),
        "cotangent": gaussian(splits[1], (TOKENS, D), 1.0, 6.0, ((0, 8),), jnp.float32),
        "w_input": gaussian(splits[2], (D, H, 2 * DK + 2 * DV), D ** -0.5, 0.125, ((0, 8), (1, 4)), jnp.float32),
        "w_rates": gaussian(splits[3], (D, H, 2), D ** -0.5, 0.125, ((0, 8), (1, 4)), jnp.float32),
        "w_conv": gaussian(splits[4], (KCONV, H, 2 * DK + DV), KCONV ** -0.5, 3.0, (), jnp.float32),
        "w_output": gaussian(splits[5], (H, DV, D), (H * DV // 4) ** -0.5, 0.1875, ((0, 4), (2, 8)), jnp.float32),
        "w_swiglu": gaussian(splits[6], (D, 2, FF), D ** -0.5, 0.125, ((0, 8), (2, 4)), jnp.float32),
        "w_down": gaussian(splits[7], (FF, D), FF ** -0.5, 0.078125, ((0, 4), (1, 8)), jnp.float32),
        "w_gains": jnp.clip(1.0 + 0.1 * jax.random.normal(splits[8], (2, D), jnp.float32), 0.5, 1.5),
        "w_scale": jnp.clip(1.0 + 0.1 * jax.random.normal(splits[9], (DV,), jnp.float32), 0.5, 1.5),
        "w_heads": draw_w_heads(jax.random.fold_in(splits[20], 71), 0),
        "m_input": draw_m_input(jax.random.fold_in(splits[20], 71), 0),
        "m_rates": draw_m_rates(jax.random.fold_in(splits[20], 71), 0),
        "m_conv": draw_m_conv(jax.random.fold_in(splits[20], 71), 0),
        "m_output": draw_m_output(jax.random.fold_in(splits[20], 71), 0),
        "m_swiglu": draw_m_swiglu(jax.random.fold_in(splits[20], 71), 0),
        "m_down": draw_m_down(jax.random.fold_in(splits[20], 71), 0),
        "m_gains": draw_m_gains(jax.random.fold_in(splits[20], 71), 0),
        "m_scale": draw_m_scale(jax.random.fold_in(splits[20], 71), 0),
        "m_heads": draw_m_heads(jax.random.fold_in(splits[20], 71), 0),
    }


HIGHEST = lax.Precision.HIGHEST

@jax.custom_vjp
def low(v):
    return lax.optimization_barrier(v.astype(jnp.bfloat16)).astype(jnp.float32)

@jax.custom_vjp
def low_back(v):
    return v

def low_keep(v):
    return (low(v), None)

def low_pass(kept, grad):
    return (grad,)

def back_keep(v):
    return (v, None)

def back_low(kept, grad):
    return (low(grad),)
low.defvjp(low_keep, low_pass)
low_back.defvjp(back_keep, back_low)

def rms_norm(rows, gain):
    return rows * lax.rsqrt(lax.optimization_barrier(jnp.mean(rows * rows, axis=-1, keepdims=True)) + 1e-06) * gain

def finish(mixer_out, gate_raw, scale_gain):
    factor = lax.rsqrt(lax.optimization_barrier(jnp.mean(mixer_out * mixer_out, axis=-1, keepdims=True)) + 1e-05)
    return mixer_out * factor * scale_gain * jax.nn.silu(gate_raw)

def prepare(mixed_rows, before, conv_weight, decay_raw, update_raw, head_rates):
    length = mixed_rows.shape[1]
    padded = jnp.concatenate([before, mixed_rows], axis=1)
    filtered = conv_weight[0] * padded[:, 0:length]
    for tap_index in range(1, conv_weight.shape[0]):
        filtered = filtered + conv_weight[tap_index] * padded[:, tap_index:tap_index + length]
    filtered = jax.nn.silu(filtered)
    query_raw = filtered[..., :DK]
    key_raw = filtered[..., DK:2 * DK]
    query = query_raw * lax.rsqrt(lax.optimization_barrier(jnp.sum(query_raw * query_raw, axis=-1, keepdims=True)) + 1e-06) * DK ** (-0.5)
    key_rows = key_raw * lax.rsqrt(lax.optimization_barrier(jnp.sum(key_raw * key_raw, axis=-1, keepdims=True)) + 1e-06)
    value_rows = filtered[..., 2 * DK:]
    update_gate = jax.nn.sigmoid(update_raw)
    log_decay = -jnp.exp(head_rates[0]) * jax.nn.softplus(decay_raw + head_rates[1])
    return (query, key_rows, value_rows, update_gate, log_decay)

def block_step(states, inputs):
    query, key_rows, value_rows, update_gate, log_decay = inputs
    length = query.shape[1]
    cumulative = jnp.cumsum(log_decay, axis=1)
    row_index = lax.broadcasted_iota(jnp.int32, (length, length), 0)
    column_index = lax.broadcasted_iota(jnp.int32, (length, length), 1)
    within = (row_index >= column_index)[None, :, :, None]
    strict = (row_index > column_index)[None, :, :, None]
    distance = cumulative[:, :, None, :] - cumulative[:, None, :, :]
    fade_within = jnp.where(within, jnp.exp(jnp.where(within, distance, 0.0)), 0.0)
    fade_strict = jnp.where(strict, fade_within, 0.0)
    key_products = jnp.einsum('bihk,bjhk->bijh', key_rows, key_rows, precision=HIGHEST)
    lower_part = update_gate[:, :, None, :] * key_products * fade_strict
    identity = jnp.eye(length, dtype=jnp.float32)
    system = identity + jnp.transpose(lower_part, (0, 3, 1, 2))
    growth = jnp.exp(cumulative)
    right_keys = jnp.transpose((update_gate * growth)[..., None] * key_rows, (0, 2, 1, 3))
    right_values = jnp.transpose(update_gate[..., None] * value_rows, (0, 2, 1, 3))
    solved_keys = jax.scipy.linalg.solve_triangular(system, right_keys, lower=True, unit_diagonal=True)
    solved_values = jax.scipy.linalg.solve_triangular(system, right_values, lower=True, unit_diagonal=True)
    fresh_values = solved_values - jnp.einsum('bhck,bhkw->bhcw', solved_keys, states, precision=HIGHEST)
    head_query = jnp.transpose(query, (0, 2, 1, 3))
    scores = jnp.einsum('bhik,bjhk->bhij', head_query, key_rows, precision=HIGHEST) * jnp.transpose(fade_within, (0, 3, 1, 2))
    carried = jnp.transpose(growth, (0, 2, 1))[..., None] * jnp.einsum('bhck,bhkw->bhcw', head_query, states, precision=HIGHEST)
    output = carried + jnp.einsum('bhij,bhjw->bhiw', scores, fresh_values, precision=HIGHEST)
    trailing = jnp.exp(cumulative[:, -1:, :] - cumulative)
    faded_keys = jnp.transpose(trailing[..., None] * key_rows, (0, 2, 1, 3))
    next_states = jnp.exp(cumulative[:, -1, :])[:, :, None, None] * states + jnp.einsum('bhck,bhcw->bhkw', faded_keys, fresh_values, precision=HIGHEST)
    return (next_states, jnp.transpose(output, (0, 2, 1, 3)))

def run_blocks(states, query, key_rows, value_rows, update_gate, log_decay):
    batches = query.shape[0]
    length = query.shape[1]
    block_count = length // BLOCK

    def split_blocks(array):
        return jnp.moveaxis(array.reshape((batches, block_count, BLOCK) + array.shape[2:]), 1, 0)
    final_states, outputs = lax.scan(jax.checkpoint(block_step), states, (split_blocks(query), split_blocks(key_rows), split_blocks(value_rows), split_blocks(update_gate), split_blocks(log_decay)))
    outputs = jnp.moveaxis(outputs, 0, 1)
    return (outputs.reshape((batches, length) + outputs.shape[3:]), final_states)

def forward(stream, w_input, w_rates, w_conv, w_output, w_swiglu, w_down, w_gains, w_scale, w_heads):
    sequences = stream.reshape(SEQS, LENGTH, D)
    conv_cols = 2 * DK + DV
    normed_in = low(rms_norm(sequences, w_gains[0]))
    projected = low_back(jnp.einsum('btd,dhc->bthc', normed_in, low(w_input), precision=HIGHEST))
    rates = low_back(jnp.einsum('btd,dhc->bthc', normed_in, low(w_rates), precision=HIGHEST))
    before = jnp.zeros((SEQS, KCONV - 1, H, conv_cols), jnp.float32)
    query, key_rows, value_rows, update_gate, log_decay = prepare(projected[..., :conv_cols], before, w_conv, rates[..., 0], rates[..., 1], w_heads)
    start_states = jnp.zeros((SEQS, H, DK, DV), jnp.float32)
    mixer_out, final_states = run_blocks(start_states, query, key_rows, value_rows, update_gate, log_decay)
    mixed = low(finish(mixer_out, projected[..., conv_cols:], w_scale))
    attention = low_back(jnp.einsum('bthv,hvd->btd', mixed, low(w_output), precision=HIGHEST))
    residual = sequences + attention
    normed_mid = low(rms_norm(residual, w_gains[1]))
    gate_up = low_back(jnp.einsum('btd,dgf->btgf', normed_mid, low(w_swiglu), precision=HIGHEST))
    activated = low(jax.nn.silu(gate_up[:, :, 0]) * gate_up[:, :, 1])
    feedforward = low_back(jnp.einsum('btf,fd->btd', activated, low(w_down), precision=HIGHEST))
    return (residual + feedforward).reshape(stream.shape)

def adam_update(weight, gradient, moments, token_count):
    mean_grad = gradient / token_count
    first = 0.5 * moments[0] + 0.5 * mean_grad
    second = 0.5 * moments[1] + 0.5 * mean_grad * mean_grad
    correction = 1.0 - 0.5 ** ADAM_STEP
    change = first / correction / (jnp.sqrt(second / correction) + 1e-08) + 0.1 * weight
    return (weight - 0.1 * change, jnp.stack([first, second]))

def reference(stream, cotangent, w_input, w_rates, w_conv, w_output, w_swiglu, w_down, w_gains, w_scale, w_heads, m_input, m_rates, m_conv, m_output, m_swiglu, m_down, m_gains, m_scale, m_heads):
    result, pullback = jax.vjp(forward, stream, w_input, w_rates, w_conv, w_output, w_swiglu, w_down, w_gains, w_scale, w_heads)
    grad_stream, g_input, g_rates, g_conv, g_output, g_swiglu, g_down, g_gains, g_scale, g_heads = pullback(cotangent)
    count = float(TOKENS)
    new_input, moment_input = adam_update(w_input, g_input, m_input, count)
    new_rates, moment_rates = adam_update(w_rates, g_rates, m_rates, count)
    new_conv, moment_conv = adam_update(w_conv, g_conv, m_conv, count)
    new_output, moment_output = adam_update(w_output, g_output, m_output, count)
    new_swiglu, moment_swiglu = adam_update(w_swiglu, g_swiglu, m_swiglu, count)
    new_down, moment_down = adam_update(w_down, g_down, m_down, count)
    new_gains, moment_gains = adam_update(w_gains, g_gains, m_gains, count)
    new_scale, moment_scale = adam_update(w_scale, g_scale, m_scale, count)
    new_heads, moment_heads = adam_update(w_heads, g_heads, m_heads, count)
    return (result, grad_stream, g_input, g_rates, g_conv, g_output, g_swiglu, g_down, g_gains, g_scale, g_heads, new_input, new_rates, new_conv, new_output, new_swiglu, new_down, new_gains, new_scale, new_heads, moment_input, moment_rates, moment_conv, moment_output, moment_swiglu, moment_down, moment_gains, moment_scale, moment_heads)
```

```python
import jax
import jax.numpy as jnp
from jax import lax
from jax.sharding import PartitionSpec as P

DK = 128
DV = 256
KCONV = 4
BLOCK = 64
ADAM_STEP = 5


HIGHEST = lax.Precision.HIGHEST


def passed_along(block, axis, distance):
    devices = range(lax.axis_size(axis))
    route = [(i - distance, i) for i in devices if i - distance in devices]
    return lax.ppermute(block, axis, route)


def rms_norm(rows, gain):
    return rows * lax.rsqrt(jnp.mean(rows * rows, axis=-1, keepdims=True) + 1e-06) * gain


def finish(mixer_out, gate_raw, scale_gain):
    factor = lax.rsqrt(jnp.mean(mixer_out * mixer_out, axis=-1, keepdims=True) + 1e-05)
    return mixer_out * factor * scale_gain * jax.nn.silu(gate_raw)


def prepare(mixed_rows, before, conv_weight, decay_raw, update_raw, head_rates):
    length = mixed_rows.shape[1]
    padded = jnp.concatenate([before, mixed_rows], axis=1)
    filtered = conv_weight[0] * padded[:, 0:length]
    for tap_index in range(1, conv_weight.shape[0]):
        filtered = filtered + conv_weight[tap_index] * padded[:, tap_index : tap_index + length]
    filtered = jax.nn.silu(filtered)
    query_raw = filtered[..., :DK]
    key_raw = filtered[..., DK : 2 * DK]
    query = (
        query_raw
        * lax.rsqrt(jnp.sum(query_raw * query_raw, axis=-1, keepdims=True) + 1e-06)
        * DK ** (-0.5)
    )
    key_rows = key_raw * lax.rsqrt(jnp.sum(key_raw * key_raw, axis=-1, keepdims=True) + 1e-06)
    value_rows = filtered[..., 2 * DK :]
    update_gate = jax.nn.sigmoid(update_raw)
    log_decay = -jnp.exp(head_rates[0]) * jax.nn.softplus(decay_raw + head_rates[1])
    return (query, key_rows, value_rows, update_gate, log_decay)


def block_parts(query, key_rows, value_rows, update_gate, log_decay):
    length = query.shape[1]
    cumulative = jnp.cumsum(log_decay, axis=1)
    row_index = lax.broadcasted_iota(jnp.int32, (length, length), 0)
    column_index = lax.broadcasted_iota(jnp.int32, (length, length), 1)
    within = (row_index >= column_index)[None, :, :, None]
    strict = (row_index > column_index)[None, :, :, None]
    distance = cumulative[:, :, None, :] - cumulative[:, None, :, :]
    fade_within = jnp.where(within, jnp.exp(jnp.where(within, distance, 0.0)), 0.0)
    fade_strict = jnp.where(strict, fade_within, 0.0)
    key_products = jnp.einsum("bihk,bjhk->bijh", key_rows, key_rows, precision=HIGHEST)
    lower_part = update_gate[:, :, None, :] * key_products * fade_strict
    identity = jnp.eye(length, dtype=jnp.float32)
    system = identity + jnp.transpose(lower_part, (0, 3, 1, 2))
    growth = jnp.exp(cumulative)
    right_keys = jnp.transpose((update_gate * growth)[..., None] * key_rows, (0, 2, 1, 3))
    right_values = jnp.transpose(update_gate[..., None] * value_rows, (0, 2, 1, 3))
    solved_keys = jax.scipy.linalg.solve_triangular(
        system, right_keys, lower=True, unit_diagonal=True
    )
    solved_values = jax.scipy.linalg.solve_triangular(
        system, right_values, lower=True, unit_diagonal=True
    )
    head_query = jnp.transpose(query, (0, 2, 1, 3))
    scores = jnp.einsum("bhik,bjhk->bhij", head_query, key_rows, precision=HIGHEST) * jnp.transpose(
        fade_within, (0, 3, 1, 2)
    )
    carried_scale = jnp.transpose(growth, (0, 2, 1))[..., None]
    trailing = jnp.exp(cumulative[:, -1:, :] - cumulative)
    faded_keys = jnp.transpose(trailing[..., None] * key_rows, (0, 2, 1, 3))
    final_decay = jnp.exp(cumulative[:, -1, :])[:, :, None, None]
    return (solved_keys, solved_values, head_query, scores, carried_scale, faded_keys, final_decay)


def state_step(states, parts):
    solved_keys, solved_values, head_query, scores, carried_scale, faded_keys, final_decay = parts
    fresh_values = solved_values - jnp.einsum(
        "bhck,bhkw->bhcw", solved_keys, states, precision=HIGHEST
    )
    carried = carried_scale * jnp.einsum("bhck,bhkw->bhcw", head_query, states, precision=HIGHEST)
    output = carried + jnp.einsum("bhij,bhjw->bhiw", scores, fresh_values, precision=HIGHEST)
    next_states = final_decay * states + jnp.einsum(
        "bhck,bhcw->bhkw", faded_keys, fresh_values, precision=HIGHEST
    )
    return (next_states, jnp.transpose(output, (0, 2, 1, 3)))


def split_blocks(array):
    batches = array.shape[0]
    block_count = array.shape[1] // BLOCK
    return jnp.moveaxis(array.reshape((batches, block_count, BLOCK) + array.shape[2:]), 1, 0)


def all_parts(query, key_rows, value_rows, update_gate, log_decay):
    blocked = [
        split_blocks(array) for array in (query, key_rows, value_rows, update_gate, log_decay)
    ]
    block_count = blocked[0].shape[0]
    merged = [array.reshape((-1,) + array.shape[2:]) for array in blocked]
    parts = block_parts(merged[0], merged[1], merged[2], merged[3], merged[4])
    return tuple((array.reshape((block_count, -1) + array.shape[1:]) for array in parts))


def run_blocks(states, query, key_rows, value_rows, update_gate, log_decay):
    batches = query.shape[0]
    length = query.shape[1]
    parts = all_parts(query, key_rows, value_rows, update_gate, log_decay)
    final_states, outputs = lax.scan(jax.checkpoint(state_step), states, parts)
    outputs = jnp.moveaxis(outputs, 0, 1)
    return (outputs.reshape((batches, length) + outputs.shape[3:]), final_states)


def state_back(carried_grad, inputs):
    parts, output_grad = inputs

    def only_states(states):
        return state_step(states, parts)

    unused, pull = jax.vjp(only_states, jnp.zeros_like(carried_grad))
    return (pull((carried_grad, output_grad))[0], None)


def states_gradient(zero_states, grad_out, query, key_rows, value_rows, update_gate, log_decay):
    parts = all_parts(query, key_rows, value_rows, update_gate, log_decay)
    result_grad, unused = lax.scan(
        state_back, zero_states, (parts, split_blocks(grad_out)), reverse=True
    )
    return result_grad


def apply_map(matrix, states):
    return jnp.einsum("bhkj,bhjw->bhkw", matrix, states, precision=HIGHEST)


def contract_rows(left, right):
    return lax.dot_general(
        left, right, (((0,), (0,)), ((), ())), preferred_element_type=jnp.float32
    )


def contract_cols(left, right):
    return lax.dot_general(
        left, right, (((1,), (1,)), ((), ())), preferred_element_type=jnp.float32
    )


def adam_update(weight, gradient, moments, token_count):
    mean_grad = gradient / token_count
    first = 0.5 * moments[0] + 0.5 * mean_grad
    second = 0.5 * moments[1] + 0.5 * mean_grad * mean_grad
    correction = 1.0 - 0.5**ADAM_STEP
    change = first / correction / (jnp.sqrt(second / correction) + 1e-08) + 0.1 * weight
    return (weight - 0.1 * change, jnp.stack([first, second]))


def body(
    stream,
    cotangent,
    w_input,
    w_rates,
    w_conv,
    w_output,
    w_swiglu,
    w_down,
    w_gains,
    w_scale,
    w_heads,
    m_input,
    m_rates,
    m_conv,
    m_output,
    m_swiglu,
    m_down,
    m_gains,
    m_scale,
    m_heads,
):
    rounded_weights = (
        w_input.astype(jnp.bfloat16),
        w_rates.astype(jnp.bfloat16),
        w_output.astype(jnp.bfloat16),
        w_swiglu.astype(jnp.bfloat16),
        w_down.astype(jnp.bfloat16),
    )
    full_input, full_rates, full_output, full_swiglu, full_down = (
        lax.all_gather(rounded_weights[0], ("dp", "seq"), axis=0, tiled=True),
        lax.all_gather(rounded_weights[1], ("dp", "seq"), axis=0, tiled=True),
        lax.all_gather(rounded_weights[2], ("dp", "seq"), axis=2, tiled=True),
        lax.all_gather(rounded_weights[3], ("dp", "seq"), axis=0, tiled=True),
        lax.all_gather(rounded_weights[4], ("dp", "seq"), axis=1, tiled=True),
    )
    tokens_dev = stream.shape[0]
    width = stream.shape[1]
    heads_local = full_input.shape[1]
    input_cols = full_input.shape[2]
    units_local = full_swiglu.shape[2]
    conv_cols = 2 * DK + DV
    first_head = lax.axis_index("tensor") * heads_local
    conv_local = lax.dynamic_slice_in_dim(w_conv, first_head, heads_local, 1)
    rates_local = lax.dynamic_slice_in_dim(w_heads, first_head, heads_local, 1)
    normed_in, norm_in_pull = jax.vjp(rms_norm, stream, w_gains[0])
    normed_in_low = normed_in.astype(jnp.bfloat16)
    projected = jnp.dot(
        normed_in_low, full_input.reshape(width, -1), preferred_element_type=jnp.float32
    ).reshape(tokens_dev, heads_local, input_cols)
    rates = jnp.dot(
        normed_in_low, full_rates.reshape(width, -1), preferred_element_type=jnp.float32
    ).reshape(tokens_dev, heads_local, 2)
    conv_input = projected[:, :, :conv_cols]
    before = passed_along(conv_input[tokens_dev - (KCONV - 1) :], "seq", 1)
    prepared, prepare_pull = jax.vjp(
        prepare,
        conv_input[None],
        before[None],
        conv_local,
        rates[None, :, :, 0],
        rates[None, :, :, 1],
        rates_local,
    )
    query, key_rows, value_rows, update_gate, log_decay = prepared
    zero_states = jnp.zeros((1, heads_local, DK, DV), jnp.float32)
    identity_maps = jnp.broadcast_to(jnp.eye(DK, dtype=jnp.float32), (1, heads_local, DK, DK))
    widened = jnp.concatenate(
        [value_rows, jnp.zeros(value_rows.shape[:-1] + (DK,), jnp.float32)], axis=-1
    )
    widened_start = jnp.concatenate([zero_states, identity_maps], axis=-1)
    ignored, transfer_state = run_blocks(
        widened_start, query, key_rows, widened, update_gate, log_decay
    )
    offset_map = transfer_state[..., :DV]
    linear_map = transfer_state[..., DV:]
    incoming = zero_states
    for hop_index in range(lax.axis_size("seq") - 1):
        incoming = passed_along(apply_map(linear_map, incoming) + offset_map, "seq", 1)
    delta_result, delta_pull = jax.vjp(
        run_blocks, incoming, query, key_rows, value_rows, update_gate, log_decay
    )
    mixer_out = delta_result[0]
    mixed, finish_pull = jax.vjp(finish, mixer_out, projected[None, :, :, conv_cols:], w_scale)
    mixed_low = mixed.astype(jnp.bfloat16).reshape(tokens_dev, heads_local * DV)
    attention = lax.psum(
        jnp.dot(
            mixed_low,
            full_output.reshape(heads_local * DV, width),
            preferred_element_type=jnp.float32,
        ).astype(jnp.bfloat16),
        "tensor",
    ).astype(jnp.float32)
    residual = stream + attention
    normed_mid, norm_mid_pull = jax.vjp(rms_norm, residual, w_gains[1])
    normed_mid_low = normed_mid.astype(jnp.bfloat16)
    gate_up = jnp.dot(
        normed_mid_low, full_swiglu.reshape(width, -1), preferred_element_type=jnp.float32
    ).reshape(tokens_dev, 2, units_local)
    gate_part = gate_up[:, 0]
    up_part = gate_up[:, 1]
    sigmoid_gate = jax.nn.sigmoid(gate_part)
    silu_gate = gate_part * sigmoid_gate
    activated_low = (silu_gate * up_part).astype(jnp.bfloat16)
    feedforward = lax.psum(
        jnp.dot(activated_low, full_down, preferred_element_type=jnp.float32).astype(jnp.bfloat16),
        "tensor",
    ).astype(jnp.float32)
    result = residual + feedforward
    grad_ffn = cotangent.astype(jnp.bfloat16)
    grad_down_full = contract_rows(activated_low, grad_ffn)
    grad_activated = contract_cols(grad_ffn, full_down)
    grad_gate = grad_activated * up_part * sigmoid_gate * (1.0 + gate_part * (1.0 - sigmoid_gate))
    grad_up = grad_activated * silu_gate
    grad_gate_up = (
        jnp.stack([grad_gate, grad_up], axis=1)
        .astype(jnp.bfloat16)
        .reshape(tokens_dev, 2 * units_local)
    )
    grad_swiglu_full = contract_rows(normed_mid_low, grad_gate_up).reshape(width, 2, units_local)
    grad_normed_mid = lax.psum(
        contract_cols(grad_gate_up, full_swiglu.reshape(width, 2 * units_local)).astype(
            jnp.bfloat16
        ),
        "tensor",
    ).astype(jnp.float32)
    grad_from_mid, grad_gain_mid = norm_mid_pull(grad_normed_mid)
    grad_residual = cotangent + grad_from_mid
    grad_attention = grad_residual.astype(jnp.bfloat16)
    grad_output_full = contract_rows(mixed_low, grad_attention).reshape(heads_local, DV, width)
    grad_mixed = contract_cols(
        grad_attention, full_output.reshape(heads_local * DV, width)
    ).reshape(1, tokens_dev, heads_local, DV)
    grad_mixer_out, grad_gate_raw, grad_scale = finish_pull(grad_mixed)
    correction = states_gradient(
        zero_states, grad_mixer_out, query, key_rows, value_rows, update_gate, log_decay
    )
    linear_turned = jnp.swapaxes(linear_map, -1, -2)
    outgoing = zero_states
    for hop_index in range(lax.axis_size("seq") - 1):
        outgoing = passed_along(apply_map(linear_turned, outgoing) + correction, "seq", -1)
    delta_grads = delta_pull((grad_mixer_out, outgoing))
    (
        grad_conv_rows,
        grad_before,
        grad_conv_local,
        grad_decay_raw,
        grad_update_raw,
        grad_rates_local,
    ) = prepare_pull(delta_grads[1:])
    returned = passed_along(grad_before[0], "seq", -1)
    grad_rows = grad_conv_rows[0].at[tokens_dev - (KCONV - 1) :].add(returned)
    grad_projected = (
        jnp.concatenate([grad_rows, grad_gate_raw[0]], axis=-1)
        .astype(jnp.bfloat16)
        .reshape(tokens_dev, heads_local * input_cols)
    )
    grad_rate_rows = (
        jnp.stack([grad_decay_raw[0], grad_update_raw[0]], axis=-1)
        .astype(jnp.bfloat16)
        .reshape(tokens_dev, heads_local * 2)
    )
    grad_input_full = contract_rows(normed_in_low, grad_projected).reshape(
        width, heads_local, input_cols
    )
    grad_rates_full = contract_rows(normed_in_low, grad_rate_rows).reshape(width, heads_local, 2)
    normed_in_term = contract_cols(
        grad_projected, full_input.reshape(width, heads_local * input_cols)
    ) + contract_cols(grad_rate_rows, full_rates.reshape(width, heads_local * 2))
    grad_normed_in = lax.psum(normed_in_term.astype(jnp.bfloat16), "tensor").astype(jnp.float32)
    grad_from_in, grad_gain_in = norm_in_pull(grad_normed_in)
    grad_stream = grad_residual + grad_from_in
    reduced = (
        lax.psum_scatter(grad_input_full.astype(jnp.bfloat16), ("dp", "seq"), scatter_dimension=0, tiled=True),
        lax.psum_scatter(grad_rates_full.astype(jnp.bfloat16), ("dp", "seq"), scatter_dimension=0, tiled=True),
        lax.psum_scatter(grad_output_full.astype(jnp.bfloat16), ("dp", "seq"), scatter_dimension=2, tiled=True),
        lax.psum_scatter(grad_swiglu_full.astype(jnp.bfloat16), ("dp", "seq"), scatter_dimension=0, tiled=True),
        lax.psum_scatter(grad_down_full.astype(jnp.bfloat16), ("dp", "seq"), scatter_dimension=1, tiled=True),
    )
    g_input, g_rates, g_output, g_swiglu, g_down = [g.astype(jnp.float32) for g in reduced]
    conv_term = lax.dynamic_update_slice_in_dim(
        jnp.zeros_like(w_conv), grad_conv_local, first_head, 1
    )
    heads_term = lax.dynamic_update_slice_in_dim(
        jnp.zeros_like(w_heads), grad_rates_local, first_head, 1
    )
    slice_width = width // lax.axis_size("tensor")
    owned = lax.broadcasted_iota(jnp.int32, (1, width), 1) // slice_width == lax.axis_index(
        "tensor"
    )
    gains_term = jnp.where(owned, jnp.stack([grad_gain_in, grad_gain_mid]), 0.0)
    g_conv, g_heads, g_gains, g_scale = lax.psum(
        (conv_term, heads_term, gains_term, grad_scale), ("dp", "seq", "tensor")
    )
    count = float(tokens_dev * lax.axis_size("dp") * lax.axis_size("seq"))
    new_input, moment_input = adam_update(w_input, g_input, m_input, count)
    new_rates, moment_rates = adam_update(w_rates, g_rates, m_rates, count)
    new_conv, moment_conv = adam_update(w_conv, g_conv, m_conv, count)
    new_output, moment_output = adam_update(w_output, g_output, m_output, count)
    new_swiglu, moment_swiglu = adam_update(w_swiglu, g_swiglu, m_swiglu, count)
    new_down, moment_down = adam_update(w_down, g_down, m_down, count)
    new_gains, moment_gains = adam_update(w_gains, g_gains, m_gains, count)
    new_scale, moment_scale = adam_update(w_scale, g_scale, m_scale, count)
    new_heads, moment_heads = adam_update(w_heads, g_heads, m_heads, count)
    return (
        result,
        grad_stream,
        g_input,
        g_rates,
        g_conv,
        g_output,
        g_swiglu,
        g_down,
        g_gains,
        g_scale,
        g_heads,
        new_input,
        new_rates,
        new_conv,
        new_output,
        new_swiglu,
        new_down,
        new_gains,
        new_scale,
        new_heads,
        moment_input,
        moment_rates,
        moment_conv,
        moment_output,
        moment_swiglu,
        moment_down,
        moment_gains,
        moment_scale,
        moment_heads,
    )


def solution(mesh):
    in_specs = (
        P(("dp", "seq"), None),
        P(("dp", "seq"), None),
        P(("dp", "seq"), "tensor", None),
        P(("dp", "seq"), "tensor", None),
        P(),
        P("tensor", None, ("dp", "seq")),
        P(("dp", "seq"), None, "tensor"),
        P("tensor", ("dp", "seq")),
        P(),
        P(),
        P(),
        P(None, ("dp", "seq"), "tensor", None),
        P(None, ("dp", "seq"), "tensor", None),
        P(),
        P(None, "tensor", None, ("dp", "seq")),
        P(None, ("dp", "seq"), None, "tensor"),
        P(None, "tensor", ("dp", "seq")),
        P(),
        P(),
        P(),
    )
    out_specs = (
        P(("dp", "seq"), None),
        P(("dp", "seq"), None),
        P(("dp", "seq"), "tensor", None),
        P(("dp", "seq"), "tensor", None),
        P(),
        P("tensor", None, ("dp", "seq")),
        P(("dp", "seq"), None, "tensor"),
        P("tensor", ("dp", "seq")),
        P(),
        P(),
        P(),
        P(("dp", "seq"), "tensor", None),
        P(("dp", "seq"), "tensor", None),
        P(),
        P("tensor", None, ("dp", "seq")),
        P(("dp", "seq"), None, "tensor"),
        P("tensor", ("dp", "seq")),
        P(),
        P(),
        P(),
        P(None, ("dp", "seq"), "tensor", None),
        P(None, ("dp", "seq"), "tensor", None),
        P(),
        P(None, "tensor", None, ("dp", "seq")),
        P(None, ("dp", "seq"), None, "tensor"),
        P(None, "tensor", ("dp", "seq")),
        P(),
        P(),
        P(),
    )
    return jax.shard_map(body, mesh=mesh, in_specs=in_specs, out_specs=out_specs, check_vma=False)
```

```python
import functools

import jax
import jax.numpy as jnp
from jax import lax
from jax.experimental import pallas as pl
from jax.experimental.pallas import tpu as pltpu
from jax.sharding import PartitionSpec as P

DK = 128
DV = 256
QKV = 2 * DK + DV
KCONV = 4
CHUNK = 128
ADAM_STEP = 5
VMEM = 48 * 2**20

F32 = jnp.float32
BF16 = jnp.bfloat16
HIGHEST = lax.Precision.HIGHEST

NN = (((1,), (0,)), ((), ()))
NT = (((1,), (1,)), ((), ()))
TN = (((0,), (0,)), ((), ()))


def dot(left, right, dims):
    return lax.dot_general(left, right, dims, preferred_element_type=F32)


def halves(array):
    high = array.astype(BF16)
    return high, (array - high.astype(F32)).astype(BF16)


def mm(left, right, dims=NN):
    left_high, left_low = halves(left)
    right_high, right_low = halves(right)
    return (
        dot(left_high, right_high, dims)
        + dot(left_high, right_low, dims)
        + dot(left_low, right_high, dims)
    )


def each(function, *lists):
    return [function(*items) for items in zip(*lists)]


def unit_lower_inverses(strict_parts, row_index, column_index):
    size = strict_parts[0].shape[0]
    identity = (row_index == column_index).astype(F32)
    same = (row_index // 8) == (column_index // 8)
    small = [jnp.where(same, part, 0.0) for part in strict_parts]
    squared = each(mm, small, small)
    fourth = each(mm, squared, squared)
    first = each(lambda n, n2: mm(identity - n, identity + n2), small, squared)
    inverse = each(lambda a, n4: a + mm(a, n4), first, fourth)
    width = 8
    while width < size:
        pair = (row_index // (2 * width)) == (column_index // (2 * width))
        below = pair & ((row_index // width) != (column_index // width))
        lower = [jnp.where(below, part, 0.0) for part in strict_parts]
        inner = each(mm, lower, inverse)
        inverse = each(lambda x, y: x - mm(x, y), inverse, inner)
        width *= 2
    return inverse


def silu_parts(values):
    gate = 1.0 / (1.0 + jnp.exp(-values))
    return values * gate, gate


def filtered_parts(padded_ref, rows_ref, halo_ref, taps_ref):
    length = rows_ref.shape[0]
    padded_ref[0:8, :] = halo_ref[0]
    padded_ref[8 : 8 + length, :] = rows_ref[...]
    raw = taps_ref[0:1, :] * padded_ref[5 : 5 + length, :]
    for tap in range(1, KCONV):
        raw = raw + taps_ref[tap : tap + 1, :] * padded_ref[5 + tap : 5 + tap + length, :]
    filtered, gate = silu_parts(raw)
    return raw, gate, filtered


def unit_rows(rows):
    factor = lax.rsqrt(jnp.sum(rows * rows, axis=-1, keepdims=True) + 1e-06)
    return rows * factor, factor


def chunk_slices(array, count):
    return [array[i * CHUNK : (i + 1) * CHUNK] for i in range(count)]


def fades(columns, g_rows, row_index, column_index):
    within = row_index >= column_index
    result = []
    for i, column in enumerate(columns):
        gap = column[:, 1:2] - g_rows[0:1, i * CHUNK : (i + 1) * CHUNK]
        result.append(jnp.where(within, jnp.exp(jnp.where(within, gap, 0.0)), 0.0))
    return result


def forward_kernel(
    rows_ref,
    halo_ref,
    taps_ref,
    columns_ref,
    g_rows_ref,
    reach_ref,
    local_ref,
    end_ref,
    starts_ref,
    inverse_ref,
    solved_values_ref,
    solved_keys_ref,
    step_ref,
    seen_ref,
    padded_ref,
):
    length = rows_ref.shape[0]
    count = length // CHUNK
    raw, gate, filtered = filtered_parts(padded_ref, rows_ref, halo_ref, taps_ref)
    query = unit_rows(filtered[:, :DK])[0] * DK ** (-0.5)
    key = unit_rows(filtered[:, DK : 2 * DK])[0]
    value = filtered[:, 2 * DK :]
    row_index = lax.broadcasted_iota(jnp.int32, (CHUNK, CHUNK), 0)
    column_index = lax.broadcasted_iota(jnp.int32, (CHUNK, CHUNK), 1)
    identity = (row_index == column_index).astype(F32)
    strict = row_index > column_index
    queries, keys, values = (chunk_slices(a, count) for a in (query, key, value))
    columns = chunk_slices(columns_ref[0], count)
    fade = fades(columns, g_rows_ref[0], row_index, column_index)
    key_products = each(lambda k: mm(k, k, NT), keys)
    parts = each(
        lambda kk, f, c: jnp.where(strict, c[:, 0:1] * kk * f, 0.0), key_products, fade, columns
    )
    inverses = unit_lower_inverses(parts, row_index, column_index)
    scores = each(lambda q, k, f: mm(q, k, NT) * f, queries, keys, fade)
    solved_values = each(lambda t, v, c: mm(t, c[:, 0:1] * v), inverses, values, columns)
    solved_keys = each(lambda t, k, c: mm(t, c[:, 0:1] * c[:, 2:3] * k), inverses, keys, columns)
    seen = each(
        lambda q, s, w, c: c[:, 2:3] * q - mm(s, w), queries, scores, solved_keys, columns
    )
    inner = each(mm, scores, solved_values)
    faded = each(lambda k, c: (c[:, 3:4] * k).T, keys, columns)
    steps = each(
        lambda k, w, c: c[CHUNK - 1 : CHUNK, 2:3] * identity - mm(k, w),
        faded,
        solved_keys,
        columns,
    )
    added = each(mm, faded, solved_values)
    state = jnp.concatenate([jnp.zeros((DK, DV), F32), identity], axis=1)
    for i in range(count):
        here = slice(i * CHUNK, (i + 1) * CHUNK)
        starts_ref[0, i] = state
        reached = mm(seen[i], state)
        local_ref[0, here, :] = reached[:, :DV] + inner[i]
        reach_ref[0, here, :] = reached[:, DV:]
        state = mm(steps[i], state)
        state = jnp.concatenate([state[:, :DV] + added[i], state[:, DV:]], axis=1)
        inverse_ref[0, here, :] = inverses[i]
        solved_values_ref[0, here, :] = solved_values[i]
        solved_keys_ref[0, here, :] = solved_keys[i]
        step_ref[0, here, :] = steps[i]
        seen_ref[0, here, :] = seen[i]
    end_ref[0] = state


def finish_kernel(local_ref, reach_ref, state_ref, gate_ref, scale_ref, mixed_ref):
    mixer_out = local_ref[0] + mm(reach_ref[0], state_ref[0])
    factor = lax.rsqrt(jnp.mean(mixer_out * mixer_out, axis=-1, keepdims=True) + 1e-05)
    opened = silu_parts(gate_ref[...])[0]
    mixed_ref[...] = (mixer_out * factor * scale_ref[...] * opened).astype(BF16)


def finish_back_kernel(
    local_ref,
    reach_ref,
    state_ref,
    gate_ref,
    scale_ref,
    grad_ref,
    grad_out_ref,
    grad_gate_ref,
    grad_scale_ref,
    correction_ref,
):
    mixer_out = local_ref[0] + mm(reach_ref[0], state_ref[0])
    factor = lax.rsqrt(jnp.mean(mixer_out * mixer_out, axis=-1, keepdims=True) + 1e-05)
    normal = mixer_out * factor
    gate_raw = gate_ref[...]
    opened, gate = silu_parts(gate_raw)
    grad = grad_ref[...]
    scale = scale_ref[...]
    with_normal = grad * normal
    grad_gate_ref[...] = (
        with_normal * scale * gate * (1.0 + gate_raw * (1.0 - gate))
    ).astype(BF16)
    summed = jnp.sum(with_normal * opened, axis=0, keepdims=True)
    grad_scale_ref[0] = jnp.broadcast_to(summed, (8, DV))
    grad_normal = grad * scale * opened
    shared = jnp.mean(grad_normal * normal, axis=-1, keepdims=True)
    grad_out = factor * (grad_normal - normal * shared)
    grad_out_ref[0] = grad_out
    correction_ref[0] = mm(reach_ref[0].T, grad_out)


def backward_kernel(
    rows_ref,
    halo_ref,
    taps_ref,
    columns_ref,
    g_rows_ref,
    starts_ref,
    inverse_ref,
    solved_values_ref,
    solved_keys_ref,
    step_ref,
    seen_ref,
    state_ref,
    later_ref,
    grad_out_ref,
    grad_rows_ref,
    tail_ref,
    before_ref,
    grad_taps_ref,
    grad_columns_ref,
    padded_ref,
    grad_padded_ref,
):
    length = rows_ref.shape[0]
    count = length // CHUNK
    raw, gate, filtered = filtered_parts(padded_ref, rows_ref, halo_ref, taps_ref)
    query_unit, query_factor = unit_rows(filtered[:, :DK])
    key, key_factor = unit_rows(filtered[:, DK : 2 * DK])
    query = query_unit * DK ** (-0.5)
    value = filtered[:, 2 * DK :]
    row_index = lax.broadcasted_iota(jnp.int32, (CHUNK, CHUNK), 0)
    column_index = lax.broadcasted_iota(jnp.int32, (CHUNK, CHUNK), 1)
    strict = row_index > column_index
    last = lax.broadcasted_iota(jnp.int32, (CHUNK, 1), 0) == CHUNK - 1
    queries, keys, values = (chunk_slices(a, count) for a in (query, key, value))
    columns = chunk_slices(columns_ref[0], count)
    inverses = chunk_slices(inverse_ref[0], count)
    solved_values = chunk_slices(solved_values_ref[0], count)
    solved_keys = chunk_slices(solved_keys_ref[0], count)
    steps = chunk_slices(step_ref[0], count)
    seen = chunk_slices(seen_ref[0], count)
    grad_outs = chunk_slices(grad_out_ref[0], count)
    fade = fades(columns, g_rows_ref[0], row_index, column_index)
    incoming = state_ref[0]
    states = [starts_ref[0, i][:, :DV] + mm(starts_ref[0, i][:, DV:], incoming) for i in range(count)]
    own_grads = each(lambda s, o: mm(s.T, o), seen, grad_outs)
    later = [None] * count
    carried = later_ref[0]
    for i in reversed(range(count)):
        later[i] = carried
        if i > 0:
            carried = mm(steps[i].T, carried) + own_grads[i]
    key_products = each(lambda k: mm(k, k, NT), keys)
    query_products = each(lambda q, k: mm(q, k, NT), queries, keys)
    scores = each(lambda p, f: p * f, query_products, fade)
    fresh = each(lambda u, w, s: u - mm(w, s), solved_values, solved_keys, states)
    faded = each(lambda k, c: c[:, 3:4] * k, keys, columns)
    grad_fresh = each(
        lambda p, o, k, l: mm(p.T, o) + mm(k, l), scores, grad_outs, faded, later
    )
    grad_scaled = each(lambda t, g: mm(t.T, g), inverses, grad_fresh)
    grad_scaled_keys = each(lambda g, s: -mm(g, s, NT), grad_scaled, states)
    grad_lower = each(
        lambda g, f: jnp.where(strict, -mm(g, f, NT), 0.0), grad_scaled, fresh
    )
    grad_scores = each(lambda o, f, d: mm(o, f, NT) * d, grad_outs, fresh, fade)
    lower_fade = each(lambda g, d: g * d, grad_lower, fade)
    pairs = each(lambda h, c: c[:, 0:1] * h, lower_fade, columns)
    from_state = each(lambda o, s: mm(o, s, NT), grad_outs, states)
    from_later = each(lambda f, l: mm(f, l, NT), fresh, later)
    grad_queries = each(
        lambda c, a, g, k: c[:, 2:3] * a + mm(g, k), columns, from_state, grad_scores, keys
    )
    grad_keys = each(
        lambda c, b, p, k, g, q, e: c[:, 0:1] * c[:, 2:3] * b
        + mm(p + p.T, k)
        + mm(g.T, q)
        + c[:, 3:4] * e,
        columns,
        grad_scaled_keys,
        pairs,
        keys,
        grad_scores,
        queries,
        from_later,
    )
    grad_values = each(lambda c, g: c[:, 0:1] * g, columns, grad_scaled)

    def across(array):
        return jnp.sum(array, axis=-1, keepdims=True)

    for i in range(count):
        column = columns[i]
        key_term = column[:, 2:3] * across(grad_scaled_keys[i] * keys[i])
        grad_update = (
            across(grad_scaled[i] * values[i])
            + key_term
            + across(lower_fade[i] * key_products[i])
        )
        both = grad_scores[i] * query_products[i] + pairs[i] * key_products[i]
        trailing = column[:, 3:4] * across(keys[i] * from_later[i])
        whole = column[CHUNK - 1 : CHUNK, 2:3] * jnp.sum(
            across(later[i] * states[i]), axis=0, keepdims=True
        ) + jnp.sum(trailing, axis=0, keepdims=True)
        grad_g = (
            across(both - both.T)
            + column[:, 2:3] * across(queries[i] * from_state[i])
            + column[:, 0:1] * key_term
            - trailing
            + jnp.where(last, whole, 0.0)
        )
        lane = lax.broadcasted_iota(jnp.int32, (CHUNK, 8), 1)
        grad_columns_ref[0, i * CHUNK : (i + 1) * CHUNK, :] = jnp.where(
            lane == 0, grad_update, grad_g
        )
    grad_query = jnp.concatenate(grad_queries, axis=0) * DK ** (-0.5)
    grad_key = jnp.concatenate(grad_keys, axis=0)
    grad_value = jnp.concatenate(grad_values, axis=0)
    grad_query = query_factor * (grad_query - query_unit * across(query_unit * grad_query))
    grad_key = key_factor * (grad_key - key * across(key * grad_key))
    grad_filtered = jnp.concatenate([grad_query, grad_key, grad_value], axis=1)
    grad_raw = grad_filtered * gate * (1.0 + raw * (1.0 - gate))
    zeros = jnp.zeros((8, QKV), F32)
    grad_padded_ref[0:8, :] = zeros
    grad_padded_ref[8 : 8 + length, :] = grad_raw
    grad_padded_ref[8 + length : 16 + length, :] = zeros
    grad_rows = taps_ref[0:1, :] * grad_padded_ref[11 : 11 + length, :]
    before = taps_ref[0:1, :] * grad_padded_ref[3:11, :]
    for tap in range(1, KCONV):
        tap_row = taps_ref[tap : tap + 1, :]
        grad_rows = grad_rows + tap_row * grad_padded_ref[11 - tap : 11 - tap + length, :]
        before = before + tap_row * grad_padded_ref[3 - tap : 11 - tap, :]
    grad_rows_ref[...] = grad_rows.astype(BF16)
    tail_ref[0] = grad_rows[length - 8 :]
    before_ref[0] = before
    sums = [
        jnp.sum(grad_raw * padded_ref[5 + tap : 5 + tap + length, :], axis=0, keepdims=True)
        for tap in range(KCONV)
    ]
    grad_taps_ref[0] = jnp.concatenate(sums, axis=0)


def chains_call(kernel, chains, heads, length, operands, outputs, scratch, flops):
    def spec(tag, shape):
        if tag == "rows":
            return pl.BlockSpec((length, shape[1] // heads), lambda i: (i // heads, i % heads))
        if tag == "edge":
            return pl.BlockSpec((1, 8, shape[2] // heads), lambda i: (i // heads, 0, i % heads))
        if tag == "taps":
            return pl.BlockSpec((shape[0], shape[1] // heads), lambda i: (0, i % heads))
        if tag == "all":
            return pl.BlockSpec(shape, lambda i: (0,) * len(shape))
        return pl.BlockSpec((1,) + tuple(shape[1:]), lambda i: (i,) + (0,) * (len(shape) - 1))

    moved = sum(a.size * a.dtype.itemsize for _, a in operands)
    return pl.pallas_call(
        kernel,
        grid=(chains,),
        in_specs=[spec(tag, a.shape) for tag, a in operands],
        out_specs=[spec(tag, shape) for tag, shape, _ in outputs],
        out_shape=[jax.ShapeDtypeStruct(shape, dtype) for _, shape, dtype in outputs],
        scratch_shapes=scratch,
        compiler_params=pltpu.CompilerParams(vmem_limit_bytes=VMEM),
        cost_estimate=pl.CostEstimate(
            flops=chains * flops, bytes_accessed=2 * moved, transcendentals=0
        ),
    )(*[a for _, a in operands])


def shifted(block, axis, distance):
    devices = range(lax.axis_size(axis))
    route = [(i, i + distance) for i in devices if i + distance in devices]
    return lax.ppermute(block, axis, route)


def swapped(block, axis, bits):
    return lax.ppermute(block, axis, [(i, i ^ bits) for i in range(lax.axis_size(axis))])


def group_swapped(block, dp_bits, tensor_bits):
    dp_size, tensor_size = lax.axis_size("dp"), lax.axis_size("tensor")
    route = [
        (d * tensor_size + t, (d ^ dp_bits) * tensor_size + (t ^ tensor_bits))
        for d in range(dp_size)
        for t in range(tensor_size)
    ]
    return lax.ppermute(block, ("dp", "tensor"), route)


def partner_bits():
    chips = lax.axis_size("tensor") // 2
    return [(d, t) for d in range(lax.axis_size("dp")) for t in range(chips) if (d, t) != (0, 0)]


def bits_slot(dp_bits, chip_bits):
    return dp_bits * (lax.axis_size("tensor") // 2) + chip_bits


def scatter_relative(partial):
    half = partial.shape[0] // 2
    summed = partial[:half].astype(F32) + swapped(partial[half:], "tensor", 1).astype(F32)
    rows = half // (lax.axis_size("dp") * lax.axis_size("tensor") // 2)
    total = summed[:rows]
    low = summed.astype(BF16)
    for d, t in partner_bits():
        slot = bits_slot(d, t)
        received = group_swapped(low[slot * rows : (slot + 1) * rows], d, 2 * t)
        total = total + received.astype(F32)
    return total


def gather_relative(own):
    parts = [own] + [group_swapped(own, d, 2 * t) for d, t in partner_bits()]
    here = jnp.concatenate(parts, axis=0)
    return jnp.concatenate([here, swapped(here, "tensor", 1)], axis=0)


def scatter_absolute(partial):
    dp_size, chips = lax.axis_size("dp"), lax.axis_size("tensor") // 2
    core = lax.axis_index("tensor") % 2
    chip = lax.axis_index("tensor") // 2
    device = lax.axis_index("dp")
    rows = partial.shape[0] // (2 * dp_size * chips)
    blocks = partial.reshape(dp_size * chips, 2, rows, -1)
    even, odd = blocks[:, 0], blocks[:, 1]
    mine = jnp.where(core == 0, even, odd)
    theirs = jnp.where(core == 0, odd, even)
    summed = mine.astype(F32) + swapped(theirs, "tensor", 1).astype(F32)
    low = summed.astype(BF16)
    total = lax.dynamic_index_in_dim(summed, device * chips + chip, 0, keepdims=False)
    for d, t in partner_bits():
        target = (device ^ d) * chips + (chip ^ t)
        block = lax.dynamic_index_in_dim(low, target, 0, keepdims=False)
        total = total + group_swapped(block, d, 2 * t).astype(F32)
    return total


def ordered(parts, core, other):
    first = jnp.where(core == 0, parts, other)
    second = jnp.where(core == 0, other, parts)
    stacked = jnp.stack([first, second], axis=1)
    return stacked.reshape((-1,) + parts.shape[2:])


def gather_absolute(own, over_dp=True):
    dp_size = lax.axis_size("dp") if over_dp else 1
    chips = lax.axis_size("tensor") // 2
    core = lax.axis_index("tensor") % 2
    chip = lax.axis_index("tensor") // 2
    device = lax.axis_index("dp") if over_dp else 0
    here = jnp.zeros((dp_size * chips,) + own.shape, own.dtype)
    here = lax.dynamic_update_index_in_dim(here, own, device * chips + chip, 0)
    for d, t in partner_bits():
        if d < dp_size:
            received = group_swapped(own, d, 2 * t)
            source = (device ^ d) * chips + (chip ^ t)
            here = lax.dynamic_update_index_in_dim(here, received, source, 0)
    return ordered(here, core, swapped(here, "tensor", 1))


def butterfly_sum(array):
    for axis in ("tensor", "dp", "seq"):
        distance = 1
        while distance < lax.axis_size(axis):
            array = array + swapped(array, axis, distance)
            distance *= 2
    return array


def contract_cols(left, right):
    return dot(left, right, NT)


def contract_rows(left, right):
    return dot(left, right, TN)


def adam_update(weight, gradient, moments, token_count):
    mean_grad = gradient / token_count
    first = 0.5 * moments[0] + 0.5 * mean_grad
    second = 0.5 * moments[1] + 0.5 * mean_grad * mean_grad
    correction = 1.0 - 0.5**ADAM_STEP
    change = first / correction / (jnp.sqrt(second / correction) + 1e-08) + 0.1 * weight
    return (weight - 0.1 * change, jnp.stack([first, second]))


def norm_parts(rows):
    factor = lax.rsqrt(jnp.mean(rows * rows, axis=-1, keepdims=True) + 1e-06)
    return factor, rows * factor


def norm_back(factor, normal, gain, grad):
    scaled = grad * gain
    shared = jnp.mean(scaled * normal, axis=-1, keepdims=True)
    return factor * (scaled - normal * shared), jnp.sum(grad * normal, axis=0)


def body(
    stream,
    cotangent,
    w_input,
    w_rates,
    w_conv,
    w_output,
    w_swiglu,
    w_down,
    w_gains,
    w_scale,
    w_heads,
    m_input,
    m_rates,
    m_conv,
    m_output,
    m_swiglu,
    m_down,
    m_gains,
    m_scale,
    m_heads,
):
    dp_size, seq_size, tensor_size = (lax.axis_size(a) for a in ("dp", "seq", "tensor"))
    length, width = stream.shape
    depth = w_input.shape[0]
    heads_stored = w_input.shape[1]
    heads = heads_stored // dp_size
    units_stored = w_swiglu.shape[2]
    units = units_stored // dp_size
    rows = length // tensor_size
    chains = dp_size * heads
    first_part = lax.axis_index("dp") == 0
    first_head = lax.axis_index("tensor") * heads_stored + lax.axis_index("dp") * heads

    def turned(array):
        cut = array.reshape(array.shape[:-1] + (dp_size, seq_size, depth))
        return jnp.swapaxes(cut, -3, -2).reshape(array.shape)

    def turned_back(array):
        cut = array.reshape(array.shape[:-1] + (seq_size, dp_size, depth))
        return jnp.swapaxes(cut, -3, -2).reshape(array.shape)

    def mine_and_theirs(low, high):
        return jnp.where(first_part, low, high), jnp.where(first_part, high, low)

    def by_device(own, received):
        return jnp.where(first_part, own, received), jnp.where(first_part, received, own)

    low_input = w_input.astype(BF16)
    low_output = jnp.transpose(w_output.astype(BF16), (2, 0, 1))
    low_swiglu = w_swiglu.astype(BF16)
    low_down = w_down.astype(BF16).T

    def half_columns(index):
        chosen = slice(index * heads, (index + 1) * heads)
        some = slice(index * units, (index + 1) * units)
        return (
            low_input[:, chosen, :QKV].reshape(depth, -1),
            jnp.concatenate(
                [
                    low_input[:, chosen, QKV:].reshape(depth, -1),
                    low_output[:, chosen].reshape(depth, -1),
                ],
                axis=1,
            ),
            jnp.concatenate(
                [low_swiglu[:, 0, some], low_swiglu[:, 1, some], low_down[:, some]], axis=1
            ),
        )

    gathered = []
    for low, high in zip(half_columns(0), half_columns(1)):
        mine, theirs = mine_and_theirs(low, high)
        received = swapped(theirs, "dp", 1)
        shard = jnp.concatenate(by_device(mine, received), axis=0)
        gathered.append(lax.all_gather(shard, "seq", axis=0, tiled=True))
    full_qkv, full_mixer, full_ffn = gathered
    full_gate, full_output = full_mixer[:, : heads * DV], full_mixer[:, heads * DV :]
    full_swiglu, full_down = full_ffn[:, : 2 * units], full_ffn[:, 2 * units :]

    copies = dp_size * seq_size
    rates_low = jnp.broadcast_to(w_rates.astype(BF16).reshape(1, -1), (copies, depth * heads_stored * 2))
    rates_all = lax.all_to_all(rates_low, ("dp", "seq"), 0, 0, tiled=True)
    rates_all = rates_all.reshape(dp_size, seq_size, depth, dp_size, heads * 2)
    rates_all = jnp.swapaxes(rates_all, 0, 1).reshape(width, dp_size, heads * 2)
    full_rates = jnp.where(first_part, rates_all[:, 0], rates_all[:, dp_size - 1])

    quarter = lax.axis_index("tensor") * rows
    stream_rows = turned(lax.dynamic_slice_in_dim(stream, quarter, rows, 0))
    cotangent_rows = turned(lax.dynamic_slice_in_dim(cotangent, quarter, rows, 0))
    gains = turned(w_gains)
    factor_in, normal_in = norm_parts(stream_rows)
    normed_in = gather_absolute((normal_in * gains[0]).astype(BF16)).reshape(-1, width)
    grad_ffn = gather_relative(cotangent_rows.astype(BF16))

    projected = dot(normed_in, full_qkv, NN)
    rates = dot(normed_in, full_rates, NN)
    last_rows = projected.reshape(dp_size, length, heads * QKV)[:, length - 8 :]
    halo = shifted(last_rows, "seq", 1)
    taps = lax.dynamic_slice_in_dim(w_conv, first_head, heads, 1).reshape(KCONV, heads * QKV)
    head_rates = lax.dynamic_slice_in_dim(w_heads, first_head, heads, 1)
    by_chain = jnp.transpose(rates.reshape(dp_size, length, heads, 2), (3, 0, 2, 1))
    decay_raw = by_chain[0] + head_rates[1][None, :, None]
    update = jax.nn.sigmoid(by_chain[1]).reshape(chains, length)
    log_decay = -jnp.exp(head_rates[0])[None, :, None] * jax.nn.softplus(decay_raw)
    count = length // CHUNK
    upper = jnp.triu(jnp.ones((CHUNK, CHUNK), F32))
    cumulative = jnp.dot(
        log_decay.reshape(-1, CHUNK), upper, precision=HIGHEST
    ).reshape(chains, count, CHUNK)
    trailing = jnp.exp(cumulative[:, :, -1:] - cumulative).reshape(chains, length)
    cumulative = cumulative.reshape(chains, length)
    zero = jnp.zeros_like(update)
    columns = jnp.stack(
        [update, cumulative, jnp.exp(cumulative), trailing, zero, zero, zero, zero], axis=-1
    )
    g_rows = jnp.broadcast_to(cumulative[:, None, :], (chains, 8, length))
    call = functools.partial(chains_call, chains=chains, heads=heads, length=length)
    unit = 2 * CHUNK * DK * DK * count
    padded = pltpu.VMEM((length + 8, QKV), F32)
    reach, local, end, starts, inverse, solved_values, solved_keys, steps, seen = call(
        forward_kernel,
        operands=[
            ("rows", projected),
            ("edge", halo),
            ("taps", taps),
            ("chain", columns),
            ("chain", g_rows),
        ],
        outputs=[
            ("chain", (chains, length, DK), F32),
            ("chain", (chains, length, DV), F32),
            ("chain", (chains, DK, DV + DK), F32),
            ("chain", (chains, count, DK, DV + DK), F32),
            ("chain", (chains, length, CHUNK), F32),
            ("chain", (chains, length, DV), F32),
            ("chain", (chains, length, DK), F32),
            ("chain", (chains, length, DK), F32),
            ("chain", (chains, length, DK), F32),
        ],
        scratch=[padded],
        flops=90 * unit,
    )
    offset_map, linear_map = end[..., :DV], end[..., DV:]
    incoming = jnp.zeros((chains, DK, DV), F32)
    for hop in range(seq_size - 1):
        moved = offset_map
        if hop > 0:
            moved = moved + jnp.einsum("bkj,bjw->bkw", linear_map, incoming, precision=HIGHEST)
        incoming = shifted(moved, "seq", 1)
    gate_raw = dot(normed_in, full_gate, NN)
    scale_row = w_scale.reshape(1, DV)
    (mixed,) = call(
        finish_kernel,
        operands=[
            ("chain", local),
            ("chain", reach),
            ("chain", incoming),
            ("rows", gate_raw),
            ("all", scale_row),
        ],
        outputs=[("rows", (dp_size * length, heads * DV), BF16)],
        scratch=[],
        flops=6 * unit,
    )
    attention = scatter_absolute(contract_cols(mixed, full_output).astype(BF16))

    residual = stream_rows + attention
    factor_mid, normal_mid = norm_parts(residual)
    normed_mid = gather_relative((normal_mid * gains[1]).astype(BF16))
    gate_up = dot(normed_mid, full_swiglu, NN)
    gate_part, up_part = gate_up[:, :units], gate_up[:, units:]
    sigmoid_gate = jax.nn.sigmoid(gate_part)
    silu_gate = gate_part * sigmoid_gate
    activated = (silu_gate * up_part).astype(BF16)
    grad_activated = dot(grad_ffn, full_down, NN)
    grad_gate = grad_activated * up_part * sigmoid_gate * (1.0 + gate_part * (1.0 - sigmoid_gate))
    grad_up = grad_activated * silu_gate
    grad_gate_up = jnp.concatenate([grad_gate.astype(BF16), grad_up.astype(BF16)], axis=1)
    grad_normed_mid = scatter_relative(contract_cols(grad_gate_up, full_swiglu).astype(BF16))
    from_mid, grad_gain_mid = norm_back(factor_mid, normal_mid, gains[1], grad_normed_mid)
    grad_attention = gather_absolute((cotangent_rows + from_mid).astype(BF16)).reshape(-1, width)
    feedforward = scatter_relative(contract_cols(activated, full_down).astype(BF16))
    grad_ffn_weights = jnp.concatenate(
        [
            contract_rows(normed_mid, grad_gate_up).astype(BF16),
            contract_rows(grad_ffn, activated).astype(BF16),
        ],
        axis=1,
    )
    added = gather_absolute((attention + feedforward).astype(BF16), False).reshape(length, width)
    result = stream + turned_back(added).astype(F32)

    grad_mixed = dot(grad_attention, full_output, NN)
    grad_mixer_out, grad_gate_raw, grad_scale, correction = call(
        finish_back_kernel,
        operands=[
            ("chain", local),
            ("chain", reach),
            ("chain", incoming),
            ("rows", gate_raw),
            ("all", scale_row),
            ("rows", grad_mixed),
        ],
        outputs=[
            ("chain", (chains, length, DV), F32),
            ("rows", (dp_size * length, heads * DV), BF16),
            ("chain", (chains, 8, DV), F32),
            ("chain", (chains, DK, DV), F32),
        ],
        scratch=[],
        flops=12 * unit,
    )
    later = jnp.zeros((chains, DK, DV), F32)
    for hop in range(seq_size - 1):
        moved = correction
        if hop > 0:
            moved = moved + jnp.einsum("bjk,bjw->bkw", linear_map, later, precision=HIGHEST)
        later = shifted(moved, "seq", -1)
    grad_mixer_weights = jnp.concatenate(
        [
            contract_rows(normed_in, grad_gate_raw).astype(BF16),
            contract_rows(grad_attention, mixed).astype(BF16),
        ],
        axis=1,
    )
    grad_rows, tail, before, grad_taps, grad_columns = call(
        backward_kernel,
        operands=[
            ("rows", projected),
            ("edge", halo),
            ("taps", taps),
            ("chain", columns),
            ("chain", g_rows),
            ("chain", starts),
            ("chain", inverse),
            ("chain", solved_values),
            ("chain", solved_keys),
            ("chain", steps),
            ("chain", seen),
            ("chain", incoming),
            ("chain", later),
            ("chain", grad_mixer_out),
        ],
        outputs=[
            ("rows", (dp_size * length, heads * QKV), BF16),
            ("edge", (dp_size, 8, heads * QKV), F32),
            ("edge", (dp_size, 8, heads * QKV), F32),
            ("chain", (chains, KCONV, QKV), F32),
            ("chain", (chains, length, 8), F32),
        ],
        scratch=[padded, pltpu.VMEM((length + 16, QKV), F32)],
        flops=120 * unit,
    )
    patched = (tail + shifted(before, "seq", -1)).astype(BF16)
    grad_projected = grad_rows.reshape(dp_size, length, heads * QKV)
    grad_projected = lax.dynamic_update_slice_in_dim(grad_projected, patched, length - 8, 1)
    grad_projected = grad_projected.reshape(dp_size * length, heads * QKV)
    grad_update = grad_columns[..., 0]
    grad_log_decay = jnp.dot(
        grad_columns[..., 1].reshape(-1, CHUNK), upper.T, precision=HIGHEST
    ).reshape(dp_size, heads, length)
    grad_decay_raw = (
        -jnp.exp(head_rates[0])[None, :, None] * grad_log_decay * jax.nn.sigmoid(decay_raw)
    )
    grad_update_raw = (grad_update * update * (1.0 - update)).reshape(dp_size, heads, length)
    grad_rates = jnp.stack([grad_decay_raw, grad_update_raw], axis=-1)
    grad_rates = jnp.transpose(grad_rates, (0, 2, 1, 3)).reshape(-1, heads * 2).astype(BF16)
    grad_heads = jnp.stack(
        [
            jnp.sum(grad_log_decay * log_decay, axis=(0, 2)),
            jnp.sum(grad_decay_raw, axis=(0, 2)),
        ]
    )
    grad_qkv_weights = contract_rows(normed_in, grad_projected).astype(BF16)
    grad_rates_weights = contract_rows(normed_in, grad_rates)
    normed_in_term = (
        contract_cols(grad_projected, full_qkv)
        + contract_cols(grad_gate_raw, full_gate)
        + contract_cols(grad_rates, full_rates)
    )
    grad_normed_in = scatter_absolute(normed_in_term.astype(BF16))
    from_in, grad_gain_in = norm_back(factor_in, normal_in, gains[0], grad_normed_in)
    changed = gather_absolute((from_mid + from_in).astype(BF16), False).reshape(length, width)
    grad_stream = cotangent + turned_back(changed).astype(F32)

    scattered = []
    for full in (grad_ffn_weights, grad_mixer_weights, grad_qkv_weights):
        part = lax.psum_scatter(full, "seq", scatter_dimension=0, tiled=True)
        own, theirs = mine_and_theirs(part[:depth], part[depth:])
        received = swapped(theirs, "dp", 1)
        scattered.append(tuple(a.astype(F32) for a in by_device(own, received)))
    ffn_parts, mixer_parts, qkv_parts = scattered
    g_input = jnp.concatenate(
        [
            jnp.concatenate(
                [
                    q.reshape(depth, heads, QKV),
                    m[:, : heads * DV].reshape(depth, heads, DV),
                ],
                axis=2,
            )
            for q, m in zip(qkv_parts, mixer_parts)
        ],
        axis=1,
    )
    g_output = jnp.concatenate(
        [m[:, heads * DV :].T.reshape(heads, DV, depth) for m in mixer_parts], axis=0
    )
    g_swiglu = jnp.stack(
        [
            jnp.concatenate([f[:, :units] for f in ffn_parts], axis=1),
            jnp.concatenate([f[:, units : 2 * units] for f in ffn_parts], axis=1),
        ],
        axis=1,
    )
    g_down = jnp.concatenate([f[:, 2 * units :].T for f in ffn_parts], axis=0)

    conv_term = jnp.zeros_like(w_conv)
    grad_taps = jnp.sum(grad_taps.reshape(dp_size, heads, KCONV, QKV), axis=0)
    conv_term = lax.dynamic_update_slice_in_dim(
        conv_term, jnp.swapaxes(grad_taps, 0, 1), first_head, 1
    )
    heads_term = lax.dynamic_update_slice_in_dim(
        jnp.zeros_like(w_heads), grad_heads, first_head, 1
    )
    gains_term = turned_back(jnp.stack([grad_gain_in, grad_gain_mid]))
    scale_term = jnp.sum(grad_scale[:, 0], axis=0)
    rates_term = lax.dynamic_update_slice_in_dim(
        jnp.zeros((dp_size, width, heads * 2), F32),
        grad_rates_weights[None],
        lax.axis_index("dp"),
        0,
    )
    rates_term = jnp.transpose(rates_term, (1, 0, 2))
    small = [conv_term, heads_term, gains_term, scale_term]
    flat = butterfly_sum(jnp.concatenate([a.reshape(-1) for a in small]))
    sums, at = [], 0
    for a in small:
        sums.append(flat[at : at + a.size].reshape(a.shape))
        at += a.size
    g_conv, g_heads, g_gains, g_scale = sums
    rates_term = rates_term.reshape(seq_size, dp_size, depth, heads_stored * 2)
    rates_term = jnp.swapaxes(rates_term, 0, 1).reshape(dp_size * seq_size, -1)
    g_rates = jnp.sum(
        lax.all_to_all(rates_term, ("dp", "seq"), 0, 0, tiled=True), axis=0
    ).reshape(depth, heads_stored, 2)

    tokens = float(length * dp_size * seq_size)
    new_input, moment_input = adam_update(w_input, g_input, m_input, tokens)
    new_rates, moment_rates = adam_update(w_rates, g_rates, m_rates, tokens)
    new_conv, moment_conv = adam_update(w_conv, g_conv, m_conv, tokens)
    new_output, moment_output = adam_update(w_output, g_output, m_output, tokens)
    new_swiglu, moment_swiglu = adam_update(w_swiglu, g_swiglu, m_swiglu, tokens)
    new_down, moment_down = adam_update(w_down, g_down, m_down, tokens)
    new_gains, moment_gains = adam_update(w_gains, g_gains, m_gains, tokens)
    new_scale, moment_scale = adam_update(w_scale, g_scale, m_scale, tokens)
    new_heads, moment_heads = adam_update(w_heads, g_heads, m_heads, tokens)
    return (
        result,
        grad_stream,
        g_input,
        g_rates,
        g_conv,
        g_output,
        g_swiglu,
        g_down,
        g_gains,
        g_scale,
        g_heads,
        new_input,
        new_rates,
        new_conv,
        new_output,
        new_swiglu,
        new_down,
        new_gains,
        new_scale,
        new_heads,
        moment_input,
        moment_rates,
        moment_conv,
        moment_output,
        moment_swiglu,
        moment_down,
        moment_gains,
        moment_scale,
        moment_heads,
    )


def solution(mesh):
    in_specs = (
        P(("dp", "seq"), None),
        P(("dp", "seq"), None),
        P(("dp", "seq"), "tensor", None),
        P(("dp", "seq"), "tensor", None),
        P(),
        P("tensor", None, ("dp", "seq")),
        P(("dp", "seq"), None, "tensor"),
        P("tensor", ("dp", "seq")),
        P(),
        P(),
        P(),
        P(None, ("dp", "seq"), "tensor", None),
        P(None, ("dp", "seq"), "tensor", None),
        P(),
        P(None, "tensor", None, ("dp", "seq")),
        P(None, ("dp", "seq"), None, "tensor"),
        P(None, "tensor", ("dp", "seq")),
        P(),
        P(),
        P(),
    )
    out_specs = (
        P(("dp", "seq"), None),
        P(("dp", "seq"), None),
        P(("dp", "seq"), "tensor", None),
        P(("dp", "seq"), "tensor", None),
        P(),
        P("tensor", None, ("dp", "seq")),
        P(("dp", "seq"), None, "tensor"),
        P("tensor", ("dp", "seq")),
        P(),
        P(),
        P(),
        P(("dp", "seq"), "tensor", None),
        P(("dp", "seq"), "tensor", None),
        P(),
        P("tensor", None, ("dp", "seq")),
        P(("dp", "seq"), None, "tensor"),
        P("tensor", ("dp", "seq")),
        P(),
        P(),
        P(),
        P(None, ("dp", "seq"), "tensor", None),
        P(None, ("dp", "seq"), "tensor", None),
        P(),
        P(None, "tensor", None, ("dp", "seq")),
        P(None, ("dp", "seq"), None, "tensor"),
        P(None, "tensor", ("dp", "seq")),
        P(),
        P(),
        P(),
    )
    return jax.shard_map(body, mesh=mesh, in_specs=in_specs, out_specs=out_specs, check_vma=False)
```

```python
import functools

import jax
import jax.numpy as jnp
from jax import lax
from jax.experimental import pallas as pl
from jax.experimental.layout import Layout, with_layout_constraint
from jax.experimental.pallas import tpu as pltpu
from jax.sharding import PartitionSpec as P

DK = 128
DV = 256
QKV = 2 * DK + DV
KCONV = 4
CHUNK = 128
ADAM_STEP = 5
VMEM = 48 * 2**20

F32 = jnp.float32
BF16 = jnp.bfloat16
HIGHEST = lax.Precision.HIGHEST

NN = (((1,), (0,)), ((), ()))
NT = (((1,), (1,)), ((), ()))
TN = (((0,), (0,)), ((), ()))


def dot(left, right, dims):
    return lax.dot_general(left, right, dims, preferred_element_type=F32)


def halves(array):
    high = array.astype(BF16)
    return high, (array - high.astype(F32)).astype(BF16)


def mm(left, right, dims=NN):
    left_high, left_low = halves(left)
    right_high, right_low = halves(right)
    return (
        dot(left_high, right_high, dims)
        + dot(left_high, right_low, dims)
        + dot(left_low, right_high, dims)
    )


def each(function, *lists):
    return [function(*items) for items in zip(*lists)]


def unit_lower_inverses(strict_parts, row_index, column_index):
    size = strict_parts[0].shape[0]
    identity = (row_index == column_index).astype(F32)
    same = (row_index // 8) == (column_index // 8)
    small = [jnp.where(same, part, 0.0) for part in strict_parts]
    squared = each(mm, small, small)
    fourth = each(mm, squared, squared)
    first = each(lambda n, n2: mm(identity - n, identity + n2), small, squared)
    inverse = each(lambda a, n4: a + mm(a, n4), first, fourth)
    width = 8
    while width < size:
        pair = (row_index // (2 * width)) == (column_index // (2 * width))
        below = pair & ((row_index // width) != (column_index // width))
        lower = [jnp.where(below, part, 0.0) for part in strict_parts]
        inner = each(mm, lower, inverse)
        inverse = each(lambda x, y: x - mm(x, y), inverse, inner)
        width *= 2
    return inverse


def silu_parts(values):
    gate = 1.0 / (1.0 + jnp.exp(-values))
    return values * gate, gate


def filtered_parts(padded_ref, rows_ref, halo_ref, taps_ref):
    length = rows_ref.shape[0]
    padded_ref[0:8, :] = halo_ref[0]
    padded_ref[8 : 8 + length, :] = rows_ref[...]
    raw = taps_ref[0:1, :] * padded_ref[5 : 5 + length, :]
    for tap in range(1, KCONV):
        raw = raw + taps_ref[tap : tap + 1, :] * padded_ref[5 + tap : 5 + tap + length, :]
    filtered, gate = silu_parts(raw)
    return raw, gate, filtered


def unit_rows(rows):
    factor = lax.rsqrt(jnp.sum(rows * rows, axis=-1, keepdims=True) + 1e-06)
    return rows * factor, factor


def chunk_slices(array, count):
    return [array[i * CHUNK : (i + 1) * CHUNK] for i in range(count)]


def fades(columns, g_rows, row_index, column_index):
    within = row_index >= column_index
    result = []
    for i, column in enumerate(columns):
        gap = column[:, 1:2] - g_rows[0:1, i * CHUNK : (i + 1) * CHUNK]
        result.append(jnp.where(within, jnp.exp(jnp.where(within, gap, 0.0)), 0.0))
    return result


def forward_kernel(
    rows_ref,
    halo_ref,
    taps_ref,
    columns_ref,
    g_rows_ref,
    reach_ref,
    local_ref,
    end_ref,
    starts_ref,
    inverse_ref,
    solved_values_ref,
    solved_keys_ref,
    step_ref,
    seen_ref,
    padded_ref,
):
    length = rows_ref.shape[0]
    count = length // CHUNK
    raw, gate, filtered = filtered_parts(padded_ref, rows_ref, halo_ref, taps_ref)
    query = unit_rows(filtered[:, :DK])[0] * DK ** (-0.5)
    key = unit_rows(filtered[:, DK : 2 * DK])[0]
    value = filtered[:, 2 * DK :]
    row_index = lax.broadcasted_iota(jnp.int32, (CHUNK, CHUNK), 0)
    column_index = lax.broadcasted_iota(jnp.int32, (CHUNK, CHUNK), 1)
    identity = (row_index == column_index).astype(F32)
    strict = row_index > column_index
    queries, keys, values = (chunk_slices(a, count) for a in (query, key, value))
    columns = chunk_slices(columns_ref[0], count)
    fade = fades(columns, g_rows_ref[0], row_index, column_index)
    key_products = each(lambda k: mm(k, k, NT), keys)
    parts = each(
        lambda kk, f, c: jnp.where(strict, c[:, 0:1] * kk * f, 0.0), key_products, fade, columns
    )
    inverses = unit_lower_inverses(parts, row_index, column_index)
    scores = each(lambda q, k, f: mm(q, k, NT) * f, queries, keys, fade)
    solved_values = each(lambda t, v, c: mm(t, c[:, 0:1] * v), inverses, values, columns)
    solved_keys = each(lambda t, k, c: mm(t, c[:, 0:1] * c[:, 2:3] * k), inverses, keys, columns)
    seen = each(
        lambda q, s, w, c: c[:, 2:3] * q - mm(s, w), queries, scores, solved_keys, columns
    )
    inner = each(mm, scores, solved_values)
    faded = each(lambda k, c: (c[:, 3:4] * k).T, keys, columns)
    steps = each(
        lambda k, w, c: c[CHUNK - 1 : CHUNK, 2:3] * identity - mm(k, w),
        faded,
        solved_keys,
        columns,
    )
    added = each(mm, faded, solved_values)
    state = jnp.concatenate([jnp.zeros((DK, DV), F32), identity], axis=1)
    for i in range(count):
        here = slice(i * CHUNK, (i + 1) * CHUNK)
        starts_ref[0, i] = state
        reached = mm(seen[i], state)
        local_ref[0, here, :] = reached[:, :DV] + inner[i]
        reach_ref[0, here, :] = reached[:, DV:]
        state = mm(steps[i], state)
        state = jnp.concatenate([state[:, :DV] + added[i], state[:, DV:]], axis=1)
        inverse_ref[0, here, :] = inverses[i]
        solved_values_ref[0, here, :] = solved_values[i]
        solved_keys_ref[0, here, :] = solved_keys[i]
        step_ref[0, here, :] = steps[i]
        seen_ref[0, here, :] = seen[i]
    end_ref[0] = state


def finish_kernel(local_ref, reach_ref, state_ref, gate_ref, scale_ref, mixed_ref):
    mixer_out = local_ref[0] + mm(reach_ref[0], state_ref[0])
    factor = lax.rsqrt(jnp.mean(mixer_out * mixer_out, axis=-1, keepdims=True) + 1e-05)
    opened = silu_parts(gate_ref[...])[0]
    mixed_ref[...] = (mixer_out * factor * scale_ref[...] * opened).astype(BF16)


def finish_back_kernel(
    local_ref,
    reach_ref,
    state_ref,
    gate_ref,
    scale_ref,
    grad_ref,
    grad_out_ref,
    grad_gate_ref,
    grad_scale_ref,
    correction_ref,
):
    mixer_out = local_ref[0] + mm(reach_ref[0], state_ref[0])
    factor = lax.rsqrt(jnp.mean(mixer_out * mixer_out, axis=-1, keepdims=True) + 1e-05)
    normal = mixer_out * factor
    gate_raw = gate_ref[...]
    opened, gate = silu_parts(gate_raw)
    grad = grad_ref[...]
    scale = scale_ref[...]
    with_normal = grad * normal
    grad_gate_ref[...] = (
        with_normal * scale * gate * (1.0 + gate_raw * (1.0 - gate))
    ).astype(BF16)
    summed = jnp.sum(with_normal * opened, axis=0, keepdims=True)
    grad_scale_ref[0] = jnp.broadcast_to(summed, (8, DV))
    grad_normal = grad * scale * opened
    shared = jnp.mean(grad_normal * normal, axis=-1, keepdims=True)
    grad_out = factor * (grad_normal - normal * shared)
    grad_out_ref[0] = grad_out
    correction_ref[0] = mm(reach_ref[0].T, grad_out)


def backward_kernel(
    rows_ref,
    halo_ref,
    taps_ref,
    columns_ref,
    g_rows_ref,
    starts_ref,
    inverse_ref,
    solved_values_ref,
    solved_keys_ref,
    step_ref,
    seen_ref,
    state_ref,
    later_ref,
    grad_out_ref,
    grad_rows_ref,
    tail_ref,
    before_ref,
    grad_taps_ref,
    grad_columns_ref,
    padded_ref,
    grad_padded_ref,
):
    length = rows_ref.shape[0]
    count = length // CHUNK
    raw, gate, filtered = filtered_parts(padded_ref, rows_ref, halo_ref, taps_ref)
    query_unit, query_factor = unit_rows(filtered[:, :DK])
    key, key_factor = unit_rows(filtered[:, DK : 2 * DK])
    query = query_unit * DK ** (-0.5)
    value = filtered[:, 2 * DK :]
    row_index = lax.broadcasted_iota(jnp.int32, (CHUNK, CHUNK), 0)
    column_index = lax.broadcasted_iota(jnp.int32, (CHUNK, CHUNK), 1)
    strict = row_index > column_index
    last = lax.broadcasted_iota(jnp.int32, (CHUNK, 1), 0) == CHUNK - 1
    queries, keys, values = (chunk_slices(a, count) for a in (query, key, value))
    columns = chunk_slices(columns_ref[0], count)
    inverses = chunk_slices(inverse_ref[0], count)
    solved_values = chunk_slices(solved_values_ref[0], count)
    solved_keys = chunk_slices(solved_keys_ref[0], count)
    steps = chunk_slices(step_ref[0], count)
    seen = chunk_slices(seen_ref[0], count)
    grad_outs = chunk_slices(grad_out_ref[0], count)
    fade = fades(columns, g_rows_ref[0], row_index, column_index)
    incoming = state_ref[0]
    states = [starts_ref[0, i][:, :DV] + mm(starts_ref[0, i][:, DV:], incoming) for i in range(count)]
    own_grads = each(lambda s, o: mm(s.T, o), seen, grad_outs)
    later = [None] * count
    carried = later_ref[0]
    for i in reversed(range(count)):
        later[i] = carried
        if i > 0:
            carried = mm(steps[i].T, carried) + own_grads[i]
    key_products = each(lambda k: mm(k, k, NT), keys)
    query_products = each(lambda q, k: mm(q, k, NT), queries, keys)
    scores = each(lambda p, f: p * f, query_products, fade)
    fresh = each(lambda u, w, s: u - mm(w, s), solved_values, solved_keys, states)
    faded = each(lambda k, c: c[:, 3:4] * k, keys, columns)
    grad_fresh = each(
        lambda p, o, k, l: mm(p.T, o) + mm(k, l), scores, grad_outs, faded, later
    )
    grad_scaled = each(lambda t, g: mm(t.T, g), inverses, grad_fresh)
    grad_scaled_keys = each(lambda g, s: -mm(g, s, NT), grad_scaled, states)
    grad_lower = each(
        lambda g, f: jnp.where(strict, -mm(g, f, NT), 0.0), grad_scaled, fresh
    )
    grad_scores = each(lambda o, f, d: mm(o, f, NT) * d, grad_outs, fresh, fade)
    lower_fade = each(lambda g, d: g * d, grad_lower, fade)
    pairs = each(lambda h, c: c[:, 0:1] * h, lower_fade, columns)
    from_state = each(lambda o, s: mm(o, s, NT), grad_outs, states)
    from_later = each(lambda f, l: mm(f, l, NT), fresh, later)
    grad_queries = each(
        lambda c, a, g, k: c[:, 2:3] * a + mm(g, k), columns, from_state, grad_scores, keys
    )
    grad_keys = each(
        lambda c, b, p, k, g, q, e: c[:, 0:1] * c[:, 2:3] * b
        + mm(p + p.T, k)
        + mm(g.T, q)
        + c[:, 3:4] * e,
        columns,
        grad_scaled_keys,
        pairs,
        keys,
        grad_scores,
        queries,
        from_later,
    )
    grad_values = each(lambda c, g: c[:, 0:1] * g, columns, grad_scaled)

    def across(array):
        return jnp.sum(array, axis=-1, keepdims=True)

    for i in range(count):
        column = columns[i]
        key_term = column[:, 2:3] * across(grad_scaled_keys[i] * keys[i])
        grad_update = (
            across(grad_scaled[i] * values[i])
            + key_term
            + across(lower_fade[i] * key_products[i])
        )
        both = grad_scores[i] * query_products[i] + pairs[i] * key_products[i]
        trailing = column[:, 3:4] * across(keys[i] * from_later[i])
        whole = column[CHUNK - 1 : CHUNK, 2:3] * jnp.sum(
            across(later[i] * states[i]), axis=0, keepdims=True
        ) + jnp.sum(trailing, axis=0, keepdims=True)
        grad_g = (
            across(both - both.T)
            + column[:, 2:3] * across(queries[i] * from_state[i])
            + column[:, 0:1] * key_term
            - trailing
            + jnp.where(last, whole, 0.0)
        )
        lane = lax.broadcasted_iota(jnp.int32, (CHUNK, 8), 1)
        grad_columns_ref[0, i * CHUNK : (i + 1) * CHUNK, :] = jnp.where(
            lane == 0, grad_update, grad_g
        )
    grad_query = jnp.concatenate(grad_queries, axis=0) * DK ** (-0.5)
    grad_key = jnp.concatenate(grad_keys, axis=0)
    grad_value = jnp.concatenate(grad_values, axis=0)
    grad_query = query_factor * (grad_query - query_unit * across(query_unit * grad_query))
    grad_key = key_factor * (grad_key - key * across(key * grad_key))
    grad_filtered = jnp.concatenate([grad_query, grad_key, grad_value], axis=1)
    grad_raw = grad_filtered * gate * (1.0 + raw * (1.0 - gate))
    zeros = jnp.zeros((8, QKV), F32)
    grad_padded_ref[0:8, :] = zeros
    grad_padded_ref[8 : 8 + length, :] = grad_raw
    grad_padded_ref[8 + length : 16 + length, :] = zeros
    grad_rows = taps_ref[0:1, :] * grad_padded_ref[11 : 11 + length, :]
    before = taps_ref[0:1, :] * grad_padded_ref[3:11, :]
    for tap in range(1, KCONV):
        tap_row = taps_ref[tap : tap + 1, :]
        grad_rows = grad_rows + tap_row * grad_padded_ref[11 - tap : 11 - tap + length, :]
        before = before + tap_row * grad_padded_ref[3 - tap : 11 - tap, :]
    grad_rows_ref[...] = grad_rows.astype(BF16)
    tail_ref[0] = grad_rows[length - 8 :]
    before_ref[0] = before
    sums = [
        jnp.sum(grad_raw * padded_ref[5 + tap : 5 + tap + length, :], axis=0, keepdims=True)
        for tap in range(KCONV)
    ]
    grad_taps_ref[0] = jnp.concatenate(sums, axis=0)


def chains_call(kernel, chains, heads, length, operands, outputs, scratch, flops):
    def spec(tag, shape):
        if tag == "rows":
            return pl.BlockSpec((length, shape[1] // heads), lambda i: (i // heads, i % heads))
        if tag == "edge":
            return pl.BlockSpec((1, 8, shape[2] // heads), lambda i: (i // heads, 0, i % heads))
        if tag == "taps":
            return pl.BlockSpec((shape[0], shape[1] // heads), lambda i: (0, i % heads))
        if tag == "all":
            return pl.BlockSpec(shape, lambda i: (0,) * len(shape))
        return pl.BlockSpec((1,) + tuple(shape[1:]), lambda i: (i,) + (0,) * (len(shape) - 1))

    moved = sum(a.size * a.dtype.itemsize for _, a in operands)
    return pl.pallas_call(
        kernel,
        grid=(chains,),
        in_specs=[spec(tag, a.shape) for tag, a in operands],
        out_specs=[spec(tag, shape) for tag, shape, _ in outputs],
        out_shape=[jax.ShapeDtypeStruct(shape, dtype) for _, shape, dtype in outputs],
        scratch_shapes=scratch,
        compiler_params=pltpu.CompilerParams(vmem_limit_bytes=VMEM),
        cost_estimate=pl.CostEstimate(
            flops=chains * flops, bytes_accessed=2 * moved, transcendentals=0
        ),
    )(*[a for _, a in operands])


def shifted(block, axis, distance):
    devices = range(lax.axis_size(axis))
    route = [(i, i + distance) for i in devices if i + distance in devices]
    return lax.ppermute(block, axis, route)


def swapped(block, axis, bits):
    return lax.ppermute(block, axis, [(i, i ^ bits) for i in range(lax.axis_size(axis))])


def group_swapped(block, dp_bits, tensor_bits):
    dp_size, tensor_size = lax.axis_size("dp"), lax.axis_size("tensor")
    route = [
        (d * tensor_size + t, (d ^ dp_bits) * tensor_size + (t ^ tensor_bits))
        for d in range(dp_size)
        for t in range(tensor_size)
    ]
    return lax.ppermute(block, ("dp", "tensor"), route)


def partner_bits():
    chips = lax.axis_size("tensor") // 2
    return [(d, t) for d in range(lax.axis_size("dp")) for t in range(chips) if (d, t) != (0, 0)]


def bits_slot(dp_bits, chip_bits):
    return dp_bits * (lax.axis_size("tensor") // 2) + chip_bits


def scatter_relative(partial):
    half = partial.shape[0] // 2
    summed = partial[:half].astype(F32) + swapped(partial[half:], "tensor", 1).astype(F32)
    rows = half // (lax.axis_size("dp") * lax.axis_size("tensor") // 2)
    total = summed[:rows]
    low = summed.astype(BF16)
    for d, t in partner_bits():
        slot = bits_slot(d, t)
        received = group_swapped(low[slot * rows : (slot + 1) * rows], d, 2 * t)
        total = total + received.astype(F32)
    return total


def gather_relative(own):
    parts = [own] + [group_swapped(own, d, 2 * t) for d, t in partner_bits()]
    here = jnp.concatenate(parts, axis=0)
    return jnp.concatenate([here, swapped(here, "tensor", 1)], axis=0)


def scatter_absolute(partial):
    dp_size, chips = lax.axis_size("dp"), lax.axis_size("tensor") // 2
    core = lax.axis_index("tensor") % 2
    chip = lax.axis_index("tensor") // 2
    device = lax.axis_index("dp")
    rows = partial.shape[0] // (2 * dp_size * chips)
    blocks = partial.reshape(dp_size * chips, 2, rows, -1)
    even, odd = blocks[:, 0], blocks[:, 1]
    mine = jnp.where(core == 0, even, odd)
    theirs = jnp.where(core == 0, odd, even)
    summed = mine.astype(F32) + swapped(theirs, "tensor", 1).astype(F32)
    low = summed.astype(BF16)
    total = lax.dynamic_index_in_dim(summed, device * chips + chip, 0, keepdims=False)
    for d, t in partner_bits():
        target = (device ^ d) * chips + (chip ^ t)
        block = lax.dynamic_index_in_dim(low, target, 0, keepdims=False)
        total = total + group_swapped(block, d, 2 * t).astype(F32)
    return total


def ordered(parts, core, other):
    first = jnp.where(core == 0, parts, other)
    second = jnp.where(core == 0, other, parts)
    stacked = jnp.stack([first, second], axis=1)
    return stacked.reshape((-1,) + parts.shape[2:])


def gather_absolute(own, over_dp=True):
    dp_size = lax.axis_size("dp") if over_dp else 1
    chips = lax.axis_size("tensor") // 2
    core = lax.axis_index("tensor") % 2
    chip = lax.axis_index("tensor") // 2
    device = lax.axis_index("dp") if over_dp else 0
    here = jnp.zeros((dp_size * chips,) + own.shape, own.dtype)
    here = lax.dynamic_update_index_in_dim(here, own, device * chips + chip, 0)
    for d, t in partner_bits():
        if d < dp_size:
            received = group_swapped(own, d, 2 * t)
            source = (device ^ d) * chips + (chip ^ t)
            here = lax.dynamic_update_index_in_dim(here, received, source, 0)
    return ordered(here, core, swapped(here, "tensor", 1))


def after(value, tokens):
    return lax.optimization_barrier((value, tokens))[0]


def butterfly_sum(array):
    for axis in ("tensor", "dp", "seq"):
        distance = 1
        while distance < lax.axis_size(axis):
            array = array + swapped(array, axis, distance)
            distance *= 2
    return array


def contract_cols(left, right):
    return dot(left, right, NT)


def contract_rows(left, right):
    return dot(left, right, TN)


def adam_update(weight, gradient, moments, token_count):
    mean_grad = gradient / token_count
    is_first = lax.broadcasted_iota(jnp.int32, moments.shape, 0) == 0
    moved = 0.5 * moments + 0.5 * jnp.where(is_first, mean_grad, mean_grad * mean_grad)
    first = 0.5 * moments[0] + 0.5 * mean_grad
    second = 0.5 * moments[1] + 0.5 * mean_grad * mean_grad
    correction = 1.0 - 0.5**ADAM_STEP
    change = first / correction / (jnp.sqrt(second / correction) + 1e-08) + 0.1 * weight
    return (weight - 0.1 * change, moved)


def norm_parts(rows):
    factor = lax.rsqrt(jnp.mean(rows * rows, axis=-1, keepdims=True) + 1e-06)
    return factor, rows * factor


def norm_back(factor, normal, gain, grad):
    scaled = grad * gain
    shared = jnp.mean(scaled * normal, axis=-1, keepdims=True)
    return factor * (scaled - normal * shared), jnp.sum(grad * normal, axis=0)


def body(
    stream,
    cotangent,
    w_input,
    w_rates,
    w_conv,
    w_output,
    w_swiglu,
    w_down,
    w_gains,
    w_scale,
    w_heads,
    m_input,
    m_rates,
    m_conv,
    m_output,
    m_swiglu,
    m_down,
    m_gains,
    m_scale,
    m_heads,
):
    dp_size, seq_size, tensor_size = (lax.axis_size(a) for a in ("dp", "seq", "tensor"))
    length, width = stream.shape
    depth = w_input.shape[0]
    heads_stored = w_input.shape[1]
    heads = heads_stored // dp_size
    units_stored = w_swiglu.shape[2]
    units = units_stored // dp_size
    rows = length // tensor_size
    chains = dp_size * heads
    first_part = lax.axis_index("dp") == 0
    first_head = lax.axis_index("tensor") * heads_stored + lax.axis_index("dp") * heads

    def blocks_of(array, order):
        return jnp.concatenate([array[..., i * depth : (i + 1) * depth] for i in order], axis=-1)

    def turned(array):
        return blocks_of(array, [d * seq_size + q for q in range(seq_size) for d in range(dp_size)])

    def turned_back(array):
        return blocks_of(array, [q * dp_size + d for d in range(dp_size) for q in range(seq_size)])

    def mine_and_theirs(low, high):
        return jnp.where(first_part, low, high), jnp.where(first_part, high, low)

    def by_device(own, received):
        return jnp.where(first_part, own, received), jnp.where(first_part, received, own)

    low_input = w_input.astype(BF16)
    low_output = jnp.transpose(w_output.astype(BF16), (2, 0, 1))
    low_swiglu = w_swiglu.astype(BF16)
    low_down = w_down.astype(BF16).T

    def half_columns(index):
        chosen = slice(index * heads, (index + 1) * heads)
        some = slice(index * units, (index + 1) * units)
        return (
            low_input[:, chosen, :QKV].reshape(depth, -1),
            jnp.concatenate(
                [
                    low_input[:, chosen, QKV:].reshape(depth, -1),
                    low_output[:, chosen].reshape(depth, -1),
                ],
                axis=1,
            ),
            jnp.concatenate([low_swiglu[:, 0, some], low_swiglu[:, 1, some]], axis=1),
            low_down[:, some],
        )

    gathered = []
    for low, high in zip(half_columns(0), half_columns(1)):
        mine, theirs = mine_and_theirs(low, high)
        received = swapped(theirs, "dp", 1)
        shard = jnp.concatenate(by_device(mine, received), axis=0)
        gathered.append(lax.all_gather(shard, "seq", axis=0, tiled=True))
    full_qkv, full_mixer, full_swiglu, full_down = gathered
    full_gate, full_output = full_mixer[:, : heads * DV], full_mixer[:, heads * DV :]

    copies = dp_size * seq_size
    rates_low = jnp.broadcast_to(w_rates.astype(BF16).reshape(1, -1), (copies, depth * heads_stored * 2))
    rates_all = lax.all_to_all(rates_low, ("dp", "seq"), 0, 0, tiled=True)
    rates_all = rates_all.reshape(dp_size, seq_size, depth, dp_size, heads * 2)
    rates_all = jnp.swapaxes(rates_all, 0, 1).reshape(width, dp_size, heads * 2)
    full_rates = jnp.where(first_part, rates_all[:, 0], rates_all[:, dp_size - 1])

    quarter = lax.axis_index("tensor") * rows
    stream_rows = turned(lax.dynamic_slice_in_dim(stream, quarter, rows, 0))
    cotangent_rows = turned(lax.dynamic_slice_in_dim(cotangent, quarter, rows, 0))
    gains = turned(w_gains)
    factor_in, normal_in = norm_parts(stream_rows)
    normed_in = gather_absolute((normal_in * gains[0]).astype(BF16)).reshape(-1, width)

    projected = dot(normed_in, full_qkv, NN)
    rates = dot(normed_in, full_rates, NN)
    last_rows = projected.reshape(dp_size, length, heads * QKV)[:, length - 8 :]
    halo = shifted(last_rows, "seq", 1)
    taps = lax.dynamic_slice_in_dim(w_conv, first_head, heads, 1).reshape(KCONV, heads * QKV)
    head_rates = lax.dynamic_slice_in_dim(w_heads, first_head, heads, 1)
    by_chain = jnp.transpose(rates.reshape(dp_size, length, heads, 2), (3, 0, 2, 1))
    decay_raw = by_chain[0] + head_rates[1][None, :, None]
    update = jax.nn.sigmoid(by_chain[1]).reshape(chains, length)
    log_decay = -jnp.exp(head_rates[0])[None, :, None] * jax.nn.softplus(decay_raw)
    count = length // CHUNK
    upper = jnp.triu(jnp.ones((CHUNK, CHUNK), F32))
    cumulative = jnp.dot(
        log_decay.reshape(-1, CHUNK), upper, precision=HIGHEST
    ).reshape(chains, count, CHUNK)
    trailing = jnp.exp(cumulative[:, :, -1:] - cumulative).reshape(chains, length)
    cumulative = cumulative.reshape(chains, length)
    zero = jnp.zeros_like(update)
    columns = jnp.stack(
        [update, cumulative, jnp.exp(cumulative), trailing, zero, zero, zero, zero], axis=-1
    )
    g_rows = jnp.broadcast_to(cumulative[:, None, :], (chains, 8, length))
    call = functools.partial(chains_call, chains=chains, heads=heads, length=length)
    unit = 2 * CHUNK * DK * DK * count
    padded = pltpu.VMEM((length + 8, QKV), F32)
    reach, local, end, starts, inverse, solved_values, solved_keys, steps, seen = call(
        forward_kernel,
        operands=[
            ("rows", projected),
            ("edge", halo),
            ("taps", taps),
            ("chain", columns),
            ("chain", g_rows),
        ],
        outputs=[
            ("chain", (chains, length, DK), F32),
            ("chain", (chains, length, DV), F32),
            ("chain", (chains, DK, DV + DK), F32),
            ("chain", (chains, count, DK, DV + DK), F32),
            ("chain", (chains, length, CHUNK), F32),
            ("chain", (chains, length, DV), F32),
            ("chain", (chains, length, DK), F32),
            ("chain", (chains, length, DK), F32),
            ("chain", (chains, length, DK), F32),
        ],
        scratch=[padded],
        flops=90 * unit,
    )
    offset_map, linear_map = end[..., :DV], end[..., DV:]
    incoming = jnp.zeros((chains, DK, DV), F32)
    for hop in range(seq_size - 1):
        moved = offset_map
        if hop > 0:
            moved = moved + jnp.einsum("bkj,bjw->bkw", linear_map, incoming, precision=HIGHEST)
        incoming = shifted(moved.astype(BF16), "seq", 1).astype(F32)
    grad_ffn = gather_relative(after(cotangent_rows.astype(BF16), end))
    gate_raw = dot(after(normed_in, grad_ffn), full_gate, NN)
    scale_row = w_scale.reshape(1, DV)
    (mixed,) = call(
        finish_kernel,
        operands=[
            ("chain", local),
            ("chain", reach),
            ("chain", incoming),
            ("rows", gate_raw),
            ("all", scale_row),
        ],
        outputs=[("rows", (dp_size * length, heads * DV), BF16)],
        scratch=[],
        flops=6 * unit,
    )
    attention = scatter_absolute(contract_cols(mixed, full_output).astype(BF16))

    residual = stream_rows + attention
    factor_mid, normal_mid = norm_parts(residual)
    normed_mid = gather_relative((normal_mid * gains[1]).astype(BF16))
    gate_up = dot(normed_mid, full_swiglu, NN)
    gate_part, up_part = gate_up[:, :units], gate_up[:, units:]
    sigmoid_gate = jax.nn.sigmoid(gate_part)
    silu_gate = gate_part * sigmoid_gate
    activated = after((silu_gate * up_part).astype(BF16), full_down)
    grad_down_weights = contract_rows(grad_ffn, activated).astype(BF16)
    down_sum = lax.psum_scatter(grad_down_weights, "seq", scatter_dimension=0, tiled=True)
    grad_activated = dot(after(grad_ffn, grad_down_weights), full_down, NN)
    grad_gate = grad_activated * up_part * sigmoid_gate * (1.0 + gate_part * (1.0 - sigmoid_gate))
    grad_up = grad_activated * silu_gate
    grad_gate_up = jnp.concatenate([grad_gate.astype(BF16), grad_up.astype(BF16)], axis=1)
    normed_mid_term = contract_cols(grad_gate_up, full_swiglu).astype(BF16)
    grad_normed_mid = scatter_relative(normed_mid_term)
    grad_swiglu_weights = contract_rows(after(normed_mid, normed_mid_term), grad_gate_up)
    grad_swiglu_weights = after(grad_swiglu_weights.astype(BF16), grad_down_weights)
    swiglu_sum = lax.psum_scatter(grad_swiglu_weights, "seq", scatter_dimension=0, tiled=True)
    from_mid, grad_gain_mid = norm_back(factor_mid, normal_mid, gains[1], grad_normed_mid)
    from_mid = after(from_mid, grad_swiglu_weights)
    grad_attention = gather_absolute((cotangent_rows + from_mid).astype(BF16)).reshape(-1, width)
    grad_mixed = dot(grad_attention, full_output, NN)
    grad_mixer_out, grad_gate_raw, grad_scale, correction = call(
        finish_back_kernel,
        operands=[
            ("chain", local),
            ("chain", reach),
            ("chain", incoming),
            ("rows", gate_raw),
            ("all", scale_row),
            ("rows", grad_mixed),
        ],
        outputs=[
            ("chain", (chains, length, DV), F32),
            ("rows", (dp_size * length, heads * DV), BF16),
            ("chain", (chains, 8, DV), F32),
            ("chain", (chains, DK, DV), F32),
        ],
        scratch=[],
        flops=12 * unit,
    )
    later = jnp.zeros((chains, DK, DV), F32)
    for hop in range(seq_size - 1):
        moved = correction
        if hop > 0:
            moved = moved + jnp.einsum("bjk,bjw->bkw", linear_map, later, precision=HIGHEST)
        later = shifted(moved.astype(BF16), "seq", -1)
        if hop == 0:
            feedforward = scatter_relative(
                contract_cols(after(activated, later), full_down).astype(BF16)
            )
        later = later.astype(F32)
    later = after(later, (swiglu_sum, feedforward))
    grad_mixer_weights = jnp.concatenate(
        [
            contract_rows(normed_in, grad_gate_raw).astype(BF16),
            contract_rows(grad_attention, mixed).astype(BF16),
        ],
        axis=1,
    )
    grad_rows, tail, before, grad_taps, grad_columns = call(
        backward_kernel,
        operands=[
            ("rows", projected),
            ("edge", halo),
            ("taps", taps),
            ("chain", columns),
            ("chain", g_rows),
            ("chain", starts),
            ("chain", inverse),
            ("chain", solved_values),
            ("chain", solved_keys),
            ("chain", steps),
            ("chain", seen),
            ("chain", incoming),
            ("chain", later),
            ("chain", grad_mixer_out),
        ],
        outputs=[
            ("rows", (dp_size * length, heads * QKV), BF16),
            ("edge", (dp_size, 8, heads * QKV), F32),
            ("edge", (dp_size, 8, heads * QKV), F32),
            ("chain", (chains, KCONV, QKV), F32),
            ("chain", (chains, length, 8), F32),
        ],
        scratch=[padded, pltpu.VMEM((length + 16, QKV), F32)],
        flops=120 * unit,
    )
    patched = (tail + shifted(before, "seq", -1)).astype(BF16)
    grad_projected = grad_rows.reshape(dp_size, length, heads * QKV)
    grad_projected = lax.dynamic_update_slice_in_dim(grad_projected, patched, length - 8, 1)
    grad_projected = grad_projected.reshape(dp_size * length, heads * QKV)
    grad_update = grad_columns[..., 0]
    grad_log_decay = jnp.dot(
        grad_columns[..., 1].reshape(-1, CHUNK), upper.T, precision=HIGHEST
    ).reshape(dp_size, heads, length)
    grad_decay_raw = (
        -jnp.exp(head_rates[0])[None, :, None] * grad_log_decay * jax.nn.sigmoid(decay_raw)
    )
    grad_update_raw = (grad_update * update * (1.0 - update)).reshape(dp_size, heads, length)
    grad_rates = jnp.stack([grad_decay_raw, grad_update_raw], axis=-1)
    grad_rates = jnp.transpose(grad_rates, (0, 2, 1, 3)).reshape(-1, heads * 2).astype(BF16)
    grad_heads = jnp.stack(
        [
            jnp.sum(grad_log_decay * log_decay, axis=(0, 2)),
            jnp.sum(grad_decay_raw, axis=(0, 2)),
        ]
    )
    grad_qkv_weights = contract_rows(normed_in, grad_projected).astype(BF16)
    mixer_sum = lax.psum_scatter(
        after(grad_mixer_weights, (swiglu_sum, down_sum)),
        "seq",
        scatter_dimension=0,
        tiled=True,
    )
    qkv_sum = lax.psum_scatter(
        after(grad_qkv_weights, swiglu_sum), "seq", scatter_dimension=0, tiled=True
    )
    grad_rates_weights = contract_rows(after(normed_in, grad_qkv_weights), grad_rates)
    normed_in_term = (
        contract_cols(after(grad_projected, (grad_qkv_weights, grad_rates_weights)), full_qkv)
        + contract_cols(grad_gate_raw, full_gate)
        + contract_cols(grad_rates, full_rates)
    )
    grad_normed_in = scatter_absolute(normed_in_term.astype(BF16))
    from_in, grad_gain_in = norm_back(factor_in, normal_in, gains[0], grad_normed_in)
    added = turned_back(jnp.concatenate([attention + feedforward, from_mid + from_in], axis=0))
    added = gather_absolute(
        jnp.concatenate([added[:rows], added[rows:]], axis=1).astype(BF16), False
    ).reshape(length, 2 * width)
    result = stream + added[:, :width].astype(F32)
    grad_stream = cotangent + added[:, width:].astype(F32)

    def exchanged(part):
        own, theirs = mine_and_theirs(part[:depth], part[depth:])
        received = swapped(theirs, "dp", 1)
        return tuple(a.astype(F32) for a in by_device(own, received))

    swiglu_parts, down_parts, mixer_parts = (
        exchanged(part) for part in (swiglu_sum, down_sum, mixer_sum)
    )
    g_output = jnp.concatenate(
        [m[:, heads * DV :].T.reshape(heads, DV, depth) for m in mixer_parts], axis=0
    )
    g_swiglu = jnp.stack(
        [
            jnp.concatenate([f[:, :units] for f in swiglu_parts], axis=1),
            jnp.concatenate([f[:, units:] for f in swiglu_parts], axis=1),
        ],
        axis=1,
    )
    g_swiglu = with_layout_constraint(g_swiglu, Layout((0, 1, 2)))
    g_down = jnp.concatenate([f.T for f in down_parts], axis=0)

    conv_term = jnp.zeros_like(w_conv)
    grad_taps = jnp.sum(grad_taps.reshape(dp_size, heads, KCONV, QKV), axis=0)
    conv_term = lax.dynamic_update_slice_in_dim(
        conv_term, jnp.swapaxes(grad_taps, 0, 1), first_head, 1
    )
    heads_term = lax.dynamic_update_slice_in_dim(
        jnp.zeros_like(w_heads), grad_heads, first_head, 1
    )
    gains_term = turned_back(jnp.stack([grad_gain_in, grad_gain_mid]))
    scale_term = jnp.sum(grad_scale[:, 0], axis=0)
    rates_term = lax.dynamic_update_slice_in_dim(
        jnp.zeros((dp_size, width, heads * 2), F32),
        grad_rates_weights[None],
        lax.axis_index("dp"),
        0,
    )
    rates_term = jnp.transpose(rates_term, (1, 0, 2))
    small = [conv_term, heads_term, gains_term, scale_term]
    flat = jnp.concatenate([a.reshape(-1) for a in small])
    flat = butterfly_sum(flat)
    sums, at = [], 0
    for a in small:
        sums.append(flat[at : at + a.size].reshape(a.shape))
        at += a.size
    g_conv, g_heads, g_gains, g_scale = sums
    rates_term = rates_term.reshape(seq_size, dp_size, depth, heads_stored * 2)
    rates_term = jnp.swapaxes(rates_term, 0, 1).reshape(dp_size * seq_size, -1)
    g_rates = jnp.sum(
        lax.all_to_all(rates_term, ("dp", "seq"), 0, 0, tiled=True), axis=0
    ).reshape(depth, heads_stored, 2)

    tokens = float(length * dp_size * seq_size)
    new_rates, moment_rates = adam_update(w_rates, g_rates, m_rates, tokens)
    new_conv, moment_conv = adam_update(w_conv, g_conv, m_conv, tokens)
    new_output, moment_output = adam_update(w_output, g_output, m_output, tokens)
    new_swiglu, moment_swiglu = adam_update(w_swiglu, g_swiglu, m_swiglu, tokens)
    new_down, moment_down = adam_update(w_down, g_down, m_down, tokens)
    new_gains, moment_gains = adam_update(w_gains, g_gains, m_gains, tokens)
    new_scale, moment_scale = adam_update(w_scale, g_scale, m_scale, tokens)
    new_heads, moment_heads = adam_update(w_heads, g_heads, m_heads, tokens)
    others = (result, grad_stream, g_conv, new_output, new_swiglu, new_down, new_rates)
    qkv_parts = exchanged(after(qkv_sum, others))
    g_input = jnp.concatenate(
        [
            jnp.concatenate(
                [
                    q.reshape(depth, heads, QKV),
                    m[:, : heads * DV].reshape(depth, heads, DV),
                ],
                axis=2,
            )
            for q, m in zip(qkv_parts, mixer_parts)
        ],
        axis=1,
    )
    new_input, moment_input = adam_update(w_input, g_input, m_input, tokens)
    return (
        result,
        grad_stream,
        g_input,
        g_rates,
        g_conv,
        g_output,
        g_swiglu,
        g_down,
        g_gains,
        g_scale,
        g_heads,
        new_input,
        new_rates,
        new_conv,
        new_output,
        new_swiglu,
        new_down,
        new_gains,
        new_scale,
        new_heads,
        moment_input,
        moment_rates,
        moment_conv,
        moment_output,
        moment_swiglu,
        moment_down,
        moment_gains,
        moment_scale,
        moment_heads,
    )


def solution(mesh):
    in_specs = (
        P(("dp", "seq"), None),
        P(("dp", "seq"), None),
        P(("dp", "seq"), "tensor", None),
        P(("dp", "seq"), "tensor", None),
        P(),
        P("tensor", None, ("dp", "seq")),
        P(("dp", "seq"), None, "tensor"),
        P("tensor", ("dp", "seq")),
        P(),
        P(),
        P(),
        P(None, ("dp", "seq"), "tensor", None),
        P(None, ("dp", "seq"), "tensor", None),
        P(),
        P(None, "tensor", None, ("dp", "seq")),
        P(None, ("dp", "seq"), None, "tensor"),
        P(None, "tensor", ("dp", "seq")),
        P(),
        P(),
        P(),
    )
    out_specs = (
        P(("dp", "seq"), None),
        P(("dp", "seq"), None),
        P(("dp", "seq"), "tensor", None),
        P(("dp", "seq"), "tensor", None),
        P(),
        P("tensor", None, ("dp", "seq")),
        P(("dp", "seq"), None, "tensor"),
        P("tensor", ("dp", "seq")),
        P(),
        P(),
        P(),
        P(("dp", "seq"), "tensor", None),
        P(("dp", "seq"), "tensor", None),
        P(),
        P("tensor", None, ("dp", "seq")),
        P(("dp", "seq"), None, "tensor"),
        P("tensor", ("dp", "seq")),
        P(),
        P(),
        P(),
        P(None, ("dp", "seq"), "tensor", None),
        P(None, ("dp", "seq"), "tensor", None),
        P(),
        P(None, "tensor", None, ("dp", "seq")),
        P(None, ("dp", "seq"), None, "tensor"),
        P(None, "tensor", ("dp", "seq")),
        P(),
        P(),
        P(),
    )
    return jax.shard_map(body, mesh=mesh, in_specs=in_specs, out_specs=out_specs, check_vma=False)
```

```python
import functools

import jax
import jax.numpy as jnp
from jax import lax
from jax.experimental import pallas as pl
from jax.experimental.layout import Layout, with_layout_constraint
from jax.experimental.pallas import tpu as pltpu
from jax.sharding import PartitionSpec as P

DK = 128
DV = 256
QKV = 2 * DK + DV
KCONV = 4
CHUNK = 128
ADAM_STEP = 5
VMEM = 48 * 2**20

F32 = jnp.float32
BF16 = jnp.bfloat16
HIGHEST = lax.Precision.HIGHEST

NN = (((1,), (0,)), ((), ()))
NT = (((1,), (1,)), ((), ()))
TN = (((0,), (0,)), ((), ()))


def dot(left, right, dims):
    return lax.dot_general(left, right, dims, preferred_element_type=F32)


def halves(array):
    high = array.astype(BF16)
    return high, (array - high.astype(F32)).astype(BF16)


def mm(left, right, dims=NN):
    left_high, left_low = halves(left)
    right_high, right_low = halves(right)
    return (
        dot(left_high, right_high, dims)
        + dot(left_high, right_low, dims)
        + dot(left_low, right_high, dims)
    )


def each(function, *lists):
    return [function(*items) for items in zip(*lists)]


def unit_lower_inverses(strict_parts, row_index, column_index):
    size = strict_parts[0].shape[0]
    identity = (row_index == column_index).astype(F32)
    same = (row_index // 8) == (column_index // 8)
    small = [jnp.where(same, part, 0.0) for part in strict_parts]
    squared = each(mm, small, small)
    fourth = each(mm, squared, squared)
    first = each(lambda n, n2: mm(identity - n, identity + n2), small, squared)
    inverse = each(lambda a, n4: a + mm(a, n4), first, fourth)
    width = 8
    while width < size:
        pair = (row_index // (2 * width)) == (column_index // (2 * width))
        below = pair & ((row_index // width) != (column_index // width))
        lower = [jnp.where(below, part, 0.0) for part in strict_parts]
        inner = each(mm, lower, inverse)
        inverse = each(lambda x, y: x - mm(x, y), inverse, inner)
        width *= 2
    return inverse


def silu_parts(values):
    gate = 1.0 / (1.0 + jnp.exp(-values))
    return values * gate, gate


def filtered_parts(padded_ref, rows_ref, halo_ref, taps_ref):
    length = rows_ref.shape[0]
    padded_ref[0:8, :] = halo_ref[0]
    padded_ref[8 : 8 + length, :] = rows_ref[...]
    raw = taps_ref[0:1, :] * padded_ref[5 : 5 + length, :]
    for tap in range(1, KCONV):
        raw = raw + taps_ref[tap : tap + 1, :] * padded_ref[5 + tap : 5 + tap + length, :]
    filtered, gate = silu_parts(raw)
    return raw, gate, filtered


def unit_rows(rows):
    factor = lax.rsqrt(jnp.sum(rows * rows, axis=-1, keepdims=True) + 1e-06)
    return rows * factor, factor


def chunk_slices(array, count):
    return [array[i * CHUNK : (i + 1) * CHUNK] for i in range(count)]


def fades(columns, g_rows, row_index, column_index):
    within = row_index >= column_index
    result = []
    for i, column in enumerate(columns):
        gap = column[:, 1:2] - g_rows[0:1, i * CHUNK : (i + 1) * CHUNK]
        result.append(jnp.where(within, jnp.exp(jnp.where(within, gap, 0.0)), 0.0))
    return result


def forward_kernel(
    rows_ref,
    halo_ref,
    taps_ref,
    columns_ref,
    g_rows_ref,
    reach_ref,
    local_ref,
    end_ref,
    starts_ref,
    inverse_ref,
    solved_values_ref,
    solved_keys_ref,
    step_ref,
    seen_ref,
    padded_ref,
):
    length = rows_ref.shape[0]
    count = length // CHUNK
    raw, gate, filtered = filtered_parts(padded_ref, rows_ref, halo_ref, taps_ref)
    query = unit_rows(filtered[:, :DK])[0] * DK ** (-0.5)
    key = unit_rows(filtered[:, DK : 2 * DK])[0]
    value = filtered[:, 2 * DK :]
    row_index = lax.broadcasted_iota(jnp.int32, (CHUNK, CHUNK), 0)
    column_index = lax.broadcasted_iota(jnp.int32, (CHUNK, CHUNK), 1)
    identity = (row_index == column_index).astype(F32)
    strict = row_index > column_index
    queries, keys, values = (chunk_slices(a, count) for a in (query, key, value))
    columns = chunk_slices(columns_ref[0], count)
    fade = fades(columns, g_rows_ref[0], row_index, column_index)
    key_products = each(lambda k: mm(k, k, NT), keys)
    parts = each(
        lambda kk, f, c: jnp.where(strict, c[:, 0:1] * kk * f, 0.0), key_products, fade, columns
    )
    inverses = unit_lower_inverses(parts, row_index, column_index)
    scores = each(lambda q, k, f: mm(q, k, NT) * f, queries, keys, fade)
    solved_values = each(lambda t, v, c: mm(t, c[:, 0:1] * v), inverses, values, columns)
    solved_keys = each(lambda t, k, c: mm(t, c[:, 0:1] * c[:, 2:3] * k), inverses, keys, columns)
    seen = each(
        lambda q, s, w, c: c[:, 2:3] * q - mm(s, w), queries, scores, solved_keys, columns
    )
    inner = each(mm, scores, solved_values)
    faded = each(lambda k, c: (c[:, 3:4] * k).T, keys, columns)
    steps = each(
        lambda k, w, c: c[CHUNK - 1 : CHUNK, 2:3] * identity - mm(k, w),
        faded,
        solved_keys,
        columns,
    )
    added = each(mm, faded, solved_values)
    state = jnp.concatenate([jnp.zeros((DK, DV), F32), identity], axis=1)
    for i in range(count):
        here = slice(i * CHUNK, (i + 1) * CHUNK)
        starts_ref[0, i] = state
        reached = mm(seen[i], state)
        local_ref[0, here, :] = reached[:, :DV] + inner[i]
        reach_ref[0, here, :] = reached[:, DV:]
        state = mm(steps[i], state)
        state = jnp.concatenate([state[:, :DV] + added[i], state[:, DV:]], axis=1)
        inverse_ref[0, here, :] = inverses[i]
        solved_values_ref[0, here, :] = solved_values[i]
        solved_keys_ref[0, here, :] = solved_keys[i]
        step_ref[0, here, :] = steps[i]
        seen_ref[0, here, :] = seen[i]
    end_ref[0] = state


def finish_kernel(local_ref, reach_ref, state_ref, gate_ref, scale_ref, mixed_ref):
    mixer_out = local_ref[0] + mm(reach_ref[0], state_ref[0])
    factor = lax.rsqrt(jnp.mean(mixer_out * mixer_out, axis=-1, keepdims=True) + 1e-05)
    opened = silu_parts(gate_ref[...])[0]
    mixed_ref[...] = (mixer_out * factor * scale_ref[...] * opened).astype(BF16)


def finish_back_kernel(
    local_ref,
    reach_ref,
    state_ref,
    gate_ref,
    scale_ref,
    grad_ref,
    grad_out_ref,
    grad_gate_ref,
    grad_scale_ref,
    correction_ref,
):
    mixer_out = local_ref[0] + mm(reach_ref[0], state_ref[0])
    factor = lax.rsqrt(jnp.mean(mixer_out * mixer_out, axis=-1, keepdims=True) + 1e-05)
    normal = mixer_out * factor
    gate_raw = gate_ref[...]
    opened, gate = silu_parts(gate_raw)
    grad = grad_ref[...]
    scale = scale_ref[...]
    with_normal = grad * normal
    grad_gate_ref[...] = (
        with_normal * scale * gate * (1.0 + gate_raw * (1.0 - gate))
    ).astype(BF16)
    summed = jnp.sum(with_normal * opened, axis=0, keepdims=True)
    grad_scale_ref[0] = jnp.broadcast_to(summed, (8, DV))
    grad_normal = grad * scale * opened
    shared = jnp.mean(grad_normal * normal, axis=-1, keepdims=True)
    grad_out = factor * (grad_normal - normal * shared)
    grad_out_ref[0] = grad_out
    correction_ref[0] = mm(reach_ref[0].T, grad_out)


def backward_kernel(
    rows_ref,
    halo_ref,
    taps_ref,
    columns_ref,
    g_rows_ref,
    starts_ref,
    inverse_ref,
    solved_values_ref,
    solved_keys_ref,
    step_ref,
    seen_ref,
    state_ref,
    later_ref,
    grad_out_ref,
    grad_rows_ref,
    tail_ref,
    before_ref,
    grad_taps_ref,
    grad_columns_ref,
    padded_ref,
    grad_padded_ref,
):
    length = rows_ref.shape[0]
    count = length // CHUNK
    raw, gate, filtered = filtered_parts(padded_ref, rows_ref, halo_ref, taps_ref)
    query_unit, query_factor = unit_rows(filtered[:, :DK])
    key, key_factor = unit_rows(filtered[:, DK : 2 * DK])
    query = query_unit * DK ** (-0.5)
    value = filtered[:, 2 * DK :]
    row_index = lax.broadcasted_iota(jnp.int32, (CHUNK, CHUNK), 0)
    column_index = lax.broadcasted_iota(jnp.int32, (CHUNK, CHUNK), 1)
    strict = row_index > column_index
    last = lax.broadcasted_iota(jnp.int32, (CHUNK, 1), 0) == CHUNK - 1
    queries, keys, values = (chunk_slices(a, count) for a in (query, key, value))
    columns = chunk_slices(columns_ref[0], count)
    inverses = chunk_slices(inverse_ref[0], count)
    solved_values = chunk_slices(solved_values_ref[0], count)
    solved_keys = chunk_slices(solved_keys_ref[0], count)
    steps = chunk_slices(step_ref[0], count)
    seen = chunk_slices(seen_ref[0], count)
    grad_outs = chunk_slices(grad_out_ref[0], count)
    fade = fades(columns, g_rows_ref[0], row_index, column_index)
    incoming = state_ref[0]
    states = [starts_ref[0, i][:, :DV] + mm(starts_ref[0, i][:, DV:], incoming) for i in range(count)]
    own_grads = each(lambda s, o: mm(s.T, o), seen, grad_outs)
    later = [None] * count
    carried = later_ref[0]
    for i in reversed(range(count)):
        later[i] = carried
        if i > 0:
            carried = mm(steps[i].T, carried) + own_grads[i]
    key_products = each(lambda k: mm(k, k, NT), keys)
    query_products = each(lambda q, k: mm(q, k, NT), queries, keys)
    scores = each(lambda p, f: p * f, query_products, fade)
    fresh = each(lambda u, w, s: u - mm(w, s), solved_values, solved_keys, states)
    faded = each(lambda k, c: c[:, 3:4] * k, keys, columns)
    grad_fresh = each(
        lambda p, o, k, l: mm(p.T, o) + mm(k, l), scores, grad_outs, faded, later
    )
    grad_scaled = each(lambda t, g: mm(t.T, g), inverses, grad_fresh)
    grad_scaled_keys = each(lambda g, s: -mm(g, s, NT), grad_scaled, states)
    grad_lower = each(
        lambda g, f: jnp.where(strict, -mm(g, f, NT), 0.0), grad_scaled, fresh
    )
    grad_scores = each(lambda o, f, d: mm(o, f, NT) * d, grad_outs, fresh, fade)
    lower_fade = each(lambda g, d: g * d, grad_lower, fade)
    pairs = each(lambda h, c: c[:, 0:1] * h, lower_fade, columns)
    from_state = each(lambda o, s: mm(o, s, NT), grad_outs, states)
    from_later = each(lambda f, l: mm(f, l, NT), fresh, later)
    grad_queries = each(
        lambda c, a, g, k: c[:, 2:3] * a + mm(g, k), columns, from_state, grad_scores, keys
    )
    grad_keys = each(
        lambda c, b, p, k, g, q, e: c[:, 0:1] * c[:, 2:3] * b
        + mm(p + p.T, k)
        + mm(g.T, q)
        + c[:, 3:4] * e,
        columns,
        grad_scaled_keys,
        pairs,
        keys,
        grad_scores,
        queries,
        from_later,
    )
    grad_values = each(lambda c, g: c[:, 0:1] * g, columns, grad_scaled)

    def across(array):
        return jnp.sum(array, axis=-1, keepdims=True)

    for i in range(count):
        column = columns[i]
        key_term = column[:, 2:3] * across(grad_scaled_keys[i] * keys[i])
        grad_update = (
            across(grad_scaled[i] * values[i])
            + key_term
            + across(lower_fade[i] * key_products[i])
        )
        both = grad_scores[i] * query_products[i] + pairs[i] * key_products[i]
        trailing = column[:, 3:4] * across(keys[i] * from_later[i])
        whole = column[CHUNK - 1 : CHUNK, 2:3] * jnp.sum(
            across(later[i] * states[i]), axis=0, keepdims=True
        ) + jnp.sum(trailing, axis=0, keepdims=True)
        grad_g = (
            across(both - both.T)
            + column[:, 2:3] * across(queries[i] * from_state[i])
            + column[:, 0:1] * key_term
            - trailing
            + jnp.where(last, whole, 0.0)
        )
        lane = lax.broadcasted_iota(jnp.int32, (CHUNK, 8), 1)
        grad_columns_ref[0, i * CHUNK : (i + 1) * CHUNK, :] = jnp.where(
            lane == 0, grad_update, grad_g
        )
    grad_query = jnp.concatenate(grad_queries, axis=0) * DK ** (-0.5)
    grad_key = jnp.concatenate(grad_keys, axis=0)
    grad_value = jnp.concatenate(grad_values, axis=0)
    grad_query = query_factor * (grad_query - query_unit * across(query_unit * grad_query))
    grad_key = key_factor * (grad_key - key * across(key * grad_key))
    grad_filtered = jnp.concatenate([grad_query, grad_key, grad_value], axis=1)
    grad_raw = grad_filtered * gate * (1.0 + raw * (1.0 - gate))
    zeros = jnp.zeros((8, QKV), F32)
    grad_padded_ref[0:8, :] = zeros
    grad_padded_ref[8 : 8 + length, :] = grad_raw
    grad_padded_ref[8 + length : 16 + length, :] = zeros
    grad_rows = taps_ref[0:1, :] * grad_padded_ref[11 : 11 + length, :]
    before = taps_ref[0:1, :] * grad_padded_ref[3:11, :]
    for tap in range(1, KCONV):
        tap_row = taps_ref[tap : tap + 1, :]
        grad_rows = grad_rows + tap_row * grad_padded_ref[11 - tap : 11 - tap + length, :]
        before = before + tap_row * grad_padded_ref[3 - tap : 11 - tap, :]
    grad_rows_ref[...] = grad_rows.astype(BF16)
    tail_ref[0] = grad_rows[length - 8 :]
    before_ref[0] = before
    sums = [
        jnp.sum(grad_raw * padded_ref[5 + tap : 5 + tap + length, :], axis=0, keepdims=True)
        for tap in range(KCONV)
    ]
    grad_taps_ref[0] = jnp.concatenate(sums, axis=0)


def chains_call(kernel, chains, heads, length, operands, outputs, scratch, flops):
    def spec(tag, shape):
        if tag == "rows":
            return pl.BlockSpec((length, shape[1] // heads), lambda i: (i // heads, i % heads))
        if tag == "edge":
            return pl.BlockSpec((1, 8, shape[2] // heads), lambda i: (i // heads, 0, i % heads))
        if tag == "taps":
            return pl.BlockSpec((shape[0], shape[1] // heads), lambda i: (0, i % heads))
        if tag == "all":
            return pl.BlockSpec(shape, lambda i: (0,) * len(shape))
        return pl.BlockSpec((1,) + tuple(shape[1:]), lambda i: (i,) + (0,) * (len(shape) - 1))

    moved = sum(a.size * a.dtype.itemsize for _, a in operands)
    return pl.pallas_call(
        kernel,
        grid=(chains,),
        in_specs=[spec(tag, a.shape) for tag, a in operands],
        out_specs=[spec(tag, shape) for tag, shape, _ in outputs],
        out_shape=[jax.ShapeDtypeStruct(shape, dtype) for _, shape, dtype in outputs],
        scratch_shapes=scratch,
        compiler_params=pltpu.CompilerParams(vmem_limit_bytes=VMEM),
        cost_estimate=pl.CostEstimate(
            flops=chains * flops, bytes_accessed=2 * moved, transcendentals=0
        ),
    )(*[a for _, a in operands])


def shifted(block, axis, distance):
    devices = range(lax.axis_size(axis))
    route = [(i, i + distance) for i in devices if i + distance in devices]
    return lax.ppermute(block, axis, route)


def swapped(block, axis, bits):
    return lax.ppermute(block, axis, [(i, i ^ bits) for i in range(lax.axis_size(axis))])


def group_swapped(block, dp_bits, tensor_bits):
    dp_size, tensor_size = lax.axis_size("dp"), lax.axis_size("tensor")
    route = [
        (d * tensor_size + t, (d ^ dp_bits) * tensor_size + (t ^ tensor_bits))
        for d in range(dp_size)
        for t in range(tensor_size)
    ]
    return lax.ppermute(block, ("dp", "tensor"), route)


def partner_bits():
    chips = lax.axis_size("tensor") // 2
    return [(d, t) for d in range(lax.axis_size("dp")) for t in range(chips) if (d, t) != (0, 0)]


def bits_slot(dp_bits, chip_bits):
    return dp_bits * (lax.axis_size("tensor") // 2) + chip_bits


def scatter_relative(partial):
    half = partial.shape[0] // 2
    summed = partial[:half].astype(F32) + swapped(partial[half:], "tensor", 1).astype(F32)
    rows = half // (lax.axis_size("dp") * lax.axis_size("tensor") // 2)
    total = summed[:rows]
    low = summed.astype(BF16)
    for d, t in partner_bits():
        slot = bits_slot(d, t)
        received = group_swapped(low[slot * rows : (slot + 1) * rows], d, 2 * t)
        total = total + received.astype(F32)
    return total


def gather_relative(own):
    parts = [own] + [group_swapped(own, d, 2 * t) for d, t in partner_bits()]
    here = jnp.concatenate(parts, axis=0)
    return jnp.concatenate([here, swapped(here, "tensor", 1)], axis=0)


def scatter_absolute(partial, tokens=(), started=None):
    dp_size, chips = lax.axis_size("dp"), lax.axis_size("tensor") // 2
    core = lax.axis_index("tensor") % 2
    chip = lax.axis_index("tensor") // 2
    device = lax.axis_index("dp")
    rows = partial.shape[0] // (2 * dp_size * chips)
    blocks = partial.reshape(dp_size * chips, 2, rows, -1)
    even, odd = blocks[:, 0], blocks[:, 1]
    mine = jnp.where(core == 0, even, odd)
    theirs = jnp.where(core == 0, odd, even)
    summed = mine.astype(F32) + swapped(theirs, "tensor", 1).astype(F32)
    low = after(summed.astype(BF16), tokens)
    if started is not None:
        started.append(low)
    total = lax.dynamic_index_in_dim(summed, device * chips + chip, 0, keepdims=False)
    for d, t in partner_bits():
        target = (device ^ d) * chips + (chip ^ t)
        block = lax.dynamic_index_in_dim(low, target, 0, keepdims=False)
        total = total + group_swapped(block, d, 2 * t).astype(F32)
    return total


def ordered(parts, core, other):
    first = jnp.where(core == 0, parts, other)
    second = jnp.where(core == 0, other, parts)
    stacked = jnp.stack([first, second], axis=1)
    return stacked.reshape((-1,) + parts.shape[2:])


def gather_absolute(own, over_dp=True):
    dp_size = lax.axis_size("dp") if over_dp else 1
    chips = lax.axis_size("tensor") // 2
    core = lax.axis_index("tensor") % 2
    chip = lax.axis_index("tensor") // 2
    device = lax.axis_index("dp") if over_dp else 0
    here = jnp.zeros((dp_size * chips,) + own.shape, own.dtype)
    here = lax.dynamic_update_index_in_dim(here, own, device * chips + chip, 0)
    for d, t in partner_bits():
        if d < dp_size:
            received = group_swapped(own, d, 2 * t)
            source = (device ^ d) * chips + (chip ^ t)
            here = lax.dynamic_update_index_in_dim(here, received, source, 0)
    return ordered(here, core, swapped(here, "tensor", 1))


def after(value, tokens):
    return lax.optimization_barrier((value, tokens))[0]


def butterfly_sum(array, axes):
    for axis in axes:
        distance, size = 1, lax.axis_size(axis)
        while distance < size:
            near = array + swapped(array, axis, distance)
            if 2 * distance < size:
                far = swapped(array, axis, 2 * distance) + swapped(array, axis, 3 * distance)
                array, distance = near + far, 4 * distance
            else:
                array, distance = near, 2 * distance
    return array


def contract_cols(left, right):
    return dot(left, right, NT)


def contract_rows(left, right):
    return dot(left, right, TN)


def adam_update(weight, gradient, moments, token_count):
    mean_grad = gradient / token_count
    is_first = lax.broadcasted_iota(jnp.int32, moments.shape, 0) == 0
    moved = 0.5 * moments + 0.5 * jnp.where(is_first, mean_grad, mean_grad * mean_grad)
    first = 0.5 * moments[0] + 0.5 * mean_grad
    second = 0.5 * moments[1] + 0.5 * mean_grad * mean_grad
    correction = 1.0 - 0.5**ADAM_STEP
    change = first / correction / (jnp.sqrt(second / correction) + 1e-08) + 0.1 * weight
    return (weight - 0.1 * change, moved)


def norm_parts(rows):
    factor = lax.rsqrt(jnp.mean(rows * rows, axis=-1, keepdims=True) + 1e-06)
    return factor, rows * factor


def norm_back(factor, normal, gain, grad):
    scaled = grad * gain
    shared = jnp.mean(scaled * normal, axis=-1, keepdims=True)
    return factor * (scaled - normal * shared), jnp.sum(grad * normal, axis=0)


def body(
    stream,
    cotangent,
    w_input,
    w_rates,
    w_conv,
    w_output,
    w_swiglu,
    w_down,
    w_gains,
    w_scale,
    w_heads,
    m_input,
    m_rates,
    m_conv,
    m_output,
    m_swiglu,
    m_down,
    m_gains,
    m_scale,
    m_heads,
):
    dp_size, seq_size, tensor_size = (lax.axis_size(a) for a in ("dp", "seq", "tensor"))
    length, width = stream.shape
    depth = w_input.shape[0]
    heads_stored = w_input.shape[1]
    heads = heads_stored // dp_size
    units_stored = w_swiglu.shape[2]
    units = units_stored // dp_size
    rows = length // tensor_size
    chains = dp_size * heads
    first_part = lax.axis_index("dp") == 0
    first_head = lax.axis_index("tensor") * heads_stored + lax.axis_index("dp") * heads

    def blocks_of(array, order):
        return jnp.concatenate([array[..., i * depth : (i + 1) * depth] for i in order], axis=-1)

    def turned(array):
        return blocks_of(array, [d * seq_size + q for q in range(seq_size) for d in range(dp_size)])

    def turned_back(array):
        return blocks_of(array, [q * dp_size + d for d in range(dp_size) for q in range(seq_size)])

    def mine_and_theirs(low, high):
        return jnp.where(first_part, low, high), jnp.where(first_part, high, low)

    def by_device(own, received):
        return jnp.where(first_part, own, received), jnp.where(first_part, received, own)

    low_input = w_input.astype(BF16)
    low_output = jnp.transpose(w_output.astype(BF16), (2, 0, 1))
    low_swiglu = w_swiglu.astype(BF16)
    low_down = w_down.astype(BF16).T

    def half_columns(index):
        chosen = slice(index * heads, (index + 1) * heads)
        some = slice(index * units, (index + 1) * units)
        return (
            low_input[:, chosen, :QKV].reshape(depth, -1),
            jnp.concatenate(
                [
                    low_input[:, chosen, QKV:].reshape(depth, -1),
                    low_output[:, chosen].reshape(depth, -1),
                ],
                axis=1,
            ),
            jnp.concatenate([low_swiglu[:, 0, some], low_swiglu[:, 1, some]], axis=1),
            low_down[:, some],
        )

    gathered = []
    for low, high in zip(half_columns(0), half_columns(1)):
        mine, theirs = mine_and_theirs(low, high)
        received = swapped(theirs, "dp", 1)
        shard = jnp.concatenate(by_device(mine, received), axis=0)
        gathered.append(lax.all_gather(shard, "seq", axis=0, tiled=True))
    full_qkv, full_mixer, full_swiglu, full_down = gathered
    full_gate, full_output = full_mixer[:, : heads * DV], full_mixer[:, heads * DV :]

    copies = dp_size * seq_size
    rates_low = jnp.broadcast_to(w_rates.astype(BF16).reshape(1, -1), (copies, depth * heads_stored * 2))
    rates_all = lax.all_to_all(rates_low, ("dp", "seq"), 0, 0, tiled=True)
    rates_all = rates_all.reshape(dp_size, seq_size, depth, dp_size, heads * 2)
    rates_all = jnp.swapaxes(rates_all, 0, 1).reshape(width, dp_size, heads * 2)
    full_rates = jnp.where(first_part, rates_all[:, 0], rates_all[:, dp_size - 1])

    quarter = lax.axis_index("tensor") * rows
    stream_rows = turned(lax.dynamic_slice_in_dim(stream, quarter, rows, 0))
    cotangent_rows = turned(lax.dynamic_slice_in_dim(cotangent, quarter, rows, 0))
    gains = turned(w_gains)
    factor_in, normal_in = norm_parts(stream_rows)
    normed_in = gather_absolute((normal_in * gains[0]).astype(BF16)).reshape(-1, width)

    projected = dot(normed_in, full_qkv, NN)
    rates = dot(normed_in, full_rates, NN)
    last_rows = projected.reshape(dp_size, length, heads * QKV)[:, length - 8 :]
    halo = shifted(last_rows, "seq", 1)
    taps = lax.dynamic_slice_in_dim(w_conv, first_head, heads, 1).reshape(KCONV, heads * QKV)
    head_rates = lax.dynamic_slice_in_dim(w_heads, first_head, heads, 1)
    by_chain = jnp.transpose(rates.reshape(dp_size, length, heads, 2), (3, 0, 2, 1))
    decay_raw = by_chain[0] + head_rates[1][None, :, None]
    update = jax.nn.sigmoid(by_chain[1]).reshape(chains, length)
    log_decay = -jnp.exp(head_rates[0])[None, :, None] * jax.nn.softplus(decay_raw)
    count = length // CHUNK
    upper = jnp.triu(jnp.ones((CHUNK, CHUNK), F32))
    cumulative = jnp.dot(
        log_decay.reshape(-1, CHUNK), upper, precision=HIGHEST
    ).reshape(chains, count, CHUNK)
    trailing = jnp.exp(cumulative[:, :, -1:] - cumulative).reshape(chains, length)
    cumulative = cumulative.reshape(chains, length)
    zero = jnp.zeros_like(update)
    columns = jnp.stack(
        [update, cumulative, jnp.exp(cumulative), trailing, zero, zero, zero, zero], axis=-1
    )
    g_rows = jnp.broadcast_to(cumulative[:, None, :], (chains, 8, length))
    call = functools.partial(chains_call, chains=chains, heads=heads, length=length)
    unit = 2 * CHUNK * DK * DK * count
    padded = pltpu.VMEM((length + 8, QKV), F32)
    reach, local, end, starts, inverse, solved_values, solved_keys, steps, seen = call(
        forward_kernel,
        operands=[
            ("rows", projected),
            ("edge", halo),
            ("taps", taps),
            ("chain", columns),
            ("chain", g_rows),
        ],
        outputs=[
            ("chain", (chains, length, DK), F32),
            ("chain", (chains, length, DV), F32),
            ("chain", (chains, DK, DV + DK), F32),
            ("chain", (chains, count, DK, DV + DK), F32),
            ("chain", (chains, length, CHUNK), F32),
            ("chain", (chains, length, DV), F32),
            ("chain", (chains, length, DK), F32),
            ("chain", (chains, length, DK), F32),
            ("chain", (chains, length, DK), F32),
        ],
        scratch=[padded],
        flops=90 * unit,
    )
    offset_map, linear_map = end[..., :DV], end[..., DV:]
    incoming = jnp.zeros((chains, DK, DV), F32)
    for hop in range(seq_size - 1):
        moved = offset_map
        if hop > 0:
            moved = moved + jnp.einsum("bkj,bjw->bkw", linear_map, incoming, precision=HIGHEST)
        incoming = shifted(moved.astype(BF16), "seq", 1).astype(F32)
    grad_ffn = gather_relative(after(cotangent_rows.astype(BF16), end))
    gate_raw = dot(after(normed_in, grad_ffn), full_gate, NN)
    scale_row = w_scale.reshape(1, DV)
    (mixed,) = call(
        finish_kernel,
        operands=[
            ("chain", local),
            ("chain", reach),
            ("chain", incoming),
            ("rows", gate_raw),
            ("all", scale_row),
        ],
        outputs=[("rows", (dp_size * length, heads * DV), BF16)],
        scratch=[],
        flops=6 * unit,
    )
    attention = scatter_absolute(contract_cols(mixed, full_output).astype(BF16))

    residual = stream_rows + attention
    factor_mid, normal_mid = norm_parts(residual)
    normed_mid = gather_relative((normal_mid * gains[1]).astype(BF16))
    gate_up = dot(normed_mid, full_swiglu, NN)
    gate_part, up_part = gate_up[:, :units], gate_up[:, units:]
    sigmoid_gate = jax.nn.sigmoid(gate_part)
    silu_gate = gate_part * sigmoid_gate
    activated = after((silu_gate * up_part).astype(BF16), full_down)
    grad_down_weights = contract_rows(grad_ffn, activated).astype(BF16)
    down_sum = lax.psum_scatter(grad_down_weights, "seq", scatter_dimension=0, tiled=True)
    grad_activated = dot(after(grad_ffn, grad_down_weights), full_down, NN)
    grad_gate = grad_activated * up_part * sigmoid_gate * (1.0 + gate_part * (1.0 - sigmoid_gate))
    grad_up = grad_activated * silu_gate
    grad_gate_up = jnp.concatenate([grad_gate.astype(BF16), grad_up.astype(BF16)], axis=1)
    normed_mid_term = contract_cols(grad_gate_up, full_swiglu).astype(BF16)
    grad_normed_mid = scatter_relative(normed_mid_term)
    grad_swiglu_weights = contract_rows(after(normed_mid, normed_mid_term), grad_gate_up)
    grad_swiglu_weights = after(grad_swiglu_weights.astype(BF16), grad_down_weights)
    swiglu_sum = lax.psum_scatter(grad_swiglu_weights, "seq", scatter_dimension=0, tiled=True)
    from_mid, grad_gain_mid = norm_back(factor_mid, normal_mid, gains[1], grad_normed_mid)
    from_mid = after(from_mid, grad_swiglu_weights)
    grad_attention = gather_absolute((cotangent_rows + from_mid).astype(BF16)).reshape(-1, width)
    grad_mixed = dot(grad_attention, full_output, NN)
    grad_mixer_out, grad_gate_raw, grad_scale, correction = call(
        finish_back_kernel,
        operands=[
            ("chain", local),
            ("chain", reach),
            ("chain", incoming),
            ("rows", gate_raw),
            ("all", scale_row),
            ("rows", grad_mixed),
        ],
        outputs=[
            ("chain", (chains, length, DV), F32),
            ("rows", (dp_size * length, heads * DV), BF16),
            ("chain", (chains, 8, DV), F32),
            ("chain", (chains, DK, DV), F32),
        ],
        scratch=[],
        flops=12 * unit,
    )
    later = jnp.zeros((chains, DK, DV), F32)
    for hop in range(seq_size - 1):
        moved = correction
        if hop > 0:
            moved = moved + jnp.einsum("bjk,bjw->bkw", linear_map, later, precision=HIGHEST)
        later = shifted(moved.astype(BF16), "seq", -1)
        if hop == 0:
            feedforward = scatter_relative(
                contract_cols(after(activated, later), full_down).astype(BF16)
            )
        later = later.astype(F32)
    later = after(later, (swiglu_sum, feedforward))
    grad_mixer_weights = jnp.concatenate(
        [
            contract_rows(normed_in, grad_gate_raw).astype(BF16),
            contract_rows(grad_attention, mixed).astype(BF16),
        ],
        axis=1,
    )
    grad_rows, tail, before, grad_taps, grad_columns = call(
        backward_kernel,
        operands=[
            ("rows", projected),
            ("edge", halo),
            ("taps", taps),
            ("chain", columns),
            ("chain", g_rows),
            ("chain", starts),
            ("chain", inverse),
            ("chain", solved_values),
            ("chain", solved_keys),
            ("chain", steps),
            ("chain", seen),
            ("chain", incoming),
            ("chain", later),
            ("chain", grad_mixer_out),
        ],
        outputs=[
            ("rows", (dp_size * length, heads * QKV), BF16),
            ("edge", (dp_size, 8, heads * QKV), F32),
            ("edge", (dp_size, 8, heads * QKV), F32),
            ("chain", (chains, KCONV, QKV), F32),
            ("chain", (chains, length, 8), F32),
        ],
        scratch=[padded, pltpu.VMEM((length + 16, QKV), F32)],
        flops=120 * unit,
    )
    patched = (tail + shifted(before, "seq", -1)).astype(BF16)
    grad_projected = grad_rows.reshape(dp_size, length, heads * QKV)
    grad_projected = lax.dynamic_update_slice_in_dim(grad_projected, patched, length - 8, 1)
    grad_projected = grad_projected.reshape(dp_size * length, heads * QKV)
    grad_update = grad_columns[..., 0]
    grad_log_decay = jnp.dot(
        grad_columns[..., 1].reshape(-1, CHUNK), upper.T, precision=HIGHEST
    ).reshape(dp_size, heads, length)
    grad_decay_raw = (
        -jnp.exp(head_rates[0])[None, :, None] * grad_log_decay * jax.nn.sigmoid(decay_raw)
    )
    grad_update_raw = (grad_update * update * (1.0 - update)).reshape(dp_size, heads, length)
    grad_rates = jnp.stack([grad_decay_raw, grad_update_raw], axis=-1)
    grad_rates = jnp.transpose(grad_rates, (0, 2, 1, 3)).reshape(-1, heads * 2).astype(BF16)
    grad_heads = jnp.stack(
        [
            jnp.sum(grad_log_decay * log_decay, axis=(0, 2)),
            jnp.sum(grad_decay_raw, axis=(0, 2)),
        ]
    )
    grad_qkv_weights = contract_rows(normed_in, grad_projected).astype(BF16)
    mixer_sum = lax.psum_scatter(
        after(grad_mixer_weights, (swiglu_sum, down_sum)),
        "seq",
        scatter_dimension=0,
        tiled=True,
    )
    qkv_sum = lax.psum_scatter(
        after(grad_qkv_weights, swiglu_sum), "seq", scatter_dimension=0, tiled=True
    )
    grad_rates_weights = contract_rows(grad_rates, after(normed_in, grad_qkv_weights))
    def halves_of(part):
        return mine_and_theirs(part[:depth], part[depth:])

    def exchanged(halves):
        own, theirs = halves
        received = swapped(theirs, "dp", 1)
        return tuple(a.astype(F32) for a in by_device(own, received))

    mixer_parts = exchanged(halves_of(mixer_sum))
    started = []
    normed_in_term = (
        contract_cols(after(grad_projected, (grad_qkv_weights, grad_rates_weights)), full_qkv)
        + contract_cols(grad_gate_raw, full_gate)
        + contract_cols(grad_rates, full_rates)
    )
    grad_normed_in = scatter_absolute(normed_in_term.astype(BF16), mixer_parts, started)
    from_in, grad_gain_in = norm_back(factor_in, normal_in, gains[0], grad_normed_in)
    added = turned_back(jnp.concatenate([attention + feedforward, from_mid + from_in], axis=0))
    added = gather_absolute(
        jnp.concatenate([added[:rows], added[rows:]], axis=1).astype(BF16), False
    ).reshape(length, 2 * width)
    gathered_rows = added
    qkv_halves = halves_of(after(qkv_sum, added))
    added = after(added, qkv_halves)
    result = stream + added[:, :width].astype(F32)
    grad_stream = cotangent + added[:, width:].astype(F32)

    swiglu_parts = exchanged(halves_of(after(swiglu_sum, started)))
    down_parts = exchanged(halves_of(after(down_sum, started)))
    g_output = jnp.concatenate(
        [m[:, heads * DV :].T.reshape(heads, DV, depth) for m in mixer_parts], axis=0
    )
    g_swiglu = jnp.stack(
        [
            jnp.concatenate([f[:, :units] for f in swiglu_parts], axis=1),
            jnp.concatenate([f[:, units:] for f in swiglu_parts], axis=1),
        ],
        axis=1,
    )
    g_swiglu = with_layout_constraint(g_swiglu, Layout((0, 1, 2)))
    g_down = jnp.concatenate([f.T for f in down_parts], axis=0)

    conv_term = jnp.zeros_like(w_conv)
    grad_taps = jnp.sum(grad_taps.reshape(dp_size, heads, KCONV, QKV), axis=0)
    conv_term = lax.dynamic_update_slice_in_dim(
        conv_term, jnp.swapaxes(grad_taps, 0, 1), first_head, 1
    )
    heads_term = lax.dynamic_update_slice_in_dim(
        jnp.zeros_like(w_heads), grad_heads, first_head, 1
    )
    gains_term = turned_back(jnp.stack([grad_gain_in, grad_gain_mid]))
    scale_term = jnp.sum(grad_scale[:, 0], axis=0)
    first = lax.axis_index("dp") == 0
    rates_term = jnp.concatenate(
        [jnp.where(first, grad_rates_weights, 0.0), jnp.where(first, 0.0, grad_rates_weights)], axis=0
    )
    small = [conv_term, heads_term, gains_term, scale_term]
    flat = jnp.concatenate([a.reshape(-1) for a in small])
    flat = butterfly_sum(after(flat, gathered_rows), ("tensor",))
    flat = jnp.concatenate([flat, rates_term.reshape(-1)])
    flat = butterfly_sum(flat, ("dp", "seq"))
    sums, at = [], 0
    for a in small:
        sums.append(flat[at : at + a.size].reshape(a.shape))
        at += a.size
    g_conv, g_heads, g_gains, g_scale = sums
    block = lax.axis_index("seq") * dp_size + lax.axis_index("dp")
    g_rates = lax.dynamic_slice_in_dim(
        flat[at:].reshape(heads_stored * 2, width), block * depth, depth, 1
    ).T.reshape(depth, heads_stored, 2)

    tokens = float(length * dp_size * seq_size)
    new_rates, moment_rates = adam_update(w_rates, g_rates, m_rates, tokens)
    new_conv, moment_conv = adam_update(w_conv, g_conv, m_conv, tokens)
    new_output, moment_output = adam_update(w_output, g_output, m_output, tokens)
    new_swiglu, moment_swiglu = adam_update(w_swiglu, g_swiglu, m_swiglu, tokens)
    new_down, moment_down = adam_update(w_down, g_down, m_down, tokens)
    new_gains, moment_gains = adam_update(w_gains, g_gains, m_gains, tokens)
    new_scale, moment_scale = adam_update(w_scale, g_scale, m_scale, tokens)
    new_heads, moment_heads = adam_update(w_heads, g_heads, m_heads, tokens)
    qkv_parts = exchanged(qkv_halves)
    g_input = jnp.concatenate(
        [
            jnp.concatenate(
                [
                    q.reshape(depth, heads, QKV),
                    m[:, : heads * DV].reshape(depth, heads, DV),
                ],
                axis=2,
            )
            for q, m in zip(qkv_parts, mixer_parts)
        ],
        axis=1,
    )
    new_input, moment_input = adam_update(w_input, g_input, m_input, tokens)
    return (
        result,
        grad_stream,
        g_input,
        g_rates,
        g_conv,
        g_output,
        g_swiglu,
        g_down,
        g_gains,
        g_scale,
        g_heads,
        new_input,
        new_rates,
        new_conv,
        new_output,
        new_swiglu,
        new_down,
        new_gains,
        new_scale,
        new_heads,
        moment_input,
        moment_rates,
        moment_conv,
        moment_output,
        moment_swiglu,
        moment_down,
        moment_gains,
        moment_scale,
        moment_heads,
    )


def solution(mesh):
    in_specs = (
        P(("dp", "seq"), None),
        P(("dp", "seq"), None),
        P(("dp", "seq"), "tensor", None),
        P(("dp", "seq"), "tensor", None),
        P(),
        P("tensor", None, ("dp", "seq")),
        P(("dp", "seq"), None, "tensor"),
        P("tensor", ("dp", "seq")),
        P(),
        P(),
        P(),
        P(None, ("dp", "seq"), "tensor", None),
        P(None, ("dp", "seq"), "tensor", None),
        P(),
        P(None, "tensor", None, ("dp", "seq")),
        P(None, ("dp", "seq"), None, "tensor"),
        P(None, "tensor", ("dp", "seq")),
        P(),
        P(),
        P(),
    )
    out_specs = (
        P(("dp", "seq"), None),
        P(("dp", "seq"), None),
        P(("dp", "seq"), "tensor", None),
        P(("dp", "seq"), "tensor", None),
        P(),
        P("tensor", None, ("dp", "seq")),
        P(("dp", "seq"), None, "tensor"),
        P("tensor", ("dp", "seq")),
        P(),
        P(),
        P(),
        P(("dp", "seq"), "tensor", None),
        P(("dp", "seq"), "tensor", None),
        P(),
        P("tensor", None, ("dp", "seq")),
        P(("dp", "seq"), None, "tensor"),
        P("tensor", ("dp", "seq")),
        P(),
        P(),
        P(),
        P(None, ("dp", "seq"), "tensor", None),
        P(None, ("dp", "seq"), "tensor", None),
        P(),
        P(None, "tensor", None, ("dp", "seq")),
        P(None, ("dp", "seq"), None, "tensor"),
        P(None, "tensor", ("dp", "seq")),
        P(),
        P(),
        P(),
    )
    return jax.shard_map(body, mesh=mesh, in_specs=in_specs, out_specs=out_specs, check_vma=False)
```

```python
import functools

import jax
import jax.numpy as jnp
from jax import lax
from jax.experimental import pallas as pl
from jax.experimental.layout import Layout, with_layout_constraint
from jax.experimental.pallas import tpu as pltpu
from jax.sharding import PartitionSpec as P

DK = 128
DV = 256
QKV = 2 * DK + DV
KCONV = 4
CHUNK = 128
ADAM_STEP = 5
VMEM = 48 * 2**20

F32 = jnp.float32
BF16 = jnp.bfloat16
HIGHEST = lax.Precision.HIGHEST

NN = (((1,), (0,)), ((), ()))
NT = (((1,), (1,)), ((), ()))
TN = (((0,), (0,)), ((), ()))


def dot(left, right, dims):
    return lax.dot_general(left, right, dims, preferred_element_type=F32)


def halves(array):
    high = array.astype(BF16)
    return high, (array - high.astype(F32)).astype(BF16)


def mm(left, right, dims=NN):
    left_high, left_low = halves(left)
    right_high, right_low = halves(right)
    return (
        dot(left_high, right_high, dims)
        + dot(left_high, right_low, dims)
        + dot(left_low, right_high, dims)
    )


def each(function, *lists):
    return [function(*items) for items in zip(*lists)]


def unit_lower_inverses(strict_parts, row_index, column_index):
    size = strict_parts[0].shape[0]
    identity = (row_index == column_index).astype(F32)
    same = (row_index // 8) == (column_index // 8)
    small = [jnp.where(same, part, 0.0) for part in strict_parts]
    squared = each(mm, small, small)
    fourth = each(mm, squared, squared)
    first = each(lambda n, n2: mm(identity - n, identity + n2), small, squared)
    inverse = each(lambda a, n4: a + mm(a, n4), first, fourth)
    width = 8
    while width < size:
        pair = (row_index // (2 * width)) == (column_index // (2 * width))
        below = pair & ((row_index // width) != (column_index // width))
        lower = [jnp.where(below, part, 0.0) for part in strict_parts]
        inner = each(mm, lower, inverse)
        inverse = each(lambda x, y: x - mm(x, y), inverse, inner)
        width *= 2
    return inverse


def silu_parts(values):
    gate = 1.0 / (1.0 + jnp.exp(-values))
    return values * gate, gate


def filtered_parts(padded_ref, rows_ref, halo_ref, taps_ref):
    length = rows_ref.shape[0]
    padded_ref[0:8, :] = halo_ref[0]
    padded_ref[8 : 8 + length, :] = rows_ref[...]
    raw = taps_ref[0:1, :] * padded_ref[5 : 5 + length, :]
    for tap in range(1, KCONV):
        raw = raw + taps_ref[tap : tap + 1, :] * padded_ref[5 + tap : 5 + tap + length, :]
    filtered, gate = silu_parts(raw)
    return raw, gate, filtered


def unit_rows(rows):
    factor = lax.rsqrt(jnp.sum(rows * rows, axis=-1, keepdims=True) + 1e-06)
    return rows * factor, factor


def chunk_slices(array, count):
    return [array[i * CHUNK : (i + 1) * CHUNK] for i in range(count)]


def fades(columns, g_rows, row_index, column_index):
    within = row_index >= column_index
    result = []
    for i, column in enumerate(columns):
        gap = column[:, 1:2] - g_rows[0:1, i * CHUNK : (i + 1) * CHUNK]
        result.append(jnp.where(within, jnp.exp(jnp.where(within, gap, 0.0)), 0.0))
    return result


def forward_kernel(
    rows_ref,
    halo_ref,
    taps_ref,
    columns_ref,
    g_rows_ref,
    reach_ref,
    local_ref,
    end_ref,
    starts_ref,
    inverse_ref,
    solved_values_ref,
    solved_keys_ref,
    step_ref,
    seen_ref,
    padded_ref,
):
    length = rows_ref.shape[0]
    count = length // CHUNK
    raw, gate, filtered = filtered_parts(padded_ref, rows_ref, halo_ref, taps_ref)
    query = unit_rows(filtered[:, :DK])[0] * DK ** (-0.5)
    key = unit_rows(filtered[:, DK : 2 * DK])[0]
    value = filtered[:, 2 * DK :]
    row_index = lax.broadcasted_iota(jnp.int32, (CHUNK, CHUNK), 0)
    column_index = lax.broadcasted_iota(jnp.int32, (CHUNK, CHUNK), 1)
    identity = (row_index == column_index).astype(F32)
    strict = row_index > column_index
    queries, keys, values = (chunk_slices(a, count) for a in (query, key, value))
    columns = chunk_slices(columns_ref[0], count)
    fade = fades(columns, g_rows_ref[0], row_index, column_index)
    key_products = each(lambda k: mm(k, k, NT), keys)
    parts = each(
        lambda kk, f, c: jnp.where(strict, c[:, 0:1] * kk * f, 0.0), key_products, fade, columns
    )
    inverses = unit_lower_inverses(parts, row_index, column_index)
    scores = each(lambda q, k, f: mm(q, k, NT) * f, queries, keys, fade)
    solved_values = each(lambda t, v, c: mm(t, c[:, 0:1] * v), inverses, values, columns)
    solved_keys = each(lambda t, k, c: mm(t, c[:, 0:1] * c[:, 2:3] * k), inverses, keys, columns)
    seen = each(
        lambda q, s, w, c: c[:, 2:3] * q - mm(s, w), queries, scores, solved_keys, columns
    )
    inner = each(mm, scores, solved_values)
    faded = each(lambda k, c: (c[:, 3:4] * k).T, keys, columns)
    steps = each(
        lambda k, w, c: c[CHUNK - 1 : CHUNK, 2:3] * identity - mm(k, w),
        faded,
        solved_keys,
        columns,
    )
    added = each(mm, faded, solved_values)
    state = jnp.concatenate([jnp.zeros((DK, DV), F32), identity], axis=1)
    for i in range(count):
        here = slice(i * CHUNK, (i + 1) * CHUNK)
        starts_ref[0, i] = state
        reached = mm(seen[i], state)
        local_ref[0, here, :] = reached[:, :DV] + inner[i]
        reach_ref[0, here, :] = reached[:, DV:]
        state = mm(steps[i], state)
        state = jnp.concatenate([state[:, :DV] + added[i], state[:, DV:]], axis=1)
        inverse_ref[0, here, :] = inverses[i]
        solved_values_ref[0, here, :] = solved_values[i]
        solved_keys_ref[0, here, :] = solved_keys[i]
        step_ref[0, here, :] = steps[i]
        seen_ref[0, here, :] = seen[i]
    end_ref[0] = state


def finish_kernel(local_ref, reach_ref, state_ref, gate_ref, scale_ref, mixed_ref):
    mixer_out = local_ref[0] + mm(reach_ref[0], state_ref[0])
    factor = lax.rsqrt(jnp.mean(mixer_out * mixer_out, axis=-1, keepdims=True) + 1e-05)
    opened = silu_parts(gate_ref[...])[0]
    mixed_ref[...] = (mixer_out * factor * scale_ref[...] * opened).astype(BF16)


def finish_back_kernel(
    local_ref,
    reach_ref,
    state_ref,
    gate_ref,
    scale_ref,
    grad_ref,
    grad_out_ref,
    grad_gate_ref,
    grad_scale_ref,
    correction_ref,
):
    mixer_out = local_ref[0] + mm(reach_ref[0], state_ref[0])
    factor = lax.rsqrt(jnp.mean(mixer_out * mixer_out, axis=-1, keepdims=True) + 1e-05)
    normal = mixer_out * factor
    gate_raw = gate_ref[...]
    opened, gate = silu_parts(gate_raw)
    grad = grad_ref[...]
    scale = scale_ref[...]
    with_normal = grad * normal
    grad_gate_ref[...] = (
        with_normal * scale * gate * (1.0 + gate_raw * (1.0 - gate))
    ).astype(BF16)
    summed = jnp.sum(with_normal * opened, axis=0, keepdims=True)
    grad_scale_ref[0] = jnp.broadcast_to(summed, (8, DV))
    grad_normal = grad * scale * opened
    shared = jnp.mean(grad_normal * normal, axis=-1, keepdims=True)
    grad_out = factor * (grad_normal - normal * shared)
    grad_out_ref[0] = grad_out
    correction_ref[0] = mm(reach_ref[0].T, grad_out)


def backward_kernel(
    rows_ref,
    halo_ref,
    taps_ref,
    columns_ref,
    g_rows_ref,
    starts_ref,
    inverse_ref,
    solved_values_ref,
    solved_keys_ref,
    step_ref,
    seen_ref,
    state_ref,
    later_ref,
    grad_out_ref,
    grad_rows_ref,
    tail_ref,
    before_ref,
    grad_taps_ref,
    grad_columns_ref,
    padded_ref,
    grad_padded_ref,
):
    length = rows_ref.shape[0]
    count = length // CHUNK
    raw, gate, filtered = filtered_parts(padded_ref, rows_ref, halo_ref, taps_ref)
    query_unit, query_factor = unit_rows(filtered[:, :DK])
    key, key_factor = unit_rows(filtered[:, DK : 2 * DK])
    query = query_unit * DK ** (-0.5)
    value = filtered[:, 2 * DK :]
    row_index = lax.broadcasted_iota(jnp.int32, (CHUNK, CHUNK), 0)
    column_index = lax.broadcasted_iota(jnp.int32, (CHUNK, CHUNK), 1)
    strict = row_index > column_index
    last = lax.broadcasted_iota(jnp.int32, (CHUNK, 1), 0) == CHUNK - 1
    queries, keys, values = (chunk_slices(a, count) for a in (query, key, value))
    columns = chunk_slices(columns_ref[0], count)
    inverses = chunk_slices(inverse_ref[0], count)
    solved_values = chunk_slices(solved_values_ref[0], count)
    solved_keys = chunk_slices(solved_keys_ref[0], count)
    steps = chunk_slices(step_ref[0], count)
    seen = chunk_slices(seen_ref[0], count)
    grad_outs = chunk_slices(grad_out_ref[0], count)
    fade = fades(columns, g_rows_ref[0], row_index, column_index)
    incoming = state_ref[0]
    states = [starts_ref[0, i][:, :DV] + mm(starts_ref[0, i][:, DV:], incoming) for i in range(count)]
    own_grads = each(lambda s, o: mm(s.T, o), seen, grad_outs)
    later = [None] * count
    carried = later_ref[0]
    for i in reversed(range(count)):
        later[i] = carried
        if i > 0:
            carried = mm(steps[i].T, carried) + own_grads[i]
    key_products = each(lambda k: mm(k, k, NT), keys)
    query_products = each(lambda q, k: mm(q, k, NT), queries, keys)
    scores = each(lambda p, f: p * f, query_products, fade)
    fresh = each(lambda u, w, s: u - mm(w, s), solved_values, solved_keys, states)
    faded = each(lambda k, c: c[:, 3:4] * k, keys, columns)
    grad_fresh = each(
        lambda p, o, k, l: mm(p.T, o) + mm(k, l), scores, grad_outs, faded, later
    )
    grad_scaled = each(lambda t, g: mm(t.T, g), inverses, grad_fresh)
    grad_scaled_keys = each(lambda g, s: -mm(g, s, NT), grad_scaled, states)
    grad_lower = each(
        lambda g, f: jnp.where(strict, -mm(g, f, NT), 0.0), grad_scaled, fresh
    )
    grad_scores = each(lambda o, f, d: mm(o, f, NT) * d, grad_outs, fresh, fade)
    lower_fade = each(lambda g, d: g * d, grad_lower, fade)
    pairs = each(lambda h, c: c[:, 0:1] * h, lower_fade, columns)
    from_state = each(lambda o, s: mm(o, s, NT), grad_outs, states)
    from_later = each(lambda f, l: mm(f, l, NT), fresh, later)
    grad_queries = each(
        lambda c, a, g, k: c[:, 2:3] * a + mm(g, k), columns, from_state, grad_scores, keys
    )
    grad_keys = each(
        lambda c, b, p, k, g, q, e: c[:, 0:1] * c[:, 2:3] * b
        + mm(p + p.T, k)
        + mm(g.T, q)
        + c[:, 3:4] * e,
        columns,
        grad_scaled_keys,
        pairs,
        keys,
        grad_scores,
        queries,
        from_later,
    )
    grad_values = each(lambda c, g: c[:, 0:1] * g, columns, grad_scaled)

    def across(array):
        return jnp.sum(array, axis=-1, keepdims=True)

    for i in range(count):
        column = columns[i]
        key_term = column[:, 2:3] * across(grad_scaled_keys[i] * keys[i])
        grad_update = (
            across(grad_scaled[i] * values[i])
            + key_term
            + across(lower_fade[i] * key_products[i])
        )
        both = grad_scores[i] * query_products[i] + pairs[i] * key_products[i]
        trailing = column[:, 3:4] * across(keys[i] * from_later[i])
        whole = column[CHUNK - 1 : CHUNK, 2:3] * jnp.sum(
            across(later[i] * states[i]), axis=0, keepdims=True
        ) + jnp.sum(trailing, axis=0, keepdims=True)
        grad_g = (
            across(both - both.T)
            + column[:, 2:3] * across(queries[i] * from_state[i])
            + column[:, 0:1] * key_term
            - trailing
            + jnp.where(last, whole, 0.0)
        )
        lane = lax.broadcasted_iota(jnp.int32, (CHUNK, 8), 1)
        grad_columns_ref[0, i * CHUNK : (i + 1) * CHUNK, :] = jnp.where(
            lane == 0, grad_update, grad_g
        )
    grad_query = jnp.concatenate(grad_queries, axis=0) * DK ** (-0.5)
    grad_key = jnp.concatenate(grad_keys, axis=0)
    grad_value = jnp.concatenate(grad_values, axis=0)
    grad_query = query_factor * (grad_query - query_unit * across(query_unit * grad_query))
    grad_key = key_factor * (grad_key - key * across(key * grad_key))
    grad_filtered = jnp.concatenate([grad_query, grad_key, grad_value], axis=1)
    grad_raw = grad_filtered * gate * (1.0 + raw * (1.0 - gate))
    zeros = jnp.zeros((8, QKV), F32)
    grad_padded_ref[0:8, :] = zeros
    grad_padded_ref[8 : 8 + length, :] = grad_raw
    grad_padded_ref[8 + length : 16 + length, :] = zeros
    grad_rows = taps_ref[0:1, :] * grad_padded_ref[11 : 11 + length, :]
    before = taps_ref[0:1, :] * grad_padded_ref[3:11, :]
    for tap in range(1, KCONV):
        tap_row = taps_ref[tap : tap + 1, :]
        grad_rows = grad_rows + tap_row * grad_padded_ref[11 - tap : 11 - tap + length, :]
        before = before + tap_row * grad_padded_ref[3 - tap : 11 - tap, :]
    grad_rows_ref[...] = grad_rows.astype(BF16)
    tail_ref[0] = grad_rows[length - 8 :]
    before_ref[0] = before
    sums = [
        jnp.sum(grad_raw * padded_ref[5 + tap : 5 + tap + length, :], axis=0, keepdims=True)
        for tap in range(KCONV)
    ]
    grad_taps_ref[0] = jnp.concatenate(sums, axis=0)


def chains_call(kernel, chains, heads, length, operands, outputs, scratch, flops):
    def spec(tag, shape):
        if tag == "rows":
            return pl.BlockSpec((length, shape[1] // heads), lambda i: (i // heads, i % heads))
        if tag == "edge":
            return pl.BlockSpec((1, 8, shape[2] // heads), lambda i: (i // heads, 0, i % heads))
        if tag == "taps":
            return pl.BlockSpec((shape[0], shape[1] // heads), lambda i: (0, i % heads))
        if tag == "all":
            return pl.BlockSpec(shape, lambda i: (0,) * len(shape))
        return pl.BlockSpec((1,) + tuple(shape[1:]), lambda i: (i,) + (0,) * (len(shape) - 1))

    moved = sum(a.size * a.dtype.itemsize for _, a in operands)
    return pl.pallas_call(
        kernel,
        grid=(chains,),
        in_specs=[spec(tag, a.shape) for tag, a in operands],
        out_specs=[spec(tag, shape) for tag, shape, _ in outputs],
        out_shape=[jax.ShapeDtypeStruct(shape, dtype) for _, shape, dtype in outputs],
        scratch_shapes=scratch,
        compiler_params=pltpu.CompilerParams(vmem_limit_bytes=VMEM),
        cost_estimate=pl.CostEstimate(
            flops=chains * flops, bytes_accessed=2 * moved, transcendentals=0
        ),
    )(*[a for _, a in operands])


def shifted(block, axis, distance):
    devices = range(lax.axis_size(axis))
    route = [(i, i + distance) for i in devices if i + distance in devices]
    return lax.ppermute(block, axis, route)


def swapped(block, axis, bits):
    return lax.ppermute(block, axis, [(i, i ^ bits) for i in range(lax.axis_size(axis))])


def group_swapped(block, dp_bits, tensor_bits):
    dp_size, tensor_size = lax.axis_size("dp"), lax.axis_size("tensor")
    route = [
        (d * tensor_size + t, (d ^ dp_bits) * tensor_size + (t ^ tensor_bits))
        for d in range(dp_size)
        for t in range(tensor_size)
    ]
    return lax.ppermute(block, ("dp", "tensor"), route)


def partner_bits():
    chips = lax.axis_size("tensor") // 2
    return [(d, t) for d in range(lax.axis_size("dp")) for t in range(chips) if (d, t) != (0, 0)]


def bits_slot(dp_bits, chip_bits):
    return dp_bits * (lax.axis_size("tensor") // 2) + chip_bits


def scatter_relative(partial):
    half = partial.shape[0] // 2
    summed = partial[:half].astype(F32) + swapped(partial[half:], "tensor", 1).astype(F32)
    rows = half // (lax.axis_size("dp") * lax.axis_size("tensor") // 2)
    total = summed[:rows]
    low = summed.astype(BF16)
    for d, t in partner_bits():
        slot = bits_slot(d, t)
        received = group_swapped(low[slot * rows : (slot + 1) * rows], d, 2 * t)
        total = total + received.astype(F32)
    return total


def gather_relative(own):
    parts = [own] + [group_swapped(own, d, 2 * t) for d, t in partner_bits()]
    here = jnp.concatenate(parts, axis=0)
    return jnp.concatenate([here, swapped(here, "tensor", 1)], axis=0)


def scatter_absolute(partial, tokens=(), started=None):
    dp_size, chips = lax.axis_size("dp"), lax.axis_size("tensor") // 2
    core = lax.axis_index("tensor") % 2
    chip = lax.axis_index("tensor") // 2
    device = lax.axis_index("dp")
    rows = partial.shape[0] // (2 * dp_size * chips)
    blocks = partial.reshape(dp_size * chips, 2, rows, -1)
    even, odd = blocks[:, 0], blocks[:, 1]
    mine = jnp.where(core == 0, even, odd)
    theirs = jnp.where(core == 0, odd, even)
    summed = mine.astype(F32) + swapped(theirs, "tensor", 1).astype(F32)
    low = after(summed.astype(BF16), tokens)
    if started is not None:
        started.append(low)
    total = lax.dynamic_index_in_dim(summed, device * chips + chip, 0, keepdims=False)
    for d, t in partner_bits():
        target = (device ^ d) * chips + (chip ^ t)
        block = lax.dynamic_index_in_dim(low, target, 0, keepdims=False)
        total = total + group_swapped(block, d, 2 * t).astype(F32)
    return total


def ordered(parts, core, other):
    first = jnp.where(core == 0, parts, other)
    second = jnp.where(core == 0, other, parts)
    stacked = jnp.stack([first, second], axis=1)
    return stacked.reshape((-1,) + parts.shape[2:])


def gather_absolute(own, over_dp=True):
    dp_size = lax.axis_size("dp") if over_dp else 1
    chips = lax.axis_size("tensor") // 2
    core = lax.axis_index("tensor") % 2
    chip = lax.axis_index("tensor") // 2
    device = lax.axis_index("dp") if over_dp else 0
    here = jnp.zeros((dp_size * chips,) + own.shape, own.dtype)
    here = lax.dynamic_update_index_in_dim(here, own, device * chips + chip, 0)
    for d, t in partner_bits():
        if d < dp_size:
            received = group_swapped(own, d, 2 * t)
            source = (device ^ d) * chips + (chip ^ t)
            here = lax.dynamic_update_index_in_dim(here, received, source, 0)
    return ordered(here, core, swapped(here, "tensor", 1))


def after(value, tokens):
    return lax.optimization_barrier((value, tokens))[0]


def butterfly_sum(array, axes):
    for axis in axes:
        distance, size = 1, lax.axis_size(axis)
        while distance < size:
            near = array + swapped(array, axis, distance)
            if 2 * distance < size:
                far = swapped(array, axis, 2 * distance) + swapped(array, axis, 3 * distance)
                array, distance = near + far, 4 * distance
            else:
                array, distance = near, 2 * distance
    return array


def contract_cols(left, right):
    return dot(left, right, NT)


def contract_rows(left, right):
    return dot(left, right, TN)


def adam_update(weight, gradient, moments, token_count):
    mean_grad = gradient / token_count
    is_first = lax.broadcasted_iota(jnp.int32, moments.shape, 0) == 0
    moved = 0.5 * moments + 0.5 * jnp.where(is_first, mean_grad, mean_grad * mean_grad)
    first = 0.5 * moments[0] + 0.5 * mean_grad
    second = 0.5 * moments[1] + 0.5 * mean_grad * mean_grad
    correction = 1.0 - 0.5**ADAM_STEP
    change = first / correction / (jnp.sqrt(second / correction) + 1e-08) + 0.1 * weight
    return (weight - 0.1 * change, moved)


def norm_parts(rows):
    factor = lax.rsqrt(jnp.mean(rows * rows, axis=-1, keepdims=True) + 1e-06)
    return factor, rows * factor


def norm_back(factor, normal, gain, grad):
    scaled = grad * gain
    shared = jnp.mean(scaled * normal, axis=-1, keepdims=True)
    return factor * (scaled - normal * shared), jnp.sum(grad * normal, axis=0)


def body(
    stream,
    cotangent,
    w_input,
    w_rates,
    w_conv,
    w_output,
    w_swiglu,
    w_down,
    w_gains,
    w_scale,
    w_heads,
    m_input,
    m_rates,
    m_conv,
    m_output,
    m_swiglu,
    m_down,
    m_gains,
    m_scale,
    m_heads,
):
    dp_size, seq_size, tensor_size = (lax.axis_size(a) for a in ("dp", "seq", "tensor"))
    length, width = stream.shape
    depth = w_input.shape[0]
    heads_stored = w_input.shape[1]
    heads = heads_stored // dp_size
    units_stored = w_swiglu.shape[2]
    units = units_stored // dp_size
    rows = length // tensor_size
    chains = dp_size * heads
    first_part = lax.axis_index("dp") == 0
    first_head = lax.axis_index("tensor") * heads_stored + lax.axis_index("dp") * heads

    def blocks_of(array, order):
        return jnp.concatenate([array[..., i * depth : (i + 1) * depth] for i in order], axis=-1)

    def turned(array):
        return blocks_of(array, [d * seq_size + q for q in range(seq_size) for d in range(dp_size)])

    def turned_back(array):
        return blocks_of(array, [q * dp_size + d for d in range(dp_size) for q in range(seq_size)])

    def mine_and_theirs(low, high):
        return jnp.where(first_part, low, high), jnp.where(first_part, high, low)

    def by_device(own, received):
        return jnp.where(first_part, own, received), jnp.where(first_part, received, own)

    low_input = w_input.astype(BF16)
    low_output = jnp.transpose(w_output.astype(BF16), (2, 0, 1))
    low_swiglu = w_swiglu.astype(BF16)
    low_down = w_down.astype(BF16).T

    def half_columns(index):
        chosen = slice(index * heads, (index + 1) * heads)
        some = slice(index * units, (index + 1) * units)
        return (
            low_input[:, chosen, :QKV].reshape(depth, -1),
            jnp.concatenate(
                [
                    low_input[:, chosen, QKV:].reshape(depth, -1),
                    low_output[:, chosen].reshape(depth, -1),
                ],
                axis=1,
            ),
            jnp.concatenate([low_swiglu[:, 0, some], low_swiglu[:, 1, some]], axis=1),
            low_down[:, some],
        )

    gathered = []
    for low, high in zip(half_columns(0), half_columns(1)):
        mine, theirs = mine_and_theirs(low, high)
        received = swapped(theirs, "dp", 1)
        shard = jnp.concatenate(by_device(mine, received), axis=0)
        gathered.append(lax.all_gather(shard, "seq", axis=0, tiled=True))
    full_qkv, full_mixer, full_swiglu, full_down = gathered
    full_gate, full_output = full_mixer[:, : heads * DV], full_mixer[:, heads * DV :]

    copies = dp_size * seq_size
    rates_low = jnp.broadcast_to(w_rates.astype(BF16).reshape(1, -1), (copies, depth * heads_stored * 2))
    rates_all = lax.all_to_all(rates_low, ("dp", "seq"), 0, 0, tiled=True)
    rates_all = rates_all.reshape(dp_size, seq_size, depth, dp_size, heads * 2)
    rates_all = jnp.swapaxes(rates_all, 0, 1).reshape(width, dp_size, heads * 2)
    full_rates = jnp.where(first_part, rates_all[:, 0], rates_all[:, dp_size - 1])

    quarter = lax.axis_index("tensor") * rows
    stream_rows = turned(lax.dynamic_slice_in_dim(stream, quarter, rows, 0))
    cotangent_rows = turned(lax.dynamic_slice_in_dim(cotangent, quarter, rows, 0))
    gains = turned(w_gains)
    factor_in, normal_in = norm_parts(stream_rows)
    normed_in = gather_absolute((normal_in * gains[0]).astype(BF16)).reshape(-1, width)

    projected = dot(normed_in, full_qkv, NN)
    rates = dot(normed_in, full_rates, NN)
    last_rows = projected.reshape(dp_size, length, heads * QKV)[:, length - 8 :]
    halo = shifted(last_rows, "seq", 1)
    taps = lax.dynamic_slice_in_dim(w_conv, first_head, heads, 1).reshape(KCONV, heads * QKV)
    head_rates = lax.dynamic_slice_in_dim(w_heads, first_head, heads, 1)
    by_chain = jnp.transpose(rates.reshape(dp_size, length, heads, 2), (3, 0, 2, 1))
    decay_raw = by_chain[0] + head_rates[1][None, :, None]
    update = jax.nn.sigmoid(by_chain[1]).reshape(chains, length)
    log_decay = -jnp.exp(head_rates[0])[None, :, None] * jax.nn.softplus(decay_raw)
    count = length // CHUNK
    upper = jnp.triu(jnp.ones((CHUNK, CHUNK), F32))
    cumulative = jnp.dot(
        log_decay.reshape(-1, CHUNK), upper, precision=HIGHEST
    ).reshape(chains, count, CHUNK)
    trailing = jnp.exp(cumulative[:, :, -1:] - cumulative).reshape(chains, length)
    cumulative = cumulative.reshape(chains, length)
    zero = jnp.zeros_like(update)
    columns = jnp.stack(
        [update, cumulative, jnp.exp(cumulative), trailing, zero, zero, zero, zero], axis=-1
    )
    g_rows = jnp.broadcast_to(cumulative[:, None, :], (chains, 8, length))
    call = functools.partial(chains_call, chains=chains, heads=heads, length=length)
    unit = 2 * CHUNK * DK * DK * count
    padded = pltpu.VMEM((length + 8, QKV), F32)
    reach, local, end, starts, inverse, solved_values, solved_keys, steps, seen = call(
        forward_kernel,
        operands=[
            ("rows", projected),
            ("edge", halo),
            ("taps", taps),
            ("chain", columns),
            ("chain", g_rows),
        ],
        outputs=[
            ("chain", (chains, length, DK), F32),
            ("chain", (chains, length, DV), F32),
            ("chain", (chains, DK, DV + DK), F32),
            ("chain", (chains, count, DK, DV + DK), F32),
            ("chain", (chains, length, CHUNK), F32),
            ("chain", (chains, length, DV), F32),
            ("chain", (chains, length, DK), F32),
            ("chain", (chains, length, DK), F32),
            ("chain", (chains, length, DK), F32),
        ],
        scratch=[padded],
        flops=90 * unit,
    )
    offset_map, linear_map = end[..., :DV], end[..., DV:]
    incoming = jnp.zeros((chains, DK, DV), F32)
    for hop in range(seq_size - 1):
        moved = offset_map
        if hop > 0:
            moved = moved + jnp.einsum("bkj,bjw->bkw", linear_map, incoming, precision=HIGHEST)
        incoming = shifted(moved.astype(BF16), "seq", 1).astype(F32)
    grad_ffn = gather_relative(after(cotangent_rows.astype(BF16), end))
    gate_raw = dot(after(normed_in, grad_ffn), full_gate, NN)
    scale_row = w_scale.reshape(1, DV)
    (mixed,) = call(
        finish_kernel,
        operands=[
            ("chain", local),
            ("chain", reach),
            ("chain", incoming),
            ("rows", gate_raw),
            ("all", scale_row),
        ],
        outputs=[("rows", (dp_size * length, heads * DV), BF16)],
        scratch=[],
        flops=6 * unit,
    )
    attention = scatter_absolute(contract_cols(mixed, full_output).astype(BF16))

    residual = stream_rows + attention
    factor_mid, normal_mid = norm_parts(residual)
    normed_mid = gather_relative((normal_mid * gains[1]).astype(BF16))
    gate_up = dot(normed_mid, full_swiglu, NN)
    gate_part, up_part = gate_up[:, :units], gate_up[:, units:]
    sigmoid_gate = jax.nn.sigmoid(gate_part)
    silu_gate = gate_part * sigmoid_gate
    activated = after((silu_gate * up_part).astype(BF16), full_down)
    grad_down_weights = contract_rows(grad_ffn, activated).astype(BF16)
    down_sum = lax.psum_scatter(grad_down_weights, "seq", scatter_dimension=0, tiled=True)
    grad_activated = dot(after(grad_ffn, grad_down_weights), full_down, NN)
    grad_gate = grad_activated * up_part * sigmoid_gate * (1.0 + gate_part * (1.0 - sigmoid_gate))
    grad_up = grad_activated * silu_gate
    grad_gate_up = jnp.concatenate([grad_gate.astype(BF16), grad_up.astype(BF16)], axis=1)
    normed_mid_term = contract_cols(grad_gate_up, full_swiglu).astype(BF16)
    grad_normed_mid = scatter_relative(normed_mid_term)
    grad_swiglu_weights = contract_rows(after(normed_mid, normed_mid_term), grad_gate_up)
    grad_swiglu_weights = after(grad_swiglu_weights.astype(BF16), grad_down_weights)
    swiglu_sum = lax.psum_scatter(grad_swiglu_weights, "seq", scatter_dimension=0, tiled=True)
    from_mid, grad_gain_mid = norm_back(factor_mid, normal_mid, gains[1], grad_normed_mid)
    from_mid = after(from_mid, grad_swiglu_weights)
    grad_attention = gather_absolute((cotangent_rows + from_mid).astype(BF16)).reshape(-1, width)
    grad_mixed = dot(grad_attention, full_output, NN)
    grad_mixer_out, grad_gate_raw, grad_scale, correction = call(
        finish_back_kernel,
        operands=[
            ("chain", local),
            ("chain", reach),
            ("chain", incoming),
            ("rows", gate_raw),
            ("all", scale_row),
            ("rows", grad_mixed),
        ],
        outputs=[
            ("chain", (chains, length, DV), F32),
            ("rows", (dp_size * length, heads * DV), BF16),
            ("chain", (chains, 8, DV), F32),
            ("chain", (chains, DK, DV), F32),
        ],
        scratch=[],
        flops=12 * unit,
    )
    later = jnp.zeros((chains, DK, DV), F32)
    for hop in range(seq_size - 1):
        moved = correction
        if hop > 0:
            moved = moved + jnp.einsum("bjk,bjw->bkw", linear_map, later, precision=HIGHEST)
        later = shifted(moved.astype(BF16), "seq", -1)
        if hop == 0:
            feedforward = scatter_relative(
                contract_cols(after(activated, later), full_down).astype(BF16)
            )
        later = later.astype(F32)
    later = after(later, (swiglu_sum, feedforward))
    grad_mixer_weights = jnp.concatenate(
        [
            contract_rows(normed_in, grad_gate_raw).astype(BF16),
            contract_rows(grad_attention, mixed).astype(BF16),
        ],
        axis=1,
    )
    grad_rows, tail, before, grad_taps, grad_columns = call(
        backward_kernel,
        operands=[
            ("rows", projected),
            ("edge", halo),
            ("taps", taps),
            ("chain", columns),
            ("chain", g_rows),
            ("chain", starts),
            ("chain", inverse),
            ("chain", solved_values),
            ("chain", solved_keys),
            ("chain", steps),
            ("chain", seen),
            ("chain", incoming),
            ("chain", later),
            ("chain", grad_mixer_out),
        ],
        outputs=[
            ("rows", (dp_size * length, heads * QKV), BF16),
            ("edge", (dp_size, 8, heads * QKV), F32),
            ("edge", (dp_size, 8, heads * QKV), F32),
            ("chain", (chains, KCONV, QKV), F32),
            ("chain", (chains, length, 8), F32),
        ],
        scratch=[padded, pltpu.VMEM((length + 16, QKV), F32)],
        flops=120 * unit,
    )
    patched = (tail + shifted(before, "seq", -1)).astype(BF16)
    grad_projected = grad_rows.reshape(dp_size, length, heads * QKV)
    grad_projected = lax.dynamic_update_slice_in_dim(grad_projected, patched, length - 8, 1)
    grad_projected = grad_projected.reshape(dp_size * length, heads * QKV)
    grad_update = grad_columns[..., 0]
    grad_log_decay = jnp.dot(
        grad_columns[..., 1].reshape(-1, CHUNK), upper.T, precision=HIGHEST
    ).reshape(dp_size, heads, length)
    grad_decay_raw = (
        -jnp.exp(head_rates[0])[None, :, None] * grad_log_decay * jax.nn.sigmoid(decay_raw)
    )
    grad_update_raw = (grad_update * update * (1.0 - update)).reshape(dp_size, heads, length)
    grad_rates = jnp.stack([grad_decay_raw, grad_update_raw], axis=-1)
    grad_rates = jnp.transpose(grad_rates, (0, 2, 1, 3)).reshape(-1, heads * 2).astype(BF16)
    grad_heads = jnp.stack(
        [
            jnp.sum(grad_log_decay * log_decay, axis=(0, 2)),
            jnp.sum(grad_decay_raw, axis=(0, 2)),
        ]
    )
    grad_qkv_weights = contract_rows(normed_in, grad_projected).astype(BF16)
    mixer_sum = lax.psum_scatter(
        after(grad_mixer_weights, (swiglu_sum, down_sum)),
        "seq",
        scatter_dimension=0,
        tiled=True,
    )
    qkv_sum = lax.psum_scatter(
        after(grad_qkv_weights, swiglu_sum), "seq", scatter_dimension=0, tiled=True
    )
    grad_rates_weights = contract_rows(grad_rates, after(normed_in, grad_qkv_weights))
    def halves_of(part):
        return mine_and_theirs(part[:depth], part[depth:])

    def exchanged(halves):
        own, theirs = halves
        received = swapped(theirs, "dp", 1)
        return by_device(own, received)

    mixer_parts = exchanged(halves_of(mixer_sum))
    started = []
    normed_in_term = (
        contract_cols(after(grad_projected, (grad_qkv_weights, grad_rates_weights)), full_qkv)
        + contract_cols(grad_gate_raw, full_gate)
        + contract_cols(grad_rates, full_rates)
    )
    grad_normed_in = scatter_absolute(normed_in_term.astype(BF16), mixer_parts, started)
    from_in, grad_gain_in = norm_back(factor_in, normal_in, gains[0], grad_normed_in)
    added = turned_back(jnp.concatenate([attention + feedforward, from_mid + from_in], axis=0))
    added = gather_absolute(
        jnp.concatenate([added[:rows], added[rows:]], axis=1).astype(BF16), False
    ).reshape(length, 2 * width)
    gathered_rows = added
    qkv_halves = halves_of(after(qkv_sum, added))
    added = after(added, qkv_halves)
    result = stream + added[:, :width].astype(F32)
    grad_stream = cotangent + added[:, width:].astype(F32)

    swiglu_parts = exchanged(halves_of(after(swiglu_sum, started)))
    down_parts = exchanged(halves_of(after(down_sum, started)))
    g_output = jnp.concatenate(
        [m[:, heads * DV :].T.reshape(heads, DV, depth) for m in mixer_parts], axis=0
    ).astype(F32)
    g_swiglu = jnp.stack(
        [
            jnp.concatenate([f[:, :units] for f in swiglu_parts], axis=1),
            jnp.concatenate([f[:, units:] for f in swiglu_parts], axis=1),
        ],
        axis=1,
    )
    g_swiglu = with_layout_constraint(g_swiglu.astype(F32), Layout((0, 1, 2)))
    g_down = jnp.concatenate([f.T for f in down_parts], axis=0).astype(F32)

    conv_term = jnp.zeros_like(w_conv)
    grad_taps = jnp.sum(grad_taps.reshape(dp_size, heads, KCONV, QKV), axis=0)
    conv_term = lax.dynamic_update_slice_in_dim(
        conv_term, jnp.swapaxes(grad_taps, 0, 1), first_head, 1
    )
    heads_term = lax.dynamic_update_slice_in_dim(
        jnp.zeros_like(w_heads), grad_heads, first_head, 1
    )
    gains_term = turned_back(jnp.stack([grad_gain_in, grad_gain_mid]))
    scale_term = jnp.sum(grad_scale[:, 0], axis=0)
    first = lax.axis_index("dp") == 0
    rates_term = jnp.concatenate(
        [jnp.where(first, grad_rates_weights, 0.0), jnp.where(first, 0.0, grad_rates_weights)], axis=0
    )
    small = [conv_term, heads_term, gains_term, scale_term]
    flat = jnp.concatenate([a.reshape(-1) for a in small])
    flat = butterfly_sum(after(flat, gathered_rows), ("tensor",))
    flat = jnp.concatenate([flat, rates_term.reshape(-1)])
    flat = butterfly_sum(flat, ("dp", "seq"))
    sums, at = [], 0
    for a in small:
        sums.append(flat[at : at + a.size].reshape(a.shape))
        at += a.size
    g_conv, g_heads, g_gains, g_scale = sums
    block = lax.axis_index("seq") * dp_size + lax.axis_index("dp")
    g_rates = lax.dynamic_slice_in_dim(
        flat[at:].reshape(heads_stored * 2, width), block * depth, depth, 1
    ).T.reshape(depth, heads_stored, 2)

    tokens = float(length * dp_size * seq_size)
    new_rates, moment_rates = adam_update(w_rates, g_rates, m_rates, tokens)
    new_conv, moment_conv = adam_update(w_conv, g_conv, m_conv, tokens)
    new_output, moment_output = adam_update(w_output, g_output, m_output, tokens)
    new_swiglu, moment_swiglu = adam_update(w_swiglu, g_swiglu, m_swiglu, tokens)
    new_down, moment_down = adam_update(w_down, g_down, m_down, tokens)
    new_gains, moment_gains = adam_update(w_gains, g_gains, m_gains, tokens)
    new_scale, moment_scale = adam_update(w_scale, g_scale, m_scale, tokens)
    new_heads, moment_heads = adam_update(w_heads, g_heads, m_heads, tokens)
    qkv_parts = exchanged(qkv_halves)
    g_input = jnp.concatenate(
        [
            jnp.concatenate(
                [
                    q.reshape(depth, heads, QKV),
                    m[:, : heads * DV].reshape(depth, heads, DV),
                ],
                axis=2,
            )
            for q, m in zip(qkv_parts, mixer_parts)
        ],
        axis=1,
    ).astype(F32)
    new_input, moment_input = adam_update(w_input, g_input, m_input, tokens)
    return (
        result,
        grad_stream,
        g_input,
        g_rates,
        g_conv,
        g_output,
        g_swiglu,
        g_down,
        g_gains,
        g_scale,
        g_heads,
        new_input,
        new_rates,
        new_conv,
        new_output,
        new_swiglu,
        new_down,
        new_gains,
        new_scale,
        new_heads,
        moment_input,
        moment_rates,
        moment_conv,
        moment_output,
        moment_swiglu,
        moment_down,
        moment_gains,
        moment_scale,
        moment_heads,
    )


def solution(mesh):
    in_specs = (
        P(("dp", "seq"), None),
        P(("dp", "seq"), None),
        P(("dp", "seq"), "tensor", None),
        P(("dp", "seq"), "tensor", None),
        P(),
        P("tensor", None, ("dp", "seq")),
        P(("dp", "seq"), None, "tensor"),
        P("tensor", ("dp", "seq")),
        P(),
        P(),
        P(),
        P(None, ("dp", "seq"), "tensor", None),
        P(None, ("dp", "seq"), "tensor", None),
        P(),
        P(None, "tensor", None, ("dp", "seq")),
        P(None, ("dp", "seq"), None, "tensor"),
        P(None, "tensor", ("dp", "seq")),
        P(),
        P(),
        P(),
    )
    out_specs = (
        P(("dp", "seq"), None),
        P(("dp", "seq"), None),
        P(("dp", "seq"), "tensor", None),
        P(("dp", "seq"), "tensor", None),
        P(),
        P("tensor", None, ("dp", "seq")),
        P(("dp", "seq"), None, "tensor"),
        P("tensor", ("dp", "seq")),
        P(),
        P(),
        P(),
        P(("dp", "seq"), "tensor", None),
        P(("dp", "seq"), "tensor", None),
        P(),
        P("tensor", None, ("dp", "seq")),
        P(("dp", "seq"), None, "tensor"),
        P("tensor", ("dp", "seq")),
        P(),
        P(),
        P(),
        P(None, ("dp", "seq"), "tensor", None),
        P(None, ("dp", "seq"), "tensor", None),
        P(),
        P(None, "tensor", None, ("dp", "seq")),
        P(None, ("dp", "seq"), None, "tensor"),
        P(None, "tensor", ("dp", "seq")),
        P(),
        P(),
        P(),
    )
    return jax.shard_map(body, mesh=mesh, in_specs=in_specs, out_specs=out_specs, check_vma=False)
```
